32 devices in a mesh: dp: 8 (over z, y), mp: 4 (over x, core).
Axes of the slice: x: 2, y: 2, z: 4, core: 2. Of those that a mesh axis runs over, the one named last changes fastest.
Arguments:
- tokens: bfloat16 [16384, 1024], P('dp', 'mp'), may hold values from -6 to 6
- gain_one: float32 [1024], replicated, may hold values from 0.5 to 1.5
- gain_two: float32 [1024], replicated, may hold values from 0.5 to 1.5
- w_in: bfloat16 [1024, 1024], P(None, 'mp'), may hold values from -0.1875 to 0.1875
- w_query: bfloat16 [1024, 1024], P(None, 'mp'), may hold values from -0.1875 to 0.1875
- w_out: bfloat16 [1024, 1024], P('mp'), may hold values from -3 to 3
- w_up: bfloat16 [1024, 4096], P(None, 'mp'), may hold values from -0.1875 to 0.1875
- w_down: bfloat16 [4096, 1024], P('mp'), may hold values from -0.09375 to 0.09375
- decay_rate: float32 [1024, 16], P('mp'), may hold values from 4.8828124e-06 to 0.03
- b_in: float32 [1024, 16], P('mp'), may hold values from -4 to 4
- c_key: float32 [1024, 16], P('mp'), may hold values from -3 to 3
- c_val: float32 [1024, 16], P('mp'), may hold values from -3 to 3
- short_lengths: int32 [8, 2], P('dp'), may hold values from 1 to 1024, 1536 in all within a row
- cotangent: bfloat16 [16384, 1024], P('dp', 'mp'), may hold values from -6 to 6
Outputs:
- result: bfloat16 [16384, 1024], P('dp', 'mp')
- grad_tokens: bfloat16 [16384, 1024], P('dp', 'mp')
- grad_gain_one: float32 [1024], replicated
- grad_gain_two: float32 [1024], replicated
- grad_w_in: float32 [1024, 1024], P(None, 'mp')
- grad_w_query: float32 [1024, 1024], P(None, 'mp')
- grad_w_out: float32 [1024, 1024], P('mp')
- grad_w_up: float32 [1024, 4096], P(None, 'mp')
- grad_w_down: float32 [4096, 1024], P('mp')
- grad_decay_rate: float32 [1024, 16], P('mp')
- grad_b_in: float32 [1024, 16], P('mp')
- grad_c_key: float32 [1024, 16], P('mp')
- grad_c_val: float32 [1024, 16], P('mp')
The draws below stay inside these ranges and needn't reach their ends.
Inputs may be any that keep to these rules, and one draw needn't show every extreme that they name: `short_lengths`: each device's short documents fill its last 1536 rows in order.
All inputs are finite; a program needn't handle non-finite values.
Results may differ from the reference program's by a relative error of at most 0.02.
Values may be sent and summed in bfloat16 or wider, within the bound.
A program may use at most 256 MiB of HBM per device.

```python
import math
from functools import partial
import jax
import jax.numpy as jnp
import numpy as np
from jax import lax

D = 1024
HEADS = 8
HEAD = 128
FF = 4096
STATE = 16
BLOCK = 512
CTX = 128
SHORT_DOCS = 2
LONG_DEV = 512
SHORT_DEV = 1536
SHORT_MOST = 1024
TOK_DEV = 2048
TOKENS = 16384
INNER = 1024
N_DP = 8


def shard_levels(stream_key, extent, shards, smallest, top_value):
    def one(dim, blocks):
        draws = jax.random.uniform(jax.random.fold_in(jax.random.fold_in(stream_key, 6), dim), (blocks,), jnp.float32, smallest / len(shards), top_value / len(shards))
        return jnp.repeat(jnp.exp(draws), extent[dim] // blocks).reshape((-1,) + (1,) * (len(extent) - dim - 1))

    loudness = one(*shards[0])
    for cut in shards[1:]:
        loudness = loudness * one(*cut)
    return loudness


def profile(amount, total, bound, lean):
    weights = [(1 << 20) // math.isqrt(rank ** lean) + 1 for rank in range(2, amount + 1)]
    rest, counts = total - bound - (amount - 1), [1] * (amount - 1)
    while rest > 0:
        free = [i for i in range(amount - 1) if counts[i] < bound]
        mass, remaining = sum([weights[i] for i in free]), rest
        for i in free:
            addition = min(bound - counts[i], max(1, remaining * weights[i] // mass), rest)
            counts[i] = counts[i] + addition
            rest = rest - addition
    return np.array([bound] + counts)


def uneven(stream_key, count, total, most, skew):
    if count == 2:
        one = jax.random.randint(stream_key, (), max(1, total - most), min(most, total - 1) + 1)
        return jnp.stack([one, total - one])
    tallies = jnp.asarray(profile(count, total, most, skew), jnp.int32)
    couples = (count - 1) // 2
    source_of, receiver = tallies[1:1 + 2 * couples:2], tallies[2:2 + 2 * couples:2]
    room = jnp.minimum(source_of - 1, most - receiver)
    moved = jax.random.randint(jax.random.fold_in(stream_key, 1), (couples,), 0, 1 << 20) % (room + 1)
    tallies = tallies.at[1:1 + 2 * couples:2].set(source_of - moved).at[2:2 + 2 * couples:2].set(receiver + moved)
    return tallies[jax.random.permutation(jax.random.fold_in(stream_key, 2), count)]


def gaussian(key, dims, scale, most, split=(), kind=jnp.bfloat16):
    factor_of = shard_levels(key, dims, split, -0.22, 0.18) if split else 1.0
    array = jax.random.normal(key, dims, jnp.float32) * scale * factor_of
    return jnp.minimum(jnp.maximum(array, -most), most).astype(kind)


def setup_inputs(seed: int = 0) -> dict:
    key_list = jax.random.split(jax.random.key(seed), 15)
    return {
        "tokens": gaussian(key_list[0], (TOKENS, D), 1.0, 6.0, ((0, 8), (1, 4))),
        "gain_one": jnp.clip(1.0 + 0.1 * jax.random.normal(key_list[1], (D,), jnp.float32), 0.5, 1.5),
        "gain_two": jnp.clip(1.0 + 0.1 * jax.random.normal(key_list[2], (D,), jnp.float32), 0.5, 1.5),
        "w_in": gaussian(key_list[3], (D, INNER), D ** -0.5, 0.1875, ((1, 4),)),
        "w_query": gaussian(key_list[4], (D, INNER), D ** -0.5, 0.1875, ((1, 4),)),
        "w_out": gaussian(key_list[5], (INNER, D), (max(INNER // 256, 1)) ** -0.5, 3.0, ((0, 4),)),
        "w_up": gaussian(key_list[6], (D, FF), D ** -0.5, 0.1875, ((1, 4),)),
        "w_down": gaussian(key_list[7], (FF, D), FF ** -0.5, 0.09375, ((0, 4),)),
        "decay_rate": jnp.clip(jnp.exp(math.log(0.03) - 8.723231 * jax.random.uniform(key_list[8], (INNER, STATE), jnp.float32) ** shard_levels(key_list[8], (INNER, STATE), ((0, 4),), -0.2, 0.2)), 4.882812390860636e-06, 0.03),
        "b_in": gaussian(key_list[9], (INNER, STATE), 1.0, 4.0, ((0, 4),), jnp.float32),
        "c_key": gaussian(key_list[10], (INNER, STATE), 0.5, 3.0, ((0, 4),), jnp.float32),
        "c_val": gaussian(key_list[11], (INNER, STATE), 0.5, 3.0, ((0, 4),), jnp.float32),
        "short_lengths": jax.vmap(lambda own: uneven(own, SHORT_DOCS, SHORT_DEV, SHORT_MOST, 0))(jax.random.split(key_list[12], N_DP)).reshape((N_DP, SHORT_DOCS)).astype(jnp.int32),
        "cotangent": gaussian(key_list[13], (TOKENS, D), 1.0, 6.0, ((0, 8), (1, 4))),
    }


@jax.custom_vjp
def low(v):
    return lax.optimization_barrier(v.astype(jnp.bfloat16)).astype(jnp.float32)

@jax.custom_vjp
def low_back(v):
    return v

def low_keep(v):
    return (low(v), None)

def low_pass(kept, grad):
    return (grad,)

def back_keep(v):
    return (v, None)

def back_low(kept, grad):
    return (low(grad),)
low.defvjp(low_keep, low_pass)
low_back.defvjp(back_keep, back_low)
EPS = 1e-05
HIGH = lax.Precision.HIGHEST

def product(left, right):
    return jnp.dot(left, right, precision=HIGH, preferred_element_type=jnp.float32)

def layer_norm(values_in, gain_vec):
    row_mean = lax.optimization_barrier(jnp.mean(values_in, axis=-1, keepdims=True))
    centred = values_in - row_mean
    row_var = lax.optimization_barrier(jnp.mean(centred * centred, axis=-1, keepdims=True))
    return centred * lax.rsqrt(row_var + EPS) * gain_vec

def row_layout(lengths, device):
    positions = jnp.arange(TOK_DEV, dtype=jnp.int32)
    doc_ends = jnp.cumsum(lengths).astype(jnp.int32)
    shifted = positions - LONG_DEV
    passed = (shifted[:, None] >= doc_ends[None, :]).astype(jnp.int32)
    short_ids = 1 + lax.optimization_barrier(jnp.sum(passed, axis=1))
    short_places = shifted - lax.optimization_barrier(jnp.sum(passed * lengths[None, :], axis=1))
    in_long = positions < LONG_DEV
    doc_ids = jnp.where(in_long, 0, short_ids).astype(jnp.int32)
    places = jnp.where(in_long, device * LONG_DEV + positions, short_places).astype(jnp.int32)
    return (doc_ids, places)

def key_layout(doc_ids, places, device):
    ctx_places = (device * LONG_DEV - CTX + jnp.arange(CTX, dtype=jnp.int32)).astype(jnp.int32)
    key_docs = jnp.concatenate([jnp.full((BLOCK,), -2, jnp.int32), jnp.zeros((CTX,), jnp.int32), doc_ids])
    key_places = jnp.concatenate([jnp.full((BLOCK,), -1, jnp.int32), ctx_places, places])
    return (key_docs, key_places)

def block_mask(row_start, doc_ids, places, key_docs, key_places):
    key_span = 2 * BLOCK + CTX
    query_docs = lax.dynamic_slice_in_dim(doc_ids, row_start, BLOCK, 0)
    query_places = lax.dynamic_slice_in_dim(places, row_start, BLOCK, 0)
    span_docs = lax.dynamic_slice_in_dim(key_docs, row_start, key_span, 0)
    span_places = lax.dynamic_slice_in_dim(key_places, row_start, key_span, 0)
    first_place = query_places // BLOCK * BLOCK - CTX
    same_doc = query_docs[:, None] == span_docs[None, :]
    return same_doc & (span_places[None, :] >= 0) & (span_places[None, :] >= first_place[:, None]) & (span_places[None, :] <= query_places[:, None])

def attend(queries, keys_ext, values_ext, doc_ids, places, key_docs, key_places):
    key_span = 2 * BLOCK + CTX
    score_scale = HEAD ** (-0.5)

    def one_block(block_index):
        row_start = block_index * BLOCK
        query_block = lax.dynamic_slice_in_dim(queries, row_start, BLOCK, 0).reshape(BLOCK, HEADS, HEAD)
        key_block = lax.dynamic_slice_in_dim(keys_ext, row_start, key_span, 0).reshape(key_span, HEADS, HEAD)
        value_block = lax.dynamic_slice_in_dim(values_ext, row_start, key_span, 0).reshape(key_span, HEADS, HEAD)
        allowed = block_mask(row_start, doc_ids, places, key_docs, key_places)
        scores = low_back(jnp.einsum('qhd,khd->hqk', query_block, key_block, precision=HIGH) * score_scale)
        scores = jnp.where(allowed[None], scores, -1e+30)
        row_top = lax.optimization_barrier(jnp.max(scores, axis=2, keepdims=True))
        exponents = jnp.exp(scores - row_top)
        probabilities = exponents / lax.optimization_barrier(jnp.sum(exponents, axis=2, keepdims=True))
        mixed = jnp.einsum('hqk,khd->qhd', low(probabilities), value_block, precision=HIGH)
        return mixed.reshape(BLOCK, HEADS * HEAD)
    mixed = lax.map(jax.checkpoint(one_block), jnp.arange(TOK_DEV // BLOCK, dtype=jnp.int32))
    return mixed.reshape(TOK_DEV, HEADS * HEAD)

def recurrence(ssm_input, doc_ids, state_in, decay_rate, b_in, c_key, c_val):
    decay_step = jnp.exp(-decay_rate)
    drive_gain = jnp.sqrt(-jnp.expm1(-2.0 * decay_rate)) * b_in
    before = jnp.concatenate([jnp.zeros((1,), jnp.int32), doc_ids[:-1]])
    keep_flags = (doc_ids == before).astype(jnp.float32)

    def advance(ssm_state, inputs):
        row_values, keep_row = inputs
        ssm_state = decay_step * ssm_state * keep_row + drive_gain * row_values[:, None]
        return (ssm_state, (lax.optimization_barrier(jnp.sum(c_key * ssm_state, axis=1)), lax.optimization_barrier(jnp.sum(c_val * ssm_state, axis=1))))
    long_end, (keys_long, values_long) = lax.scan(advance, state_in, (ssm_input[:LONG_DEV], keep_flags[:LONG_DEV]))
    _, (keys_short, values_short) = lax.scan(advance, jnp.zeros_like(state_in), (ssm_input[LONG_DEV:], keep_flags[LONG_DEV:]))
    return (long_end, jnp.concatenate([keys_long, keys_short]), jnp.concatenate([values_long, values_short]))

def device_fn(params, carry, inputs):
    gain_one, gain_two, w_in, w_query, w_out, w_up, w_down, decay_rate, b_in, c_key, c_val = params
    state_in, ctx_keys, ctx_values = carry
    tokens, lengths, device = inputs
    doc_ids, places = row_layout(lengths, device)
    key_docs, key_places = key_layout(doc_ids, places, device)
    normed_one = low(layer_norm(tokens, gain_one))
    ssm_input = low_back(product(normed_one, w_in))
    queries = low(low_back(product(normed_one, w_query)))
    long_end, keys_raw, values_raw = recurrence(ssm_input, doc_ids, state_in, decay_rate, b_in, c_key, c_val)
    keys = low(keys_raw)
    values = low(values_raw)
    padding = jnp.zeros((BLOCK, HEADS * HEAD), jnp.float32)
    keys_ext = jnp.concatenate([padding, ctx_keys, keys])
    values_ext = jnp.concatenate([padding, ctx_values, values])
    attended = low(low_back(attend(queries, keys_ext, values_ext, doc_ids, places, key_docs, key_places)))
    middle = tokens + low_back(product(attended, w_out))
    normed_two = low(layer_norm(low(middle), gain_two))
    act = low(jax.nn.gelu(low_back(product(normed_two, w_up)), approximate=False))
    result = middle + product(act, w_down)
    new_carry = (long_end, keys[LONG_DEV - CTX:LONG_DEV], values[LONG_DEV - CTX:LONG_DEV])
    return (new_carry, result)

def forward(tokens, gain_one, gain_two, w_in, w_query, w_out, w_up, w_down, decay_rate, b_in, c_key, c_val, lengths):
    params = (gain_one, gain_two, w_in, w_query, w_out, w_up, w_down, decay_rate, b_in, c_key, c_val)
    checked = jax.checkpoint(device_fn)

    def scan_body(carry, inputs):
        return checked(params, carry, inputs)
    initial = (jnp.zeros((HEADS * HEAD, STATE), jnp.float32), jnp.zeros((CTX, HEADS * HEAD), jnp.float32), jnp.zeros((CTX, HEADS * HEAD), jnp.float32))
    _, outputs = lax.scan(scan_body, initial, (tokens, lengths, jnp.arange(N_DP, dtype=jnp.int32)))
    return outputs

def reference(tokens, gain_one, gain_two, w_in, w_query, w_out, w_up, w_down, decay_rate, b_in, c_key, c_val, short_lengths, cotangent):
    floats = [tokens.astype(jnp.float32).reshape(N_DP, TOK_DEV, D), gain_one, gain_two, w_in.astype(jnp.float32), w_query.astype(jnp.float32), w_out.astype(jnp.float32), w_up.astype(jnp.float32), w_down.astype(jnp.float32), decay_rate, b_in, c_key, c_val]
    run_layer = partial(forward, lengths=short_lengths)
    result, pullback = jax.vjp(run_layer, *floats)
    gradients = pullback(cotangent.astype(jnp.float32).reshape(N_DP, TOK_DEV, D))
    return (result.reshape(TOKENS, D).astype(jnp.bfloat16), gradients[0].reshape(TOKENS, D).astype(jnp.bfloat16), gradients[1], gradients[2], gradients[3], gradients[4], gradients[5], gradients[6], gradients[7], gradients[8], gradients[9], gradients[10], gradients[11])
```

```python
import functools

import jax
import jax.numpy as jnp
from jax import lax
from jax.experimental import pallas as pl
from jax.experimental.pallas import tpu as pltpu
from jax.sharding import PartitionSpec as P

HEAD = 128
BLOCK = 512
CTX = 128
LONG_DEV = 512
EPS = 1e-05
SEG = 8
GROUP = 8
STATES = 16
LANES = 128
VMEM = pl.BlockSpec(memory_space=pltpu.VMEM)
SMEM = pl.BlockSpec(memory_space=pltpu.SMEM)


def seg_scan_params(par_ref, wide_ref):
    for p in range(par_ref.shape[0]):
        for n in range(STATES):
            for lt in range(par_ref.shape[2] // LANES):
                row = par_ref[p, n : n + 1, lt * LANES : (lt + 1) * LANES]
                wide_ref[p, n, lt] = jnp.broadcast_to(row, (SEG, LANES))


def keep_mask(bounds_ref, span, step):
    rows = lax.broadcasted_iota(jnp.int32, (SEG, LANES), 0) * span + step
    keep = jnp.ones((SEG, LANES), jnp.float32)
    for k in range(bounds_ref.shape[0]):
        keep = jnp.where(rows == bounds_ref[k], 0.0, keep)
    return keep


def has_bound(bounds_ref, span, group):
    found = False
    for k in range(bounds_ref.shape[0]):
        b = bounds_ref[k]
        inside = lax.rem(b, span) // GROUP == group
        found = jnp.logical_or(found, jnp.logical_and(b >= 0, inside))
    return found


def steps_of(ref, lt, group, span):
    return [ref[lt, pl.ds(group * GROUP + j, SEG, stride=span), :] for j in range(GROUP)]


def split_lanes(src_ref, dst_ref):
    for lt in range(dst_ref.shape[0]):
        dst_ref[lt] = src_ref[:, lt * LANES : (lt + 1) * LANES].astype(jnp.float32)


def with_masks(bounds_ref, span, group, body):
    flag = has_bound(bounds_ref, span, group)

    @pl.when(flag)
    def _():
        body([keep_mask(bounds_ref, span, group * GROUP + j) for j in range(GROUP)])

    @pl.when(jnp.logical_not(flag))
    def _():
        body(None)


def forward_ends(bounds_ref, u_ref, wide_ref, state_ref, span, tiles):
    state_ref[...] = jnp.zeros_like(state_ref)

    @pl.loop(0, span // GROUP)
    def _(group):
        def body(keep):
            for lt in range(tiles):
                u = steps_of(u_ref, lt, group, span)
                for n in range(STATES):
                    a = wide_ref[0, n, lt]
                    s = state_ref[lt, n * SEG : (n + 1) * SEG, :]
                    for j in range(GROUP):
                        s = a * s
                        if keep is not None:
                            s = s * keep[j]
                        s = s + u[j]
                    state_ref[lt, n * SEG : (n + 1) * SEG, :] = s

        with_masks(bounds_ref, span, group, body)


def no_bound_in_seg(bounds_ref, span, seg):
    ok = jnp.float32(1.0)
    for k in range(bounds_ref.shape[0]):
        b = bounds_ref[k]
        inside = jnp.logical_and(b >= seg * span, b < (seg + 1) * span)
        ok = jnp.where(inside, jnp.float32(0.0), ok)
    return ok


def chain_forward(bounds_ref, state_ref, first, far_ref, span, tiles):
    for lt in range(tiles):
        lanes = slice(lt * LANES, (lt + 1) * LANES)
        start = first[:, lanes]
        far = far_ref[:, lanes]
        for seg in range(SEG):
            rows = pl.ds(seg, STATES, stride=SEG)
            end = state_ref[lt, rows, :]
            state_ref[lt, rows, :] = start
            start = end + far * start * no_bound_in_seg(bounds_ref, span, seg)


def chain_backward(bounds_ref, adj_ref, last, far_ref, span, tiles):
    for lt in range(tiles):
        lanes = slice(lt * LANES, (lt + 1) * LANES)
        start = last[:, lanes]
        far = far_ref[:, lanes]
        for seg in reversed(range(SEG)):
            rows = pl.ds(seg, STATES, stride=SEG)
            end = adj_ref[lt, rows, :]
            adj_ref[lt, rows, :] = start
            start = end + far * start * no_bound_in_seg(bounds_ref, span, seg)
        yield start


def ends_kernel(span, tiles, bounds_ref, u_in, par_ref, far_ref, out_ref, u_ref, wide_ref, state_ref):
    split_lanes(u_in, u_ref)
    seg_scan_params(par_ref, wide_ref)
    forward_ends(bounds_ref, u_ref, wide_ref, state_ref, span, tiles)
    for lt in range(tiles):
        lanes = slice(lt * LANES, (lt + 1) * LANES)
        start = jnp.zeros((STATES, LANES), jnp.float32)
        for seg in range(SEG):
            end = state_ref[lt, pl.ds(seg, STATES, stride=SEG), :]
            start = end + far_ref[:, lanes] * start * no_bound_in_seg(bounds_ref, span, seg)
        out_ref[:, lanes] = start


def forward_kernel(span, tiles, bounds_ref, u_in, par_ref, far_ref, first_ref, k_out, v_out, ckpt_ref,
                   u_ref, k_ref, v_ref, wide_ref, state_ref):
    split_lanes(u_in, u_ref)
    seg_scan_params(par_ref, wide_ref)
    forward_ends(bounds_ref, u_ref, wide_ref, state_ref, span, tiles)
    chain_forward(bounds_ref, state_ref, first_ref[...], far_ref, span, tiles)

    @pl.loop(0, span // GROUP)
    def _(group):
        def body(keep):
            for lt in range(tiles):
                u = steps_of(u_ref, lt, group, span)
                ks = [jnp.zeros((SEG, LANES), jnp.float32)] * GROUP
                vs = [jnp.zeros((SEG, LANES), jnp.float32)] * GROUP
                for n in range(STATES):
                    a, ck, cv = wide_ref[0, n, lt], wide_ref[1, n, lt], wide_ref[2, n, lt]
                    s = state_ref[lt, n * SEG : (n + 1) * SEG, :]
                    ckpt_ref[group, lt, n * SEG : (n + 1) * SEG, :] = s
                    for j in range(GROUP):
                        s = a * s
                        if keep is not None:
                            s = s * keep[j]
                        s = s + u[j]
                        ks[j] = ks[j] + ck * s
                        vs[j] = vs[j] + cv * s
                    state_ref[lt, n * SEG : (n + 1) * SEG, :] = s
                for j in range(GROUP):
                    rows = pl.ds(group * GROUP + j, SEG, stride=span)
                    k_ref[lt, rows, :] = ks[j]
                    v_ref[lt, rows, :] = vs[j]

        with_masks(bounds_ref, span, group, body)

    for lt in range(tiles):
        k_out[:, lt * LANES : (lt + 1) * LANES] = k_ref[lt].astype(k_out.dtype)
        v_out[:, lt * LANES : (lt + 1) * LANES] = v_ref[lt].astype(v_out.dtype)


def adjoint_ends(bounds_ref, gk_ref, gv_ref, wide_ref, adj_ref, span, tiles):
    adj_ref[...] = jnp.zeros_like(adj_ref)
    groups = span // GROUP

    @pl.loop(0, groups)
    def _(step):
        group = groups - 1 - step

        def body(keep):
            for lt in range(tiles):
                gk = steps_of(gk_ref, lt, group, span)
                gv = steps_of(gv_ref, lt, group, span)
                for n in range(STATES):
                    a, ck, cv = wide_ref[0, n, lt], wide_ref[1, n, lt], wide_ref[2, n, lt]
                    m = adj_ref[lt, n * SEG : (n + 1) * SEG, :]
                    for j in reversed(range(GROUP)):
                        m = a * (m + (ck * gk[j] + cv * gv[j]))
                        if keep is not None:
                            m = m * keep[j]
                    adj_ref[lt, n * SEG : (n + 1) * SEG, :] = m

        with_masks(bounds_ref, span, group, body)


def adjoint_ends_kernel(span, tiles, bounds_ref, gk_in, gv_in, par_ref, far_ref, out_ref, gk_ref, gv_ref, wide_ref, adj_ref):
    split_lanes(gk_in, gk_ref)
    split_lanes(gv_in, gv_ref)
    seg_scan_params(par_ref, wide_ref)
    adjoint_ends(bounds_ref, gk_ref, gv_ref, wide_ref, adj_ref, span, tiles)
    for lt in range(tiles):
        lanes = slice(lt * LANES, (lt + 1) * LANES)
        start = jnp.zeros((STATES, LANES), jnp.float32)
        for seg in reversed(range(SEG)):
            end = adj_ref[lt, pl.ds(seg, STATES, stride=SEG), :]
            start = end + far_ref[:, lanes] * start * no_bound_in_seg(bounds_ref, span, seg)
        out_ref[:, lanes] = start


def backward_kernel(span, tiles, bounds_ref, u_in, gk_in, gv_in, par_ref, far_ref, last_ref, ckpt_ref,
                    gu_out, sums_out, u_ref, gk_ref, gv_ref, gu_ref, wide_ref, adj_ref, acc_ref):
    split_lanes(u_in, u_ref)
    split_lanes(gk_in, gk_ref)
    split_lanes(gv_in, gv_ref)
    seg_scan_params(par_ref, wide_ref)
    adjoint_ends(bounds_ref, gk_ref, gv_ref, wide_ref, adj_ref, span, tiles)
    for _ in chain_backward(bounds_ref, adj_ref, last_ref[...], far_ref, span, tiles):
        pass
    acc_ref[...] = jnp.zeros_like(acc_ref)
    groups = span // GROUP

    @pl.loop(0, groups)
    def _(step):
        group = groups - 1 - step

        def body(keep):
            for lt in range(tiles):
                u = steps_of(u_ref, lt, group, span)
                gk = steps_of(gk_ref, lt, group, span)
                gv = steps_of(gv_ref, lt, group, span)
                gu = [jnp.zeros((SEG, LANES), jnp.float32)] * GROUP
                for n in range(STATES):
                    mine = slice(n * SEG, (n + 1) * SEG)
                    a, ck, cv = wide_ref[0, n, lt], wide_ref[1, n, lt], wide_ref[2, n, lt]
                    states = [ckpt_ref[group, lt, mine, :]]
                    for j in range(GROUP):
                        s = a * states[j]
                        if keep is not None:
                            s = s * keep[j]
                        states.append(s + u[j])
                    m = adj_ref[lt, mine, :]
                    sum_k, sum_v, sum_a = acc_ref[0, lt, mine, :], acc_ref[1, lt, mine, :], acc_ref[2, lt, mine, :]
                    for j in reversed(range(GROUP)):
                        lam = m + (ck * gk[j] + cv * gv[j])
                        gu[j] = gu[j] + lam
                        sum_k = sum_k + gk[j] * states[j + 1]
                        sum_v = sum_v + gv[j] * states[j + 1]
                        m = a * lam
                        if keep is not None:
                            m = m * keep[j]
                        sum_a = sum_a + m * states[j]
                    acc_ref[0, lt, mine, :] = sum_k
                    acc_ref[1, lt, mine, :] = sum_v
                    acc_ref[2, lt, mine, :] = sum_a
                    adj_ref[lt, mine, :] = m
                for j in range(GROUP):
                    gu_ref[lt, pl.ds(group * GROUP + j, SEG, stride=span), :] = gu[j]

        with_masks(bounds_ref, span, group, body)

    for lt in range(tiles):
        lanes = slice(lt * LANES, (lt + 1) * LANES)
        gu_out[:, lanes] = gu_ref[lt].astype(gu_out.dtype)
        for p in range(3):
            total = acc_ref[p, lt, pl.ds(0, STATES, stride=SEG), :]
            for seg in range(1, SEG):
                total = total + acc_ref[p, lt, pl.ds(seg, STATES, stride=SEG), :]
            sums_out[p, :, lanes] = total


LIMIT = pltpu.CompilerParams(vmem_limit_bytes=48 * 2**20)


def f32(*shape):
    return pltpu.VMEM(shape, jnp.float32)


def ssm_ends(bounds, u, par, far, name="ssm_ends"):
    rows, width = u.shape
    span, tiles = rows // SEG, width // LANES
    return pl.pallas_call(
        functools.partial(ends_kernel, span, tiles),
        out_shape=jax.ShapeDtypeStruct((STATES, width), jnp.float32),
        in_specs=[SMEM] + [VMEM] * 3, out_specs=VMEM,
        scratch_shapes=[f32(tiles, rows, LANES), f32(3, STATES, tiles, SEG, LANES), f32(tiles, STATES * SEG, LANES)],
        compiler_params=LIMIT, name=name)(bounds, u, par, far)


def ssm_forward(bounds, u, par, far, first, name="ssm_forward"):
    rows, width = u.shape
    span, tiles = rows // SEG, width // LANES
    return pl.pallas_call(
        functools.partial(forward_kernel, span, tiles),
        out_shape=(jax.ShapeDtypeStruct((rows, width), jnp.bfloat16), jax.ShapeDtypeStruct((rows, width), jnp.bfloat16),
                   jax.ShapeDtypeStruct((span // GROUP, tiles, STATES * SEG, LANES), jnp.float32)),
        in_specs=[SMEM] + [VMEM] * 4, out_specs=(VMEM,) * 3,
        scratch_shapes=[f32(tiles, rows, LANES)] * 3 + [f32(3, STATES, tiles, SEG, LANES), f32(tiles, STATES * SEG, LANES)],
        compiler_params=LIMIT, name=name)(bounds, u, par, far, first)


def ssm_adjoint_ends(bounds, gk, gv, par, far, name="ssm_adjoint_ends"):
    rows, width = gk.shape
    span, tiles = rows // SEG, width // LANES
    return pl.pallas_call(
        functools.partial(adjoint_ends_kernel, span, tiles),
        out_shape=jax.ShapeDtypeStruct((STATES, width), jnp.float32),
        in_specs=[SMEM] + [VMEM] * 4, out_specs=VMEM,
        scratch_shapes=[f32(tiles, rows, LANES)] * 2 + [f32(3, STATES, tiles, SEG, LANES), f32(tiles, STATES * SEG, LANES)],
        compiler_params=LIMIT, name=name)(bounds, gk, gv, par, far)


def ssm_backward(bounds, u, gk, gv, par, far, last, ckpt, name="ssm_backward"):
    rows, width = u.shape
    span, tiles = rows // SEG, width // LANES
    return pl.pallas_call(
        functools.partial(backward_kernel, span, tiles),
        out_shape=(jax.ShapeDtypeStruct((rows, width), jnp.bfloat16), jax.ShapeDtypeStruct((3, STATES, width), jnp.float32)),
        in_specs=[SMEM] + [VMEM] * 7, out_specs=(VMEM,) * 2,
        scratch_shapes=[f32(tiles, rows, LANES)] * 4 + [f32(3, STATES, tiles, SEG, LANES), f32(tiles, STATES * SEG, LANES), f32(3, tiles, STATES * SEG, LANES)],
        compiler_params=LIMIT, name=name)(bounds, u, gk, gv, par, far, last, ckpt)


QT = 256
NEG = -1e30
SCALE = HEAD ** (-0.5)


def tiles_of(rows, shift):
    out = []
    for r in range(0, rows, QT):
        first = max(0, r + shift - (BLOCK + CTX)) if shift == 0 else 0
        out.append((r, first, r + shift + QT))
    return out


def lowest_key(starts_ref, row0, shift):
    if shift:
        return jnp.full((1, QT), starts_ref[0], jnp.int32)
    rows = lax.broadcasted_iota(jnp.int32, (1, QT), 1) + row0
    start = jnp.zeros((1, QT), jnp.int32)
    for k in range(starts_ref.shape[0]):
        start = jnp.where(rows >= starts_ref[k], starts_ref[k], start)
    block = ((rows - start) // BLOCK) * BLOCK - CTX
    return start + jnp.maximum(block, 0)


def allowed_keys(starts_ref, q0, k0, k1, shift):
    low = lowest_key(starts_ref, q0, shift)
    high = lax.broadcasted_iota(jnp.int32, (1, QT), 1) + (q0 + shift)
    keys = lax.broadcasted_iota(jnp.int32, (k1 - k0, QT), 0) + k0
    return (keys >= low) & (keys <= high)


def dot_nt(a, b):
    return lax.dot_general(a, b, (((1,), (1,)), ((), ())), preferred_element_type=jnp.float32)


def dot_nn(a, b):
    return lax.dot_general(a, b, (((1,), (0,)), ((), ())), preferred_element_type=jnp.float32)


def attend_kernel(tiles, shift, starts_ref, q_ref, k_ref, v_ref, o_ref, lse_ref, vt_ref):
    vt_ref[...] = v_ref[...].T
    for q0, k0, k1 in tiles:
        scores = dot_nt(k_ref[k0:k1, :], q_ref[q0 : q0 + QT, :]) * SCALE
        scores = jnp.where(allowed_keys(starts_ref, q0, k0, k1, shift), scores, NEG)
        top = jnp.max(scores, axis=0, keepdims=True)
        exps = jnp.exp(scores - top)
        total = jnp.sum(exps, axis=0, keepdims=True)
        probs = (exps * (1.0 / total)).astype(jnp.bfloat16)
        mixed = dot_nn(vt_ref[:, k0:k1], probs)
        o_ref[q0 : q0 + QT, :] = mixed.T.astype(o_ref.dtype)
        lse_ref[0, 0, q0 : q0 + QT] = (top + jnp.log(total))[0]


def attend(starts, q, k, v, shift, name):
    rows, width = q.shape
    heads = width // HEAD
    keys = k.shape[0]
    lane = lambda h: (0, h)
    return pl.pallas_call(
        functools.partial(attend_kernel, tiles_of(rows, shift), shift),
        grid=(heads,),
        out_shape=(jax.ShapeDtypeStruct((rows, width), jnp.bfloat16), jax.ShapeDtypeStruct((heads, 1, rows), jnp.float32)),
        in_specs=[SMEM, pl.BlockSpec((rows, HEAD), lane), pl.BlockSpec((keys, HEAD), lane), pl.BlockSpec((keys, HEAD), lane)],
        out_specs=(pl.BlockSpec((rows, HEAD), lane), pl.BlockSpec((1, 1, rows), lambda h: (h, 0, 0))),
        scratch_shapes=[pltpu.VMEM((HEAD, keys), jnp.bfloat16)],
        compiler_params=pltpu.CompilerParams(vmem_limit_bytes=40 * 2**20),
        name=name)(starts, q, k, v)


def attend_back_kernel(tiles, shift, starts_ref, q_ref, k_ref, v_ref, g_ref, lse_ref, dq_ref, dk_ref, dv_ref, kt_ref):
    kt_ref[...] = k_ref[...].T
    dk_ref[...] = jnp.zeros_like(dk_ref)
    dv_ref[...] = jnp.zeros_like(dv_ref)
    for q0, k0, k1 in tiles:
        q = q_ref[q0 : q0 + QT, :]
        g = g_ref[q0 : q0 + QT, :]
        lse = lse_ref[0, :, q0 : q0 + QT]
        scores = dot_nt(k_ref[k0:k1, :], q) * SCALE
        probs = jnp.where(allowed_keys(starts_ref, q0, k0, k1, shift), jnp.exp(scores - lse), 0.0)
        grad_probs = dot_nt(v_ref[k0:k1, :], g)
        dv_ref[k0:k1, :] += dot_nn(probs.astype(jnp.bfloat16), g)
        delta = jnp.sum(probs * grad_probs, axis=0, keepdims=True)
        grad_scores = (probs * (grad_probs - delta)).astype(jnp.bfloat16)
        dk_ref[k0:k1, :] += dot_nn(grad_scores, q) * SCALE
        dq_ref[q0 : q0 + QT, :] = (dot_nn(kt_ref[:, k0:k1], grad_scores) * SCALE).T.astype(dq_ref.dtype)


def attend_back(starts, q, k, v, g, lse, shift, name):
    rows, width = q.shape
    heads = width // HEAD
    keys = k.shape[0]
    lane = lambda h: (0, h)
    rspec, kspec = pl.BlockSpec((rows, HEAD), lane), pl.BlockSpec((keys, HEAD), lane)
    return pl.pallas_call(
        functools.partial(attend_back_kernel, tiles_of(rows, shift), shift),
        grid=(heads,),
        out_shape=(jax.ShapeDtypeStruct((rows, width), jnp.bfloat16), jax.ShapeDtypeStruct((keys, width), jnp.float32), jax.ShapeDtypeStruct((keys, width), jnp.float32)),
        in_specs=[SMEM, rspec, kspec, kspec, rspec, pl.BlockSpec((1, 1, rows), lambda h: (h, 0, 0))],
        out_specs=(rspec, kspec, kspec),
        scratch_shapes=[pltpu.VMEM((HEAD, keys), jnp.bfloat16)],
        compiler_params=pltpu.CompilerParams(vmem_limit_bytes=40 * 2**20),
        name=name)(starts, q, k, v, g, lse)


def gather_features(values_in):
    return lax.all_gather(values_in, "mp", axis=1, tiled=True)


def reduce_features(values_in):
    return lax.psum_scatter(
        values_in.astype(jnp.bfloat16), "mp", scatter_dimension=1, tiled=True
    ).astype(jnp.float32)


def from_behind(value, axis, steps):
    count = lax.axis_size(axis)
    initial, last = (max(0, -steps), min(count, count - steps))
    return lax.ppermute(value, axis, [(source, source + steps) for source in range(initial, last)])


def norm_forward(values_in, gain_vec):
    row_mean = jnp.mean(values_in, axis=1, keepdims=True)
    centred = values_in - row_mean
    row_var = jnp.mean(centred * centred, axis=1, keepdims=True)
    inverse = lax.rsqrt(row_var + EPS)
    normed = centred * inverse
    return (normed, inverse, normed * gain_vec)


def norm_backward(upstream, normed, inverse, gain_vec):
    gain_grad = jnp.sum(upstream * normed, axis=0)
    scaled = upstream * gain_vec
    plain_mean = jnp.mean(scaled, axis=1, keepdims=True)
    cross_mean = jnp.mean(scaled * normed, axis=1, keepdims=True)
    return (inverse * (scaled - plain_mean - normed * cross_mean), gain_grad)


def gelu_exact(values_in):
    return jax.nn.gelu(values_in, approximate=False)


def fold_pieces(pieces, decay_rate, gap_count):
    live_rows = gap_count >= 0
    weights = jnp.exp(
        -decay_rate[None]
        * (LONG_DEV * jnp.maximum(gap_count, 0)).astype(jnp.float32)[:, None, None]
    )
    return jnp.sum(jnp.where(live_rows[:, None, None], weights * pieces, 0.0), axis=0)


def dot(left, right, dims):
    return lax.dot_general(left, right, ((dims[0], dims[1]), ((), ())), preferred_element_type=jnp.float32)


def on_device(
    tokens,
    gain_one,
    gain_two,
    w_in,
    w_query,
    w_out,
    w_up,
    w_down,
    decay_rate,
    b_in,
    c_key,
    c_val,
    short_lengths,
    cotangent,
):
    low = jnp.bfloat16
    device = lax.axis_index("dp")
    lengths = short_lengths[0]
    ends = jnp.cumsum(lengths).astype(jnp.int32)
    short_starts = jnp.concatenate([jnp.zeros((1,), jnp.int32), ends[:-1]])
    no_bound = jnp.full((1,), -1, jnp.int32)
    long_low = jnp.where(device > 0, 0, CTX).astype(jnp.int32).reshape(1)
    rate_t = decay_rate.T
    root = jnp.sqrt(-jnp.expm1(-2.0 * rate_t))
    drive = root * b_in.T
    ck_t, cv_t = c_key.T, c_val.T
    decay = jnp.exp(-rate_t)
    par = jnp.stack([decay, drive * ck_t, drive * cv_t])
    short_rows = tokens.shape[0] - LONG_DEV
    far_long = jnp.exp(-rate_t * (LONG_DEV // SEG))
    far_short = jnp.exp(-rate_t * (short_rows // SEG))

    tokens_full = gather_features(tokens).astype(jnp.float32)
    cotangent_full = gather_features(cotangent)
    normed_one, inverse_one, hidden_one = norm_forward(tokens_full, gain_one)
    normed_one_low = hidden_one.astype(low)
    ssm_input = jnp.dot(normed_one_low, w_in, preferred_element_type=jnp.float32)
    queries = jnp.dot(normed_one_low, w_query, preferred_element_type=jnp.float32).astype(low)
    u_long, u_short = ssm_input[:LONG_DEV], ssm_input[LONG_DEV:]
    local_end = ssm_ends(no_bound, u_long, par, far_long)
    pieces = lax.all_gather(local_end[None], "dp", axis=0, tiled=True)
    others = jnp.arange(pieces.shape[0], dtype=jnp.int32)
    state_in = fold_pieces(pieces, rate_t, device - 1 - others)
    zero_state = jnp.zeros_like(state_in)
    k_short, v_short, ckpt_short = ssm_forward(short_starts, u_short, par, far_short, zero_state, "ssm_short")
    k_long, v_long, ckpt_long = ssm_forward(no_bound, u_long, par, far_long, state_in, "ssm_long")
    ctx_k, ctx_v = from_behind((k_long[LONG_DEV - CTX :], v_long[LONG_DEV - CTX :]), "dp", 1)
    k_long = jnp.concatenate([ctx_k, k_long])
    v_long = jnp.concatenate([ctx_v, v_long])
    q_long, q_short = queries[:LONG_DEV], queries[LONG_DEV:]
    att_short, lse_short = attend(short_starts, q_short, k_short, v_short, 0, "attend_short")
    att_long, lse_long = attend(long_low, q_long, k_long, v_long, CTX, "attend_long")
    attended = jnp.concatenate([att_long, att_short])
    middle = tokens.astype(jnp.float32) + reduce_features(
        jnp.dot(attended, w_out, preferred_element_type=jnp.float32)
    )
    middle_full = gather_features(middle.astype(low)).astype(jnp.float32)
    normed_two, inverse_two, hidden_two = norm_forward(middle_full, gain_two)
    normed_two_low = hidden_two.astype(low)
    pre_act = jnp.dot(normed_two_low, w_up, preferred_element_type=jnp.float32)
    act_value, act_pull = jax.vjp(gelu_exact, pre_act)
    act_low = act_value.astype(low)
    result = (
        middle + reduce_features(jnp.dot(act_low, w_down, preferred_element_type=jnp.float32))
    ).astype(low)
    grad_w_down = dot(act_low, cotangent_full, ((0,), (0,)))
    grad_act = dot(cotangent_full, w_down, ((1,), (1,)))
    grad_pre = act_pull(grad_act)[0].astype(low)
    grad_w_up = dot(normed_two_low, grad_pre, ((0,), (0,)))
    grad_hidden_two = dot(grad_pre, w_up, ((1,), (1,)))
    middle_part, grad_gain_two = norm_backward(grad_hidden_two, normed_two, inverse_two, gain_two)
    grad_middle = cotangent.astype(jnp.float32) + reduce_features(middle_part)
    grad_mid_full = gather_features(grad_middle.astype(low))
    grad_w_out = dot(attended, grad_mid_full, ((0,), (0,)))
    grad_attended = dot(grad_mid_full, w_out, ((1,), (1,))).astype(low)

    gq_long, gk_long, gv_long = attend_back(
        long_low, q_long, k_long, v_long, grad_attended[:LONG_DEV], lse_long, CTX, "attend_back_long"
    )
    back_k, back_v = from_behind((gk_long[:CTX].astype(low), gv_long[:CTX].astype(low)), "dp", -1)
    gq_short, gk_short, gv_short = attend_back(
        short_starts, q_short, k_short, v_short, grad_attended[LONG_DEV:], lse_short, 0, "attend_back_short"
    )
    gk_long = gk_long[CTX:].at[LONG_DEV - CTX :].add(back_k.astype(jnp.float32))
    gv_long = gv_long[CTX:].at[LONG_DEV - CTX :].add(back_v.astype(jnp.float32))
    local_in = ssm_adjoint_ends(no_bound, gk_long, gv_long, par, far_long)
    grad_pieces = lax.all_gather(local_in[None], "dp", axis=0, tiled=True)
    grad_end = fold_pieces(grad_pieces, rate_t, others - device - 1)
    gu_short, sums_short = ssm_backward(
        short_starts, u_short, gk_short, gv_short, par, far_short, zero_state, ckpt_short, "ssm_back_short"
    )
    gu_long, sums_long = ssm_backward(
        no_bound, u_long, gk_long, gv_long, par, far_long, grad_end, ckpt_long, "ssm_back_long"
    )
    sums = sums_short + sums_long
    grad_ssm = jnp.concatenate([gu_long, gu_short])
    grad_queries = jnp.concatenate([gq_long, gq_short])
    grad_w_in = dot(normed_one_low, grad_ssm, ((0,), (0,)))
    grad_w_query = dot(normed_one_low, grad_queries, ((0,), (0,)))
    grad_hidden_one = dot(grad_ssm, w_in, ((1,), (1,))) + dot(grad_queries, w_query, ((1,), (1,)))
    token_part, grad_gain_one = norm_backward(grad_hidden_one, normed_one, inverse_one, gain_one)
    grad_tokens = (grad_middle + reduce_features(token_part)).astype(low)

    grad_w_in, grad_w_query, grad_w_out, grad_w_up, grad_w_down = (
        g.astype(jnp.float32)
        for g in lax.psum(
            tuple(g.astype(low) for g in (grad_w_in, grad_w_query, grad_w_out, grad_w_up, grad_w_down)), "dp"
        )
    )
    sums = lax.psum(sums, "dp")
    grad_ck = (drive * sums[0]).T
    grad_cv = (drive * sums[1]).T
    grad_drive = ck_t * sums[0] + cv_t * sums[1]
    grad_b = (root * grad_drive).T
    grad_rate = (grad_drive * b_in.T * jnp.exp(-2.0 * rate_t) / root - sums[2]).T
    grad_gain_one, grad_gain_two = lax.psum((grad_gain_one, grad_gain_two), ("dp", "mp"))
    return (
        result,
        grad_tokens,
        grad_gain_one,
        grad_gain_two,
        grad_w_in,
        grad_w_query,
        grad_w_out,
        grad_w_up,
        grad_w_down,
        grad_rate,
        grad_b,
        grad_ck,
        grad_cv,
    )


def solution(mesh):
    placed = (
        P("dp", "mp"),
        P(),
        P(),
        P(None, "mp"),
        P(None, "mp"),
        P("mp", None),
        P(None, "mp"),
        P("mp", None),
        P("mp", None),
        P("mp", None),
        P("mp", None),
        P("mp", None),
        P("dp", None),
        P("dp", "mp"),
    )
    return jax.shard_map(
        on_device,
        mesh=mesh,
        in_specs=placed,
        out_specs=(
            P("dp", "mp"),
            P("dp", "mp"),
            P(),
            P(),
            P(None, "mp"),
            P(None, "mp"),
            P("mp", None),
            P(None, "mp"),
            P("mp", None),
            P("mp", None),
            P("mp", None),
            P("mp", None),
            P("mp", None),
        ),
        check_vma=False,
    )
```

```python
import functools

import jax
import jax.numpy as jnp
from jax import lax
from jax.experimental import pallas as pl
from jax.experimental.pallas import tpu as pltpu
from jax.sharding import PartitionSpec as P

HEAD = 128
BLOCK = 512
CTX = 128
LONG_DEV = 512
EPS = 1e-05
SEG = 8
GROUP = 8
STATES = 16
LANES = 128
VMEM = pl.BlockSpec(memory_space=pltpu.VMEM)
SMEM = pl.BlockSpec(memory_space=pltpu.SMEM)


def seg_scan_params(par_ref, wide_ref):
    for p in range(par_ref.shape[0]):
        for n in range(STATES):
            for lt in range(par_ref.shape[2] // LANES):
                row = par_ref[p, n : n + 1, lt * LANES : (lt + 1) * LANES]
                wide_ref[p, n, lt] = jnp.broadcast_to(row, (SEG, LANES))


def keep_mask(bounds_ref, span, step):
    rows = lax.broadcasted_iota(jnp.int32, (SEG, LANES), 0) * span + step
    keep = jnp.ones((SEG, LANES), jnp.float32)
    for k in range(bounds_ref.shape[0]):
        keep = jnp.where(rows == bounds_ref[k], 0.0, keep)
    return keep


def has_bound(bounds_ref, span, group):
    found = False
    for k in range(bounds_ref.shape[0]):
        b = bounds_ref[k]
        inside = lax.rem(b, span) // GROUP == group
        found = jnp.logical_or(found, jnp.logical_and(b >= 0, inside))
    return found


def steps_of(ref, lt, group, span):
    return [ref[lt, pl.ds(group * GROUP + j, SEG, stride=span), :] for j in range(GROUP)]


def split_lanes(src_ref, dst_ref):
    for lt in range(dst_ref.shape[0]):
        dst_ref[lt] = src_ref[:, lt * LANES : (lt + 1) * LANES].astype(jnp.float32)


def with_masks(bounds_ref, span, group, body):
    flag = has_bound(bounds_ref, span, group)

    @pl.when(flag)
    def _():
        body([keep_mask(bounds_ref, span, group * GROUP + j) for j in range(GROUP)])

    @pl.when(jnp.logical_not(flag))
    def _():
        body(None)


def forward_ends(bounds_ref, u_ref, wide_ref, state_ref, span, tiles):
    state_ref[...] = jnp.zeros_like(state_ref)

    @pl.loop(0, span // GROUP)
    def _(group):
        def body(keep):
            for lt in range(tiles):
                u = steps_of(u_ref, lt, group, span)
                for n in range(STATES):
                    a = wide_ref[0, n, lt]
                    s = state_ref[lt, n * SEG : (n + 1) * SEG, :]
                    for j in range(GROUP):
                        s = a * s
                        if keep is not None:
                            s = s * keep[j]
                        s = s + u[j]
                    state_ref[lt, n * SEG : (n + 1) * SEG, :] = s

        with_masks(bounds_ref, span, group, body)


def no_bound_in_seg(bounds_ref, span, seg):
    ok = jnp.float32(1.0)
    for k in range(bounds_ref.shape[0]):
        b = bounds_ref[k]
        inside = jnp.logical_and(b >= seg * span, b < (seg + 1) * span)
        ok = jnp.where(inside, jnp.float32(0.0), ok)
    return ok


def chain_forward(bounds_ref, state_ref, first, far_ref, span, tiles):
    for lt in range(tiles):
        lanes = slice(lt * LANES, (lt + 1) * LANES)
        start = first[:, lanes]
        far = far_ref[:, lanes]
        for seg in range(SEG):
            rows = pl.ds(seg, STATES, stride=SEG)
            end = state_ref[lt, rows, :]
            state_ref[lt, rows, :] = start
            start = end + far * start * no_bound_in_seg(bounds_ref, span, seg)


def chain_backward(bounds_ref, adj_ref, last, far_ref, span, tiles):
    for lt in range(tiles):
        lanes = slice(lt * LANES, (lt + 1) * LANES)
        start = last[:, lanes]
        far = far_ref[:, lanes]
        for seg in reversed(range(SEG)):
            rows = pl.ds(seg, STATES, stride=SEG)
            end = adj_ref[lt, rows, :]
            adj_ref[lt, rows, :] = start
            start = end + far * start * no_bound_in_seg(bounds_ref, span, seg)
        yield start


def ends_kernel(span, tiles, bounds_ref, u_in, par_ref, far_ref, out_ref, u_ref, wide_ref, state_ref):
    split_lanes(u_in, u_ref)
    seg_scan_params(par_ref, wide_ref)
    forward_ends(bounds_ref, u_ref, wide_ref, state_ref, span, tiles)
    for lt in range(tiles):
        lanes = slice(lt * LANES, (lt + 1) * LANES)
        start = jnp.zeros((STATES, LANES), jnp.float32)
        for seg in range(SEG):
            end = state_ref[lt, pl.ds(seg, STATES, stride=SEG), :]
            start = end + far_ref[:, lanes] * start * no_bound_in_seg(bounds_ref, span, seg)
        out_ref[:, lanes] = start


def forward_kernel(span, tiles, bounds_ref, u_in, par_ref, far_ref, first_ref, k_out, v_out, ckpt_ref,
                   u_ref, k_ref, v_ref, wide_ref, state_ref):
    split_lanes(u_in, u_ref)
    seg_scan_params(par_ref, wide_ref)
    forward_ends(bounds_ref, u_ref, wide_ref, state_ref, span, tiles)
    chain_forward(bounds_ref, state_ref, first_ref[...], far_ref, span, tiles)

    @pl.loop(0, span // GROUP)
    def _(group):
        def body(keep):
            for lt in range(tiles):
                u = steps_of(u_ref, lt, group, span)
                ks = [jnp.zeros((SEG, LANES), jnp.float32)] * GROUP
                vs = [jnp.zeros((SEG, LANES), jnp.float32)] * GROUP
                for n in range(STATES):
                    a, ck, cv = wide_ref[0, n, lt], wide_ref[1, n, lt], wide_ref[2, n, lt]
                    s = state_ref[lt, n * SEG : (n + 1) * SEG, :]
                    ckpt_ref[group, lt, n * SEG : (n + 1) * SEG, :] = s
                    for j in range(GROUP):
                        s = a * s
                        if keep is not None:
                            s = s * keep[j]
                        s = s + u[j]
                        ks[j] = ks[j] + ck * s
                        vs[j] = vs[j] + cv * s
                    state_ref[lt, n * SEG : (n + 1) * SEG, :] = s
                for j in range(GROUP):
                    rows = pl.ds(group * GROUP + j, SEG, stride=span)
                    k_ref[lt, rows, :] = ks[j]
                    v_ref[lt, rows, :] = vs[j]

        with_masks(bounds_ref, span, group, body)

    for lt in range(tiles):
        k_out[:, lt * LANES : (lt + 1) * LANES] = k_ref[lt].astype(k_out.dtype)
        v_out[:, lt * LANES : (lt + 1) * LANES] = v_ref[lt].astype(v_out.dtype)


def adjoint_ends(bounds_ref, gk_ref, gv_ref, wide_ref, adj_ref, span, tiles):
    adj_ref[...] = jnp.zeros_like(adj_ref)
    groups = span // GROUP

    @pl.loop(0, groups)
    def _(step):
        group = groups - 1 - step

        def body(keep):
            for lt in range(tiles):
                gk = steps_of(gk_ref, lt, group, span)
                gv = steps_of(gv_ref, lt, group, span)
                for n in range(STATES):
                    a, ck, cv = wide_ref[0, n, lt], wide_ref[1, n, lt], wide_ref[2, n, lt]
                    m = adj_ref[lt, n * SEG : (n + 1) * SEG, :]
                    for j in reversed(range(GROUP)):
                        m = a * (m + (ck * gk[j] + cv * gv[j]))
                        if keep is not None:
                            m = m * keep[j]
                    adj_ref[lt, n * SEG : (n + 1) * SEG, :] = m

        with_masks(bounds_ref, span, group, body)


def adjoint_ends_kernel(span, tiles, bounds_ref, gk_in, gv_in, par_ref, far_ref, out_ref, gk_ref, gv_ref, wide_ref, adj_ref):
    split_lanes(gk_in, gk_ref)
    split_lanes(gv_in, gv_ref)
    seg_scan_params(par_ref, wide_ref)
    adjoint_ends(bounds_ref, gk_ref, gv_ref, wide_ref, adj_ref, span, tiles)
    for lt in range(tiles):
        lanes = slice(lt * LANES, (lt + 1) * LANES)
        start = jnp.zeros((STATES, LANES), jnp.float32)
        for seg in reversed(range(SEG)):
            end = adj_ref[lt, pl.ds(seg, STATES, stride=SEG), :]
            start = end + far_ref[:, lanes] * start * no_bound_in_seg(bounds_ref, span, seg)
        out_ref[:, lanes] = start


def backward_kernel(span, tiles, bounds_ref, u_in, gk_in, gv_in, par_ref, far_ref, last_ref, ckpt_ref,
                    gu_out, sums_out, u_ref, gk_ref, gv_ref, gu_ref, wide_ref, adj_ref, acc_ref):
    split_lanes(u_in, u_ref)
    split_lanes(gk_in, gk_ref)
    split_lanes(gv_in, gv_ref)
    seg_scan_params(par_ref, wide_ref)
    adjoint_ends(bounds_ref, gk_ref, gv_ref, wide_ref, adj_ref, span, tiles)
    for _ in chain_backward(bounds_ref, adj_ref, last_ref[...], far_ref, span, tiles):
        pass
    acc_ref[...] = jnp.zeros_like(acc_ref)
    groups = span // GROUP

    @pl.loop(0, groups)
    def _(step):
        group = groups - 1 - step

        def body(keep):
            for lt in range(tiles):
                u = steps_of(u_ref, lt, group, span)
                gk = steps_of(gk_ref, lt, group, span)
                gv = steps_of(gv_ref, lt, group, span)
                gu = [jnp.zeros((SEG, LANES), jnp.float32)] * GROUP
                for n in range(STATES):
                    mine = slice(n * SEG, (n + 1) * SEG)
                    a, ck, cv = wide_ref[0, n, lt], wide_ref[1, n, lt], wide_ref[2, n, lt]
                    states = [ckpt_ref[group, lt, mine, :]]
                    for j in range(GROUP):
                        s = a * states[j]
                        if keep is not None:
                            s = s * keep[j]
                        states.append(s + u[j])
                    m = adj_ref[lt, mine, :]
                    sum_k, sum_v, sum_a = acc_ref[0, lt, mine, :], acc_ref[1, lt, mine, :], acc_ref[2, lt, mine, :]
                    for j in reversed(range(GROUP)):
                        lam = m + (ck * gk[j] + cv * gv[j])
                        gu[j] = gu[j] + lam
                        sum_k = sum_k + gk[j] * states[j + 1]
                        sum_v = sum_v + gv[j] * states[j + 1]
                        m = a * lam
                        if keep is not None:
                            m = m * keep[j]
                        sum_a = sum_a + m * states[j]
                    acc_ref[0, lt, mine, :] = sum_k
                    acc_ref[1, lt, mine, :] = sum_v
                    acc_ref[2, lt, mine, :] = sum_a
                    adj_ref[lt, mine, :] = m
                for j in range(GROUP):
                    gu_ref[lt, pl.ds(group * GROUP + j, SEG, stride=span), :] = gu[j]

        with_masks(bounds_ref, span, group, body)

    for lt in range(tiles):
        lanes = slice(lt * LANES, (lt + 1) * LANES)
        gu_out[:, lanes] = gu_ref[lt].astype(gu_out.dtype)
        for p in range(3):
            total = acc_ref[p, lt, pl.ds(0, STATES, stride=SEG), :]
            for seg in range(1, SEG):
                total = total + acc_ref[p, lt, pl.ds(seg, STATES, stride=SEG), :]
            sums_out[p, :, lanes] = total


LIMIT = pltpu.CompilerParams(vmem_limit_bytes=48 * 2**20)


def f32(*shape):
    return pltpu.VMEM(shape, jnp.float32)


def ssm_ends(bounds, u, par, far, name="ssm_ends"):
    rows, width = u.shape
    span, tiles = rows // SEG, width // LANES
    return pl.pallas_call(
        functools.partial(ends_kernel, span, tiles),
        out_shape=jax.ShapeDtypeStruct((STATES, width), jnp.float32),
        in_specs=[SMEM] + [VMEM] * 3, out_specs=VMEM,
        scratch_shapes=[f32(tiles, rows, LANES), f32(3, STATES, tiles, SEG, LANES), f32(tiles, STATES * SEG, LANES)],
        compiler_params=LIMIT, name=name)(bounds, u, par, far)


def ssm_forward(bounds, u, par, far, first, name="ssm_forward"):
    rows, width = u.shape
    span, tiles = rows // SEG, width // LANES
    return pl.pallas_call(
        functools.partial(forward_kernel, span, tiles),
        out_shape=(jax.ShapeDtypeStruct((rows, width), jnp.bfloat16), jax.ShapeDtypeStruct((rows, width), jnp.bfloat16),
                   jax.ShapeDtypeStruct((span // GROUP, tiles, STATES * SEG, LANES), jnp.float32)),
        in_specs=[SMEM] + [VMEM] * 4, out_specs=(VMEM,) * 3,
        scratch_shapes=[f32(tiles, rows, LANES)] * 3 + [f32(3, STATES, tiles, SEG, LANES), f32(tiles, STATES * SEG, LANES)],
        compiler_params=LIMIT, name=name)(bounds, u, par, far, first)


def ssm_adjoint_ends(bounds, gk, gv, par, far, name="ssm_adjoint_ends"):
    rows, width = gk.shape
    span, tiles = rows // SEG, width // LANES
    return pl.pallas_call(
        functools.partial(adjoint_ends_kernel, span, tiles),
        out_shape=jax.ShapeDtypeStruct((STATES, width), jnp.float32),
        in_specs=[SMEM] + [VMEM] * 4, out_specs=VMEM,
        scratch_shapes=[f32(tiles, rows, LANES)] * 2 + [f32(3, STATES, tiles, SEG, LANES), f32(tiles, STATES * SEG, LANES)],
        compiler_params=LIMIT, name=name)(bounds, gk, gv, par, far)


def ssm_backward(bounds, u, gk, gv, par, far, last, ckpt, name="ssm_backward"):
    rows, width = u.shape
    span, tiles = rows // SEG, width // LANES
    return pl.pallas_call(
        functools.partial(backward_kernel, span, tiles),
        out_shape=(jax.ShapeDtypeStruct((rows, width), jnp.bfloat16), jax.ShapeDtypeStruct((3, STATES, width), jnp.float32)),
        in_specs=[SMEM] + [VMEM] * 7, out_specs=(VMEM,) * 2,
        scratch_shapes=[f32(tiles, rows, LANES)] * 4 + [f32(3, STATES, tiles, SEG, LANES), f32(tiles, STATES * SEG, LANES), f32(3, tiles, STATES * SEG, LANES)],
        compiler_params=LIMIT, name=name)(bounds, u, gk, gv, par, far, last, ckpt)


QT = 256
NEG = -1e30
SCALE = HEAD ** (-0.5)


def tiles_of(rows, shift):
    out = []
    for r in range(0, rows, QT):
        first = max(0, r + shift - (BLOCK + CTX)) if shift == 0 else 0
        out.append((r, first, r + shift + QT))
    return out


def lowest_key(starts_ref, row0, shift):
    if shift:
        return jnp.full((1, QT), starts_ref[0], jnp.int32)
    rows = lax.broadcasted_iota(jnp.int32, (1, QT), 1) + row0
    start = jnp.zeros((1, QT), jnp.int32)
    for k in range(starts_ref.shape[0]):
        start = jnp.where(rows >= starts_ref[k], starts_ref[k], start)
    block = ((rows - start) // BLOCK) * BLOCK - CTX
    return start + jnp.maximum(block, 0)


def allowed_keys(starts_ref, q0, k0, k1, shift):
    low = lowest_key(starts_ref, q0, shift)
    high = lax.broadcasted_iota(jnp.int32, (1, QT), 1) + (q0 + shift)
    keys = lax.broadcasted_iota(jnp.int32, (k1 - k0, QT), 0) + k0
    return (keys >= low) & (keys <= high)


def dot_nt(a, b):
    return lax.dot_general(a, b, (((1,), (1,)), ((), ())), preferred_element_type=jnp.float32)


def dot_nn(a, b):
    return lax.dot_general(a, b, (((1,), (0,)), ((), ())), preferred_element_type=jnp.float32)


def attend_kernel(tiles, shift, starts_ref, q_ref, k_ref, v_ref, o_ref, lse_ref, vt_ref):
    vt_ref[...] = v_ref[...].T
    for q0, k0, k1 in tiles:
        scores = dot_nt(k_ref[k0:k1, :], q_ref[q0 : q0 + QT, :]) * SCALE
        scores = jnp.where(allowed_keys(starts_ref, q0, k0, k1, shift), scores, NEG)
        top = jnp.max(scores, axis=0, keepdims=True)
        exps = jnp.exp(scores - top)
        total = jnp.sum(exps, axis=0, keepdims=True)
        probs = (exps * (1.0 / total)).astype(jnp.bfloat16)
        mixed = dot_nn(vt_ref[:, k0:k1], probs)
        o_ref[q0 : q0 + QT, :] = mixed.T.astype(o_ref.dtype)
        lse_ref[0, 0, q0 : q0 + QT] = (top + jnp.log(total))[0]


def attend(starts, q, k, v, shift, name):
    rows, width = q.shape
    heads = width // HEAD
    keys = k.shape[0]
    lane = lambda h: (0, h)
    return pl.pallas_call(
        functools.partial(attend_kernel, tiles_of(rows, shift), shift),
        grid=(heads,),
        out_shape=(jax.ShapeDtypeStruct((rows, width), jnp.bfloat16), jax.ShapeDtypeStruct((heads, 1, rows), jnp.float32)),
        in_specs=[SMEM, pl.BlockSpec((rows, HEAD), lane), pl.BlockSpec((keys, HEAD), lane), pl.BlockSpec((keys, HEAD), lane)],
        out_specs=(pl.BlockSpec((rows, HEAD), lane), pl.BlockSpec((1, 1, rows), lambda h: (h, 0, 0))),
        scratch_shapes=[pltpu.VMEM((HEAD, keys), jnp.bfloat16)],
        compiler_params=pltpu.CompilerParams(vmem_limit_bytes=40 * 2**20),
        name=name)(starts, q, k, v)


def attend_back_kernel(tiles, shift, starts_ref, q_ref, k_ref, v_ref, g_ref, lse_ref, dq_ref, dk_ref, dv_ref, kt_ref):
    kt_ref[...] = k_ref[...].T
    dk_ref[...] = jnp.zeros_like(dk_ref)
    dv_ref[...] = jnp.zeros_like(dv_ref)
    for q0, k0, k1 in tiles:
        q = q_ref[q0 : q0 + QT, :]
        g = g_ref[q0 : q0 + QT, :]
        lse = lse_ref[0, :, q0 : q0 + QT]
        scores = dot_nt(k_ref[k0:k1, :], q) * SCALE
        probs = jnp.where(allowed_keys(starts_ref, q0, k0, k1, shift), jnp.exp(scores - lse), 0.0)
        grad_probs = dot_nt(v_ref[k0:k1, :], g)
        dv_ref[k0:k1, :] += dot_nn(probs.astype(jnp.bfloat16), g)
        delta = jnp.sum(probs * grad_probs, axis=0, keepdims=True)
        grad_scores = (probs * (grad_probs - delta)).astype(jnp.bfloat16)
        dk_ref[k0:k1, :] += dot_nn(grad_scores, q) * SCALE
        dq_ref[q0 : q0 + QT, :] = (dot_nn(kt_ref[:, k0:k1], grad_scores) * SCALE).T.astype(dq_ref.dtype)


def attend_back(starts, q, k, v, g, lse, shift, name):
    rows, width = q.shape
    heads = width // HEAD
    keys = k.shape[0]
    lane = lambda h: (0, h)
    rspec, kspec = pl.BlockSpec((rows, HEAD), lane), pl.BlockSpec((keys, HEAD), lane)
    return pl.pallas_call(
        functools.partial(attend_back_kernel, tiles_of(rows, shift), shift),
        grid=(heads,),
        out_shape=(jax.ShapeDtypeStruct((rows, width), jnp.bfloat16), jax.ShapeDtypeStruct((keys, width), jnp.float32), jax.ShapeDtypeStruct((keys, width), jnp.float32)),
        in_specs=[SMEM, rspec, kspec, kspec, rspec, pl.BlockSpec((1, 1, rows), lambda h: (h, 0, 0))],
        out_specs=(rspec, kspec, kspec),
        scratch_shapes=[pltpu.VMEM((HEAD, keys), jnp.bfloat16)],
        compiler_params=pltpu.CompilerParams(vmem_limit_bytes=40 * 2**20),
        name=name)(starts, q, k, v, g, lse)


ROWS = 256
SUB = 32
DEEP = 3
MESH = pl.DeviceIdType.MESH


def group_of_four():
    me = lax.axis_index("mp")
    mate = me + 1 - 2 * (me % 2)
    return me, mate, (me + 2) % 4, (mate + 2) % 4


def greet_group():
    _, mate, over, _ = group_of_four()
    dp = lax.axis_index("dp")
    barrier = pltpu.get_barrier_semaphore()
    for peer in (mate, over):
        pl.semaphore_signal(barrier, inc=1, device_id=(dp, peer), device_id_type=MESH)
    pl.semaphore_wait(barrier, 2)


class Mover:
    def __init__(self, send_sem, recv_sem):
        self.send_sem, self.recv_sem = send_sem, recv_sem
        self.dp = lax.axis_index("dp")

    def copy(self, src, dst, kind, c, peer):
        return pltpu.make_async_remote_copy(
            src_ref=src, dst_ref=dst, send_sem=self.send_sem.at[kind, c], recv_sem=self.recv_sem.at[kind, c],
            device_id=(self.dp, peer), device_id_type=MESH)


class Gather:
    def __init__(self, mover, base, full, rows):
        self.mover, self.base, self.full, self.rows = mover, base, full, rows
        self.me, self.mate, self.over, self.far = group_of_four()

    def at(self, owner, c):
        return self.full.at[owner, pl.ds(pl.multiple_of(c * self.rows, self.rows), self.rows)]

    def near(self, c):
        return self.mover.copy(self.at(self.me, c), self.at(self.me, c), self.base, c, self.mate)

    def across(self, c):
        return self.mover.copy(self.at(self.me, c), self.at(self.me, c), self.base + 1, c, self.over)

    def onward(self, c):
        return self.mover.copy(self.at(self.over, c), self.at(self.over, c), self.base + 2, c, self.mate)

    def start(self, c):
        self.across(c).start()
        self.near(c).start()

    def forward(self, c):
        self.across(c).wait_recv()
        self.onward(c).start()

    def finish(self, c):
        self.near(c).wait()
        self.across(c).wait_send()
        self.onward(c).wait()


class Scatter:
    def __init__(self, mover, base, part, near, across, joint):
        self.mover, self.base = mover, base
        self.part, self.near, self.across, self.joint = part, near, across, joint
        self.me, self.mate, self.over, self.far = group_of_four()

    def to_join(self, c):
        return self.mover.copy(self.part.at[c % DEEP, self.far], self.near.at[c, 1], self.base + 1, c, self.mate)

    def to_keep(self, c):
        return self.mover.copy(self.part.at[c % DEEP, self.mate], self.near.at[c, 0], self.base, c, self.mate)

    def joined(self, c):
        return self.mover.copy(self.joint.at[c % DEEP], self.across.at[c], self.base + 2, c, self.over)

    def start(self, c, parts):
        for d in range(4):
            self.part[c % DEEP, d] = parts(d).astype(jnp.bfloat16)
        self.to_join(c).start()
        self.to_keep(c).start()

    def combine(self, c):
        s = c % DEEP
        self.to_join(c).wait_recv()
        self.joint[s] = (self.part[s, self.over].astype(jnp.float32) + self.near[c, 1].astype(jnp.float32)).astype(jnp.bfloat16)
        self.joined(c).start()

    def finish(self, c):
        self.to_join(c).wait_send()
        self.to_keep(c).wait()
        self.joined(c).wait()
        return (self.part[c % DEEP, self.me].astype(jnp.float32) + self.near[c, 0].astype(jnp.float32)
                + self.across[c].astype(jnp.float32))


def mm(left, right, left_dim, right_dim):
    return lax.dot_general(left, right, (((left_dim,), (right_dim,)), ((), ())), preferred_element_type=jnp.float32)


def cut(d, width):
    return slice(d * width, (d + 1) * width)


def normed(full, c, sub, rows):
    first = pl.multiple_of(c * rows + sub * SUB, SUB)
    return jnp.concatenate([full[d, pl.ds(first, SUB), :].astype(jnp.float32) for d in range(4)], axis=1)


def middle_kernel(chunks, att_ref, tok_ref, cot_ref, w_out_ref, w_up_ref, w_down_ref, gain_ref,
                  result_ref, gm_ref, gatt_ref, gdown_ref, gup_ref, gout_ref, ggain_ref,
                  mid_full, gm_full, mid_ref, part, near, across, joint, n2_ref, act_ref, gpre_ref, pre_ref, gact_ref, mean_ref, inv_ref,
                  send_sem, recv_sem):
    width = att_ref.shape[1]
    rows = ROWS
    me = lax.axis_index("mp")
    mover = Mover(send_sem, recv_sem)
    sums = [Scatter(mover, 3 * r, part.at[r], near.at[r], across.at[r], joint.at[r]) for r in range(3)]
    gather_mid = Gather(mover, 9, mid_full, rows)
    gather_gm = Gather(mover, 12, gm_full, rows)
    greet_group()
    gdown_ref[...] = jnp.zeros_like(gdown_ref)
    gup_ref[...] = jnp.zeros_like(gup_ref)
    gout_ref[...] = jnp.zeros_like(gout_ref)
    ggain_ref[...] = jnp.zeros_like(ggain_ref)

    def span(c):
        return pl.ds(pl.multiple_of(c * rows, rows), rows)

    def project(c):
        att = att_ref[span(c), :]
        sums[0].start(c, lambda d: mm(att, w_out_ref[:, cut(d, width)], 1, 0))

    def add_middle(c):
        middle = tok_ref[span(c), :].astype(jnp.float32) + sums[0].finish(c)
        mid_ref[span(c), :] = middle
        mid_full[me, span(c), :] = middle.astype(jnp.bfloat16)
        gather_mid.start(c)

    def feed_forward(c):
        gather_mid.finish(c)

        @pl.loop(0, rows // SUB)
        def _(sub):
            mine = pl.ds(pl.multiple_of(sub * SUB, SUB), SUB)
            v = normed(mid_full, c, sub, rows)
            mean = jnp.mean(v, axis=1, keepdims=True)
            centred = v - mean
            inv = lax.rsqrt(jnp.mean(centred * centred, axis=1, keepdims=True) + EPS)
            mean_ref[mine, :] = mean
            inv_ref[mine, :] = inv
            n2_ref[mine, :] = (centred * inv * gain_ref[...]).astype(jnp.bfloat16)

        cot = cot_ref[span(c), :]
        pre_ref[...] = mm(n2_ref[...], w_up_ref[...], 1, 0)
        gact_ref[...] = mm(cot, w_down_ref[...], 1, 1)

        @pl.loop(0, rows // SUB)
        def _(sub):
            mine = pl.ds(pl.multiple_of(sub * SUB, SUB), SUB)
            v = pre_ref[mine, :]
            cdf = 0.5 * (1.0 + lax.erf(v * (0.5**0.5)))
            act_ref[mine, :] = (v * cdf).astype(jnp.bfloat16)
            slope = cdf + v * (jnp.exp(-0.5 * v * v) * 0.3989422804014327)
            gpre_ref[mine, :] = (slope * gact_ref[mine, :]).astype(jnp.bfloat16)

        sums[1].start(c, lambda d: mm(act_ref[...], w_down_ref[:, cut(d, width)], 1, 0))
        gact_ref[...] = mm(gpre_ref[...], w_up_ref[...], 1, 1)

        @pl.loop(0, rows // SUB)
        def _(sub):
            mine = pl.ds(pl.multiple_of(sub * SUB, SUB), SUB)
            xhat = (normed(mid_full, c, sub, rows) - mean_ref[mine, :]) * inv_ref[mine, :]
            up = gact_ref[mine, :]
            both = up * xhat
            ggain_ref[...] += jnp.sum(both.reshape(SUB // 8, 8, both.shape[1]), axis=0)
            scaled = up * gain_ref[...]
            plain = jnp.mean(scaled, axis=1, keepdims=True)
            cross = jnp.mean(scaled * xhat, axis=1, keepdims=True)
            gact_ref[mine, :] = inv_ref[mine, :] * (scaled - plain - xhat * cross)

        sums[2].start(c, lambda d: gact_ref[:, cut(d, width)])
        gdown_ref[...] += mm(act_ref[...], cot, 0, 0)
        gup_ref[...] += mm(n2_ref[...], gpre_ref[...], 0, 0)

    def finish_sums(c):
        own = pl.ds(pl.multiple_of(me * width, width), width)
        gm = cot_ref[span(c), own].astype(jnp.float32) + sums[2].finish(c)
        gm_ref[span(c), :] = gm
        gm_full[me, span(c), :] = gm.astype(jnp.bfloat16)
        gather_gm.start(c)
        result_ref[span(c), :] = (mid_ref[span(c), :] + sums[1].finish(c)).astype(result_ref.dtype)

    def back_project(c):
        gather_gm.finish(c)
        att = att_ref[span(c), :]
        total = None
        for d in range(4):
            gm = gm_full[d, span(c), :]
            gout_ref[:, cut(d, width)] += mm(att, gm, 0, 0)
            term = mm(gm, w_out_ref[:, cut(d, width)], 1, 1)
            total = term if total is None else total + term
        gatt_ref[span(c), :] = total.astype(gatt_ref.dtype)

    def combine_late(c):
        sums[2].combine(c)
        sums[1].combine(c)

    stages = [(add_middle, 2), (finish_sums, 6), (sums[0].combine, 1), (combine_late, 5), (gather_mid.forward, 3),
              (gather_gm.forward, 7), (project, 0), (feed_forward, 4), (back_project, 8)]

    @pl.loop(0, chunks + 8)
    def _(i):
        for stage, lag in stages:
            @pl.when(jnp.logical_and(i >= lag, i < chunks + lag))
            def _(stage=stage, lag=lag):
                stage(i - lag)


def middle_phase(att, tok, cot_full, w_out, w_up, w_down, gain):
    rows, width = att.shape
    full = cot_full.shape[1]
    hidden = w_up.shape[1]
    chunks = rows // ROWS
    bf = jnp.bfloat16

    def out(shape, dtype):
        return jax.ShapeDtypeStruct(shape, dtype)

    def buf(*shape, dtype=bf):
        return pltpu.VMEM(shape, dtype)

    return pl.pallas_call(
        functools.partial(middle_kernel, chunks),
        out_shape=(out((rows, width), bf), out((rows, width), jnp.float32), out((rows, width), bf),
                   out((hidden, full), jnp.float32), out((full, hidden), jnp.float32), out((width, full), jnp.float32),
                   out((8, full), jnp.float32)),
        in_specs=[VMEM] * 7, out_specs=(VMEM,) * 7,
        scratch_shapes=[
            buf(4, rows, width), buf(4, rows, width), buf(rows, width, dtype=jnp.float32),
            buf(3, DEEP, 4, ROWS, width), buf(3, chunks, 2, ROWS, width), buf(3, chunks, ROWS, width), buf(3, DEEP, ROWS, width),
            buf(ROWS, full), buf(ROWS, hidden), buf(ROWS, hidden),
            buf(ROWS, hidden, dtype=jnp.float32), buf(ROWS, hidden, dtype=jnp.float32),
            buf(ROWS, 1, dtype=jnp.float32), buf(ROWS, 1, dtype=jnp.float32),
            pltpu.SemaphoreType.DMA((15, chunks)), pltpu.SemaphoreType.DMA((15, chunks)),
        ],
        compiler_params=pltpu.CompilerParams(collective_id=0, has_side_effects=True, vmem_limit_bytes=60 * 2**20),
        cost_estimate=pl.CostEstimate(flops=30 * 10**9, bytes_accessed=30 * 10**6, transcendentals=4 * 10**6),
        name="middle_phase")(att, tok, cot_full, w_out, w_up, w_down, gain)


def gather_features(values_in):
    return lax.all_gather(values_in, "mp", axis=1, tiled=True)


def reduce_features(values_in):
    return lax.psum_scatter(
        values_in.astype(jnp.bfloat16), "mp", scatter_dimension=1, tiled=True
    ).astype(jnp.float32)


def from_behind(value, axis, steps):
    count = lax.axis_size(axis)
    initial, last = (max(0, -steps), min(count, count - steps))
    return lax.ppermute(value, axis, [(source, source + steps) for source in range(initial, last)])


def norm_forward(values_in, gain_vec):
    row_mean = jnp.mean(values_in, axis=1, keepdims=True)
    centred = values_in - row_mean
    row_var = jnp.mean(centred * centred, axis=1, keepdims=True)
    inverse = lax.rsqrt(row_var + EPS)
    normed = centred * inverse
    return (normed, inverse, normed * gain_vec)


def norm_backward(upstream, normed, inverse, gain_vec):
    gain_grad = jnp.sum(upstream * normed, axis=0)
    scaled = upstream * gain_vec
    plain_mean = jnp.mean(scaled, axis=1, keepdims=True)
    cross_mean = jnp.mean(scaled * normed, axis=1, keepdims=True)
    return (inverse * (scaled - plain_mean - normed * cross_mean), gain_grad)


def gelu_exact(values_in):
    return jax.nn.gelu(values_in, approximate=False)


def fold_pieces(pieces, decay_rate, gap_count):
    live_rows = gap_count >= 0
    weights = jnp.exp(
        -decay_rate[None]
        * (LONG_DEV * jnp.maximum(gap_count, 0)).astype(jnp.float32)[:, None, None]
    )
    return jnp.sum(jnp.where(live_rows[:, None, None], weights * pieces, 0.0), axis=0)


def dot(left, right, dims):
    return lax.dot_general(left, right, ((dims[0], dims[1]), ((), ())), preferred_element_type=jnp.float32)


def on_device(
    tokens,
    gain_one,
    gain_two,
    w_in,
    w_query,
    w_out,
    w_up,
    w_down,
    decay_rate,
    b_in,
    c_key,
    c_val,
    short_lengths,
    cotangent,
):
    low = jnp.bfloat16
    device = lax.axis_index("dp")
    lengths = short_lengths[0]
    ends = jnp.cumsum(lengths).astype(jnp.int32)
    short_starts = jnp.concatenate([jnp.zeros((1,), jnp.int32), ends[:-1]])
    no_bound = jnp.full((1,), -1, jnp.int32)
    long_low = jnp.where(device > 0, 0, CTX).astype(jnp.int32).reshape(1)
    rate_t = decay_rate.T
    root = jnp.sqrt(-jnp.expm1(-2.0 * rate_t))
    drive = root * b_in.T
    ck_t, cv_t = c_key.T, c_val.T
    decay = jnp.exp(-rate_t)
    par = jnp.stack([decay, drive * ck_t, drive * cv_t])
    short_rows = tokens.shape[0] - LONG_DEV
    far_long = jnp.exp(-rate_t * (LONG_DEV // SEG))
    far_short = jnp.exp(-rate_t * (short_rows // SEG))

    tokens_full = gather_features(tokens).astype(jnp.float32)
    cotangent_full = gather_features(cotangent)
    normed_one, inverse_one, hidden_one = norm_forward(tokens_full, gain_one)
    normed_one_low = hidden_one.astype(low)
    ssm_input = jnp.dot(normed_one_low, w_in, preferred_element_type=jnp.float32)
    queries = jnp.dot(normed_one_low, w_query, preferred_element_type=jnp.float32).astype(low)
    u_long, u_short = ssm_input[:LONG_DEV], ssm_input[LONG_DEV:]
    local_end = ssm_ends(no_bound, u_long, par, far_long)
    pieces = lax.all_gather(local_end[None], "dp", axis=0, tiled=True)
    others = jnp.arange(pieces.shape[0], dtype=jnp.int32)
    state_in = fold_pieces(pieces, rate_t, device - 1 - others)
    zero_state = jnp.zeros_like(state_in)
    k_short, v_short, ckpt_short = ssm_forward(short_starts, u_short, par, far_short, zero_state, "ssm_short")
    k_long, v_long, ckpt_long = ssm_forward(no_bound, u_long, par, far_long, state_in, "ssm_long")
    ctx_k, ctx_v = from_behind((k_long[LONG_DEV - CTX :], v_long[LONG_DEV - CTX :]), "dp", 1)
    k_long = jnp.concatenate([ctx_k, k_long])
    v_long = jnp.concatenate([ctx_v, v_long])
    q_long, q_short = queries[:LONG_DEV], queries[LONG_DEV:]
    att_short, lse_short = attend(short_starts, q_short, k_short, v_short, 0, "attend_short")
    att_long, lse_long = attend(long_low, q_long, k_long, v_long, CTX, "attend_long")
    attended = jnp.concatenate([att_long, att_short])
    result, grad_middle, grad_attended, grad_w_down, grad_w_up, grad_w_out, gain_parts = middle_phase(
        attended, tokens, cotangent_full, w_out, w_up, w_down, gain_two[None]
    )
    grad_gain_two = jnp.sum(gain_parts, axis=0)

    gq_long, gk_long, gv_long = attend_back(
        long_low, q_long, k_long, v_long, grad_attended[:LONG_DEV], lse_long, CTX, "attend_back_long"
    )
    back_k, back_v = from_behind((gk_long[:CTX].astype(low), gv_long[:CTX].astype(low)), "dp", -1)
    gq_short, gk_short, gv_short = attend_back(
        short_starts, q_short, k_short, v_short, grad_attended[LONG_DEV:], lse_short, 0, "attend_back_short"
    )
    gk_long = gk_long[CTX:].at[LONG_DEV - CTX :].add(back_k.astype(jnp.float32))
    gv_long = gv_long[CTX:].at[LONG_DEV - CTX :].add(back_v.astype(jnp.float32))
    local_in = ssm_adjoint_ends(no_bound, gk_long, gv_long, par, far_long)
    grad_pieces = lax.all_gather(local_in[None], "dp", axis=0, tiled=True)
    grad_end = fold_pieces(grad_pieces, rate_t, others - device - 1)
    gu_short, sums_short = ssm_backward(
        short_starts, u_short, gk_short, gv_short, par, far_short, zero_state, ckpt_short, "ssm_back_short"
    )
    gu_long, sums_long = ssm_backward(
        no_bound, u_long, gk_long, gv_long, par, far_long, grad_end, ckpt_long, "ssm_back_long"
    )
    sums = sums_short + sums_long
    grad_ssm = jnp.concatenate([gu_long, gu_short])
    grad_queries = jnp.concatenate([gq_long, gq_short])
    grad_w_in = dot(normed_one_low, grad_ssm, ((0,), (0,)))
    grad_w_query = dot(normed_one_low, grad_queries, ((0,), (0,)))
    grad_hidden_one = dot(grad_ssm, w_in, ((1,), (1,))) + dot(grad_queries, w_query, ((1,), (1,)))
    token_part, grad_gain_one = norm_backward(grad_hidden_one, normed_one, inverse_one, gain_one)
    grad_tokens = (grad_middle + reduce_features(token_part)).astype(low)

    grad_w_in, grad_w_query, grad_w_out, grad_w_up, grad_w_down = (
        g.astype(jnp.float32)
        for g in lax.psum(
            tuple(g.astype(low) for g in (grad_w_in, grad_w_query, grad_w_out, grad_w_up, grad_w_down)), "dp"
        )
    )
    sums = lax.psum(sums, "dp")
    grad_ck = (drive * sums[0]).T
    grad_cv = (drive * sums[1]).T
    grad_drive = ck_t * sums[0] + cv_t * sums[1]
    grad_b = (root * grad_drive).T
    grad_rate = (grad_drive * b_in.T * jnp.exp(-2.0 * rate_t) / root - sums[2]).T
    grad_gain_one, grad_gain_two = lax.psum((grad_gain_one, grad_gain_two), ("dp", "mp"))
    return (
        result,
        grad_tokens,
        grad_gain_one,
        grad_gain_two,
        grad_w_in,
        grad_w_query,
        grad_w_out,
        grad_w_up,
        grad_w_down,
        grad_rate,
        grad_b,
        grad_ck,
        grad_cv,
    )


def solution(mesh):
    placed = (
        P("dp", "mp"),
        P(),
        P(),
        P(None, "mp"),
        P(None, "mp"),
        P("mp", None),
        P(None, "mp"),
        P("mp", None),
        P("mp", None),
        P("mp", None),
        P("mp", None),
        P("mp", None),
        P("dp", None),
        P("dp", "mp"),
    )
    return jax.shard_map(
        on_device,
        mesh=mesh,
        in_specs=placed,
        out_specs=(
            P("dp", "mp"),
            P("dp", "mp"),
            P(),
            P(),
            P(None, "mp"),
            P(None, "mp"),
            P("mp", None),
            P(None, "mp"),
            P("mp", None),
            P("mp", None),
            P("mp", None),
            P("mp", None),
            P("mp", None),
        ),
        check_vma=False,
    )
```

```python
import functools

import jax
import jax.numpy as jnp
from jax import lax
from jax.experimental import pallas as pl
from jax.experimental.pallas import tpu as pltpu
from jax.sharding import PartitionSpec as P

HEAD = 128
BLOCK = 512
CTX = 128
LONG_DEV = 512
EPS = 1e-05
SEG = 8
GROUP = 8
STATES = 16
LANES = 128
VMEM = pl.BlockSpec(memory_space=pltpu.VMEM)
SMEM = pl.BlockSpec(memory_space=pltpu.SMEM)


def seg_scan_params(par_ref, wide_ref):
    for p in range(par_ref.shape[0]):
        for n in range(STATES):
            for lt in range(par_ref.shape[2] // LANES):
                row = par_ref[p, n : n + 1, lt * LANES : (lt + 1) * LANES]
                wide_ref[p, n, lt] = jnp.broadcast_to(row, (SEG, LANES))


def keep_mask(bounds_ref, span, step):
    rows = lax.broadcasted_iota(jnp.int32, (SEG, LANES), 0) * span + step
    keep = jnp.ones((SEG, LANES), jnp.float32)
    for k in range(bounds_ref.shape[0]):
        keep = jnp.where(rows == bounds_ref[k], 0.0, keep)
    return keep


def has_bound(bounds_ref, span, group):
    found = False
    for k in range(bounds_ref.shape[0]):
        b = bounds_ref[k]
        inside = lax.rem(b, span) // GROUP == group
        found = jnp.logical_or(found, jnp.logical_and(b >= 0, inside))
    return found


def steps_of(ref, lt, group, span):
    return [ref[lt, pl.ds(group * GROUP + j, SEG, stride=span), :] for j in range(GROUP)]


def split_lanes(src_ref, dst_ref):
    for lt in range(dst_ref.shape[0]):
        dst_ref[lt] = src_ref[:, lt * LANES : (lt + 1) * LANES].astype(jnp.float32)


def with_masks(bounds_ref, span, group, body):
    flag = has_bound(bounds_ref, span, group)

    @pl.when(flag)
    def _():
        body([keep_mask(bounds_ref, span, group * GROUP + j) for j in range(GROUP)])

    @pl.when(jnp.logical_not(flag))
    def _():
        body(None)


def forward_ends(bounds_ref, u_ref, wide_ref, state_ref, span, tiles):
    state_ref[...] = jnp.zeros_like(state_ref)

    @pl.loop(0, span // GROUP)
    def _(group):
        def body(keep):
            for lt in range(tiles):
                u = steps_of(u_ref, lt, group, span)
                for n in range(STATES):
                    a = wide_ref[0, n, lt]
                    s = state_ref[lt, n * SEG : (n + 1) * SEG, :]
                    for j in range(GROUP):
                        s = a * s
                        if keep is not None:
                            s = s * keep[j]
                        s = s + u[j]
                    state_ref[lt, n * SEG : (n + 1) * SEG, :] = s

        with_masks(bounds_ref, span, group, body)


def no_bound_in_seg(bounds_ref, span, seg):
    ok = jnp.float32(1.0)
    for k in range(bounds_ref.shape[0]):
        b = bounds_ref[k]
        inside = jnp.logical_and(b >= seg * span, b < (seg + 1) * span)
        ok = jnp.where(inside, jnp.float32(0.0), ok)
    return ok


def chain_forward(bounds_ref, state_ref, first, far_ref, span, tiles):
    for lt in range(tiles):
        lanes = slice(lt * LANES, (lt + 1) * LANES)
        start = first[:, lanes]
        far = far_ref[:, lanes]
        for seg in range(SEG):
            rows = pl.ds(seg, STATES, stride=SEG)
            end = state_ref[lt, rows, :]
            state_ref[lt, rows, :] = start
            start = end + far * start * no_bound_in_seg(bounds_ref, span, seg)


def chain_backward(bounds_ref, adj_ref, last, far_ref, span, tiles):
    for lt in range(tiles):
        lanes = slice(lt * LANES, (lt + 1) * LANES)
        start = last[:, lanes]
        far = far_ref[:, lanes]
        for seg in reversed(range(SEG)):
            rows = pl.ds(seg, STATES, stride=SEG)
            end = adj_ref[lt, rows, :]
            adj_ref[lt, rows, :] = start
            start = end + far * start * no_bound_in_seg(bounds_ref, span, seg)
        yield start


def ends_kernel(span, tiles, bounds_ref, u_in, par_ref, far_ref, out_ref, u_ref, wide_ref, state_ref):
    split_lanes(u_in, u_ref)
    seg_scan_params(par_ref, wide_ref)
    forward_ends(bounds_ref, u_ref, wide_ref, state_ref, span, tiles)
    for lt in range(tiles):
        lanes = slice(lt * LANES, (lt + 1) * LANES)
        start = jnp.zeros((STATES, LANES), jnp.float32)
        for seg in range(SEG):
            end = state_ref[lt, pl.ds(seg, STATES, stride=SEG), :]
            start = end + far_ref[:, lanes] * start * no_bound_in_seg(bounds_ref, span, seg)
        out_ref[:, lanes] = start


def forward_kernel(span, tiles, bounds_ref, u_in, par_ref, far_ref, first_ref, k_out, v_out, ckpt_ref,
                   u_ref, k_ref, v_ref, wide_ref, state_ref):
    split_lanes(u_in, u_ref)
    seg_scan_params(par_ref, wide_ref)
    forward_ends(bounds_ref, u_ref, wide_ref, state_ref, span, tiles)
    chain_forward(bounds_ref, state_ref, first_ref[...], far_ref, span, tiles)

    @pl.loop(0, span // GROUP)
    def _(group):
        def body(keep):
            for lt in range(tiles):
                u = steps_of(u_ref, lt, group, span)
                ks = [jnp.zeros((SEG, LANES), jnp.float32)] * GROUP
                vs = [jnp.zeros((SEG, LANES), jnp.float32)] * GROUP
                for n in range(STATES):
                    a, ck, cv = wide_ref[0, n, lt], wide_ref[1, n, lt], wide_ref[2, n, lt]
                    s = state_ref[lt, n * SEG : (n + 1) * SEG, :]
                    ckpt_ref[group, lt, n * SEG : (n + 1) * SEG, :] = s
                    for j in range(GROUP):
                        s = a * s
                        if keep is not None:
                            s = s * keep[j]
                        s = s + u[j]
                        ks[j] = ks[j] + ck * s
                        vs[j] = vs[j] + cv * s
                    state_ref[lt, n * SEG : (n + 1) * SEG, :] = s
                for j in range(GROUP):
                    rows = pl.ds(group * GROUP + j, SEG, stride=span)
                    k_ref[lt, rows, :] = ks[j]
                    v_ref[lt, rows, :] = vs[j]

        with_masks(bounds_ref, span, group, body)

    for lt in range(tiles):
        k_out[:, lt * LANES : (lt + 1) * LANES] = k_ref[lt].astype(k_out.dtype)
        v_out[:, lt * LANES : (lt + 1) * LANES] = v_ref[lt].astype(v_out.dtype)


def adjoint_ends(bounds_ref, gk_ref, gv_ref, wide_ref, adj_ref, span, tiles):
    adj_ref[...] = jnp.zeros_like(adj_ref)
    groups = span // GROUP

    @pl.loop(0, groups)
    def _(step):
        group = groups - 1 - step

        def body(keep):
            for lt in range(tiles):
                gk = steps_of(gk_ref, lt, group, span)
                gv = steps_of(gv_ref, lt, group, span)
                for n in range(STATES):
                    a, ck, cv = wide_ref[0, n, lt], wide_ref[1, n, lt], wide_ref[2, n, lt]
                    m = adj_ref[lt, n * SEG : (n + 1) * SEG, :]
                    for j in reversed(range(GROUP)):
                        m = a * (m + (ck * gk[j] + cv * gv[j]))
                        if keep is not None:
                            m = m * keep[j]
                    adj_ref[lt, n * SEG : (n + 1) * SEG, :] = m

        with_masks(bounds_ref, span, group, body)


def adjoint_ends_kernel(span, tiles, bounds_ref, gk_in, gv_in, par_ref, far_ref, out_ref, gk_ref, gv_ref, wide_ref, adj_ref):
    split_lanes(gk_in, gk_ref)
    split_lanes(gv_in, gv_ref)
    seg_scan_params(par_ref, wide_ref)
    adjoint_ends(bounds_ref, gk_ref, gv_ref, wide_ref, adj_ref, span, tiles)
    for lt in range(tiles):
        lanes = slice(lt * LANES, (lt + 1) * LANES)
        start = jnp.zeros((STATES, LANES), jnp.float32)
        for seg in reversed(range(SEG)):
            end = adj_ref[lt, pl.ds(seg, STATES, stride=SEG), :]
            start = end + far_ref[:, lanes] * start * no_bound_in_seg(bounds_ref, span, seg)
        out_ref[:, lanes] = start


def backward_kernel(span, tiles, bounds_ref, u_in, gk_in, gv_in, par_ref, far_ref, last_ref, ckpt_ref,
                    gu_out, sums_out, u_ref, gk_ref, gv_ref, gu_ref, wide_ref, adj_ref, acc_ref):
    split_lanes(u_in, u_ref)
    split_lanes(gk_in, gk_ref)
    split_lanes(gv_in, gv_ref)
    seg_scan_params(par_ref, wide_ref)
    adjoint_ends(bounds_ref, gk_ref, gv_ref, wide_ref, adj_ref, span, tiles)
    for _ in chain_backward(bounds_ref, adj_ref, last_ref[...], far_ref, span, tiles):
        pass
    acc_ref[...] = jnp.zeros_like(acc_ref)
    groups = span // GROUP

    @pl.loop(0, groups)
    def _(step):
        group = groups - 1 - step

        def body(keep):
            for lt in range(tiles):
                u = steps_of(u_ref, lt, group, span)
                gk = steps_of(gk_ref, lt, group, span)
                gv = steps_of(gv_ref, lt, group, span)
                gu = [jnp.zeros((SEG, LANES), jnp.float32)] * GROUP
                for n in range(STATES):
                    mine = slice(n * SEG, (n + 1) * SEG)
                    a, ck, cv = wide_ref[0, n, lt], wide_ref[1, n, lt], wide_ref[2, n, lt]
                    states = [ckpt_ref[group, lt, mine, :]]
                    for j in range(GROUP):
                        s = a * states[j]
                        if keep is not None:
                            s = s * keep[j]
                        states.append(s + u[j])
                    m = adj_ref[lt, mine, :]
                    sum_k, sum_v, sum_a = acc_ref[0, lt, mine, :], acc_ref[1, lt, mine, :], acc_ref[2, lt, mine, :]
                    for j in reversed(range(GROUP)):
                        lam = m + (ck * gk[j] + cv * gv[j])
                        gu[j] = gu[j] + lam
                        sum_k = sum_k + gk[j] * states[j + 1]
                        sum_v = sum_v + gv[j] * states[j + 1]
                        m = a * lam
                        if keep is not None:
                            m = m * keep[j]
                        sum_a = sum_a + m * states[j]
                    acc_ref[0, lt, mine, :] = sum_k
                    acc_ref[1, lt, mine, :] = sum_v
                    acc_ref[2, lt, mine, :] = sum_a
                    adj_ref[lt, mine, :] = m
                for j in range(GROUP):
                    gu_ref[lt, pl.ds(group * GROUP + j, SEG, stride=span), :] = gu[j]

        with_masks(bounds_ref, span, group, body)

    for lt in range(tiles):
        lanes = slice(lt * LANES, (lt + 1) * LANES)
        gu_out[:, lanes] = gu_ref[lt].astype(gu_out.dtype)
        for p in range(3):
            total = acc_ref[p, lt, pl.ds(0, STATES, stride=SEG), :]
            for seg in range(1, SEG):
                total = total + acc_ref[p, lt, pl.ds(seg, STATES, stride=SEG), :]
            sums_out[p, :, lanes] = total


LIMIT = pltpu.CompilerParams(vmem_limit_bytes=48 * 2**20)


def f32(*shape):
    return pltpu.VMEM(shape, jnp.float32)


def ssm_ends(bounds, u, par, far, name="ssm_ends"):
    rows, width = u.shape
    span, tiles = rows // SEG, width // LANES
    return pl.pallas_call(
        functools.partial(ends_kernel, span, tiles),
        out_shape=jax.ShapeDtypeStruct((STATES, width), jnp.float32),
        in_specs=[SMEM] + [VMEM] * 3, out_specs=VMEM,
        scratch_shapes=[f32(tiles, rows, LANES), f32(3, STATES, tiles, SEG, LANES), f32(tiles, STATES * SEG, LANES)],
        compiler_params=LIMIT, name=name)(bounds, u, par, far)


def ssm_forward(bounds, u, par, far, first, name="ssm_forward"):
    rows, width = u.shape
    span, tiles = rows // SEG, width // LANES
    return pl.pallas_call(
        functools.partial(forward_kernel, span, tiles),
        out_shape=(jax.ShapeDtypeStruct((rows, width), jnp.bfloat16), jax.ShapeDtypeStruct((rows, width), jnp.bfloat16),
                   jax.ShapeDtypeStruct((span // GROUP, tiles, STATES * SEG, LANES), jnp.float32)),
        in_specs=[SMEM] + [VMEM] * 4, out_specs=(VMEM,) * 3,
        scratch_shapes=[f32(tiles, rows, LANES)] * 3 + [f32(3, STATES, tiles, SEG, LANES), f32(tiles, STATES * SEG, LANES)],
        compiler_params=LIMIT, name=name)(bounds, u, par, far, first)


def ssm_adjoint_ends(bounds, gk, gv, par, far, name="ssm_adjoint_ends"):
    rows, width = gk.shape
    span, tiles = rows // SEG, width // LANES
    return pl.pallas_call(
        functools.partial(adjoint_ends_kernel, span, tiles),
        out_shape=jax.ShapeDtypeStruct((STATES, width), jnp.float32),
        in_specs=[SMEM] + [VMEM] * 4, out_specs=VMEM,
        scratch_shapes=[f32(tiles, rows, LANES)] * 2 + [f32(3, STATES, tiles, SEG, LANES), f32(tiles, STATES * SEG, LANES)],
        compiler_params=LIMIT, name=name)(bounds, gk, gv, par, far)


def ssm_backward(bounds, u, gk, gv, par, far, last, ckpt, name="ssm_backward"):
    rows, width = u.shape
    span, tiles = rows // SEG, width // LANES
    return pl.pallas_call(
        functools.partial(backward_kernel, span, tiles),
        out_shape=(jax.ShapeDtypeStruct((rows, width), jnp.bfloat16), jax.ShapeDtypeStruct((3, STATES, width), jnp.float32)),
        in_specs=[SMEM] + [VMEM] * 7, out_specs=(VMEM,) * 2,
        scratch_shapes=[f32(tiles, rows, LANES)] * 4 + [f32(3, STATES, tiles, SEG, LANES), f32(tiles, STATES * SEG, LANES), f32(3, tiles, STATES * SEG, LANES)],
        compiler_params=LIMIT, name=name)(bounds, u, gk, gv, par, far, last, ckpt)


QT = 256
NEG = -1e30
SCALE = HEAD ** (-0.5)


def tiles_of(rows, shift):
    out = []
    for r in range(0, rows, QT):
        first = max(0, r + shift - (BLOCK + CTX)) if shift == 0 else 0
        out.append((r, first, r + shift + QT))
    return out


def lowest_key(starts_ref, row0, shift):
    if shift:
        return jnp.full((1, QT), starts_ref[0], jnp.int32)
    rows = lax.broadcasted_iota(jnp.int32, (1, QT), 1) + row0
    start = jnp.zeros((1, QT), jnp.int32)
    for k in range(starts_ref.shape[0]):
        start = jnp.where(rows >= starts_ref[k], starts_ref[k], start)
    block = ((rows - start) // BLOCK) * BLOCK - CTX
    return start + jnp.maximum(block, 0)


def allowed_keys(starts_ref, q0, k0, k1, shift):
    low = lowest_key(starts_ref, q0, shift)
    high = lax.broadcasted_iota(jnp.int32, (1, QT), 1) + (q0 + shift)
    keys = lax.broadcasted_iota(jnp.int32, (k1 - k0, QT), 0) + k0
    return (keys >= low) & (keys <= high)


def dot_nt(a, b):
    return lax.dot_general(a, b, (((1,), (1,)), ((), ())), preferred_element_type=jnp.float32)


def dot_nn(a, b):
    return lax.dot_general(a, b, (((1,), (0,)), ((), ())), preferred_element_type=jnp.float32)


def attend_kernel(tiles, shift, starts_ref, q_ref, k_ref, v_ref, o_ref, lse_ref, vt_ref):
    vt_ref[...] = v_ref[...].T
    for q0, k0, k1 in tiles:
        scores = dot_nt(k_ref[k0:k1, :], q_ref[q0 : q0 + QT, :]) * SCALE
        scores = jnp.where(allowed_keys(starts_ref, q0, k0, k1, shift), scores, NEG)
        top = jnp.max(scores, axis=0, keepdims=True)
        exps = jnp.exp(scores - top)
        total = jnp.sum(exps, axis=0, keepdims=True)
        probs = (exps * (1.0 / total)).astype(jnp.bfloat16)
        mixed = dot_nn(vt_ref[:, k0:k1], probs)
        o_ref[q0 : q0 + QT, :] = mixed.T.astype(o_ref.dtype)
        lse_ref[0, 0, q0 : q0 + QT] = (top + jnp.log(total))[0]


def attend(starts, q, k, v, shift, name):
    rows, width = q.shape
    heads = width // HEAD
    keys = k.shape[0]
    lane = lambda h: (0, h)
    return pl.pallas_call(
        functools.partial(attend_kernel, tiles_of(rows, shift), shift),
        grid=(heads,),
        out_shape=(jax.ShapeDtypeStruct((rows, width), jnp.bfloat16), jax.ShapeDtypeStruct((heads, 1, rows), jnp.float32)),
        in_specs=[SMEM, pl.BlockSpec((rows, HEAD), lane), pl.BlockSpec((keys, HEAD), lane), pl.BlockSpec((keys, HEAD), lane)],
        out_specs=(pl.BlockSpec((rows, HEAD), lane), pl.BlockSpec((1, 1, rows), lambda h: (h, 0, 0))),
        scratch_shapes=[pltpu.VMEM((HEAD, keys), jnp.bfloat16)],
        compiler_params=pltpu.CompilerParams(vmem_limit_bytes=40 * 2**20),
        name=name)(starts, q, k, v)


def attend_back_kernel(tiles, shift, starts_ref, q_ref, k_ref, v_ref, g_ref, lse_ref, dq_ref, dk_ref, dv_ref, kt_ref):
    kt_ref[...] = k_ref[...].T
    dk_ref[...] = jnp.zeros_like(dk_ref)
    dv_ref[...] = jnp.zeros_like(dv_ref)
    for q0, k0, k1 in tiles:
        q = q_ref[q0 : q0 + QT, :]
        g = g_ref[q0 : q0 + QT, :]
        lse = lse_ref[0, :, q0 : q0 + QT]
        scores = dot_nt(k_ref[k0:k1, :], q) * SCALE
        probs = jnp.where(allowed_keys(starts_ref, q0, k0, k1, shift), jnp.exp(scores - lse), 0.0)
        grad_probs = dot_nt(v_ref[k0:k1, :], g)
        dv_ref[0, k0:k1, :] += dot_nn(probs.astype(jnp.bfloat16), g)
        delta = jnp.sum(probs * grad_probs, axis=0, keepdims=True)
        grad_scores = (probs * (grad_probs - delta)).astype(jnp.bfloat16)
        dk_ref[0, k0:k1, :] += dot_nn(grad_scores, q) * SCALE
        dq_ref[q0 : q0 + QT, :] = (dot_nn(kt_ref[:, k0:k1], grad_scores) * SCALE).T.astype(dq_ref.dtype)


def attend_back(starts, q, k, v, g, lse, shift, name):
    rows, width = q.shape
    heads = width // HEAD
    keys = k.shape[0]
    lane = lambda h: (0, h)
    rspec, kspec = pl.BlockSpec((rows, HEAD), lane), pl.BlockSpec((keys, HEAD), lane)
    gspec = pl.BlockSpec((1, keys, HEAD), lambda h: (h, 0, 0))
    return pl.pallas_call(
        functools.partial(attend_back_kernel, tiles_of(rows, shift), shift),
        grid=(heads,),
        out_shape=(jax.ShapeDtypeStruct((rows, width), jnp.bfloat16), jax.ShapeDtypeStruct((heads, keys, HEAD), jnp.float32), jax.ShapeDtypeStruct((heads, keys, HEAD), jnp.float32)),
        in_specs=[SMEM, rspec, kspec, kspec, rspec, pl.BlockSpec((1, 1, rows), lambda h: (h, 0, 0))],
        out_specs=(rspec, gspec, gspec),
        scratch_shapes=[pltpu.VMEM((HEAD, keys), jnp.bfloat16)],
        compiler_params=pltpu.CompilerParams(vmem_limit_bytes=40 * 2**20),
        name=name)(starts, q, k, v, g, lse)


ROWS = 256
SUB = 32
DEEP = 3
MESH = pl.DeviceIdType.MESH


def group_of_four():
    me = lax.axis_index("mp")
    mate = me + 1 - 2 * (me % 2)
    return me, mate, (me + 2) % 4, (mate + 2) % 4


def greet_group():
    _, mate, over, _ = group_of_four()
    dp = lax.axis_index("dp")
    barrier = pltpu.get_barrier_semaphore()
    for peer in (mate, over):
        pl.semaphore_signal(barrier, inc=1, device_id=(dp, peer), device_id_type=MESH)
    pl.semaphore_wait(barrier, 2)


class Mover:
    def __init__(self, send_sem, recv_sem):
        self.send_sem, self.recv_sem = send_sem, recv_sem
        self.dp = lax.axis_index("dp")

    def copy(self, src, dst, kind, c, peer):
        return pltpu.make_async_remote_copy(
            src_ref=src, dst_ref=dst, send_sem=self.send_sem.at[kind, c], recv_sem=self.recv_sem.at[kind, c],
            device_id=(self.dp, peer), device_id_type=MESH)


class Gather:
    def __init__(self, mover, base, full, rows):
        self.mover, self.base, self.full, self.rows = mover, base, full, rows
        self.me, self.mate, self.over, self.far = group_of_four()

    def at(self, owner, c):
        return self.full.at[owner, pl.ds(pl.multiple_of(c * self.rows, self.rows), self.rows)]

    def near(self, c):
        return self.mover.copy(self.at(self.me, c), self.at(self.me, c), self.base, c, self.mate)

    def across(self, c):
        return self.mover.copy(self.at(self.me, c), self.at(self.me, c), self.base + 1, c, self.over)

    def onward(self, c):
        return self.mover.copy(self.at(self.over, c), self.at(self.over, c), self.base + 2, c, self.mate)

    def start(self, c):
        self.across(c).start()
        self.near(c).start()

    def forward(self, c):
        self.across(c).wait_recv()
        self.onward(c).start()

    def finish(self, c):
        self.near(c).wait()
        self.across(c).wait_send()
        self.onward(c).wait()


class Scatter:
    def __init__(self, mover, base, part, near, across, joint):
        self.mover, self.base = mover, base
        self.part, self.near, self.across, self.joint = part, near, across, joint
        self.me, self.mate, self.over, self.far = group_of_four()

    def to_join(self, c):
        return self.mover.copy(self.part.at[c % DEEP, self.far], self.near.at[c, 1], self.base + 1, c, self.mate)

    def to_keep(self, c):
        return self.mover.copy(self.part.at[c % DEEP, self.mate], self.near.at[c, 0], self.base, c, self.mate)

    def joined(self, c):
        return self.mover.copy(self.joint.at[c % DEEP], self.across.at[c], self.base + 2, c, self.over)

    def start(self, c, parts):
        for d in range(4):
            self.part[c % DEEP, d] = parts(d).astype(jnp.bfloat16)
        self.to_join(c).start()
        self.to_keep(c).start()

    def combine(self, c):
        s = c % DEEP
        self.to_join(c).wait_recv()
        self.joint[s] = (self.part[s, self.over].astype(jnp.float32) + self.near[c, 1].astype(jnp.float32)).astype(jnp.bfloat16)
        self.joined(c).start()

    def finish(self, c):
        self.to_join(c).wait_send()
        self.to_keep(c).wait()
        self.joined(c).wait()
        return (self.part[c % DEEP, self.me].astype(jnp.float32) + self.near[c, 0].astype(jnp.float32)
                + self.across[c].astype(jnp.float32))


def mm(left, right, left_dim, right_dim):
    return lax.dot_general(left, right, (((left_dim,), (right_dim,)), ((), ())), preferred_element_type=jnp.float32)


def cut(d, width):
    return slice(d * width, (d + 1) * width)


def normed(full, c, sub, rows):
    first = pl.multiple_of(c * rows + sub * SUB, SUB)
    return jnp.concatenate([full[d, pl.ds(first, SUB), :].astype(jnp.float32) for d in range(4)], axis=1)


def middle_kernel(chunks, att_ref, tok_ref, cot_ref, w_out_ref, w_up_ref, w_down_ref, gain_ref,
                  result_ref, gm_ref, gatt_ref, grads_ref, ggain_ref,
                  gdown_ref, gup_ref, gout_ref, mid_full, gm_full, mid_ref, part, near, across, joint, n2_ref, act_ref, gpre_ref, pre_ref, gact_ref, mean_ref, inv_ref,
                  send_sem, recv_sem):
    width = att_ref.shape[1]
    rows = ROWS
    me = lax.axis_index("mp")
    mover = Mover(send_sem, recv_sem)
    sums = [Scatter(mover, 3 * r, part.at[r], near.at[r], across.at[r], joint.at[r]) for r in range(3)]
    gather_mid = Gather(mover, 9, mid_full, rows)
    gather_gm = Gather(mover, 12, gm_full, rows)
    greet_group()
    gdown_ref[...] = jnp.zeros_like(gdown_ref)
    gup_ref[...] = jnp.zeros_like(gup_ref)
    gout_ref[...] = jnp.zeros_like(gout_ref)
    ggain_ref[...] = jnp.zeros_like(ggain_ref)

    def span(c):
        return pl.ds(pl.multiple_of(c * rows, rows), rows)

    def project(c):
        att = att_ref[span(c), :]
        sums[0].start(c, lambda d: mm(att, w_out_ref[:, cut(d, width)], 1, 0))

    def add_middle(c):
        middle = tok_ref[span(c), :].astype(jnp.float32) + sums[0].finish(c)
        mid_ref[span(c), :] = middle
        mid_full[me, span(c), :] = middle.astype(jnp.bfloat16)
        gather_mid.start(c)

    def feed_forward(c):
        gather_mid.finish(c)

        @pl.loop(0, rows // SUB)
        def _(sub):
            mine = pl.ds(pl.multiple_of(sub * SUB, SUB), SUB)
            v = normed(mid_full, c, sub, rows)
            mean = jnp.mean(v, axis=1, keepdims=True)
            centred = v - mean
            inv = lax.rsqrt(jnp.mean(centred * centred, axis=1, keepdims=True) + EPS)
            mean_ref[mine, :] = mean
            inv_ref[mine, :] = inv
            n2_ref[mine, :] = (centred * inv * gain_ref[...]).astype(jnp.bfloat16)

        cot = cot_ref[span(c), :]
        pre_ref[...] = mm(n2_ref[...], w_up_ref[...], 1, 0)
        gact_ref[...] = mm(cot, w_down_ref[...], 1, 1)

        @pl.loop(0, rows // SUB)
        def _(sub):
            mine = pl.ds(pl.multiple_of(sub * SUB, SUB), SUB)
            v = pre_ref[mine, :]
            cdf = 0.5 * (1.0 + lax.erf(v * (0.5**0.5)))
            act_ref[mine, :] = (v * cdf).astype(jnp.bfloat16)
            slope = cdf + v * (jnp.exp(-0.5 * v * v) * 0.3989422804014327)
            gpre_ref[mine, :] = (slope * gact_ref[mine, :]).astype(jnp.bfloat16)

        sums[1].start(c, lambda d: mm(act_ref[...], w_down_ref[:, cut(d, width)], 1, 0))
        gact_ref[...] = mm(gpre_ref[...], w_up_ref[...], 1, 1)

        @pl.loop(0, rows // SUB)
        def _(sub):
            mine = pl.ds(pl.multiple_of(sub * SUB, SUB), SUB)
            xhat = (normed(mid_full, c, sub, rows) - mean_ref[mine, :]) * inv_ref[mine, :]
            up = gact_ref[mine, :]
            both = up * xhat
            ggain_ref[...] += jnp.sum(both.reshape(SUB // 8, 8, both.shape[1]), axis=0)
            scaled = up * gain_ref[...]
            plain = jnp.mean(scaled, axis=1, keepdims=True)
            cross = jnp.mean(scaled * xhat, axis=1, keepdims=True)
            gact_ref[mine, :] = inv_ref[mine, :] * (scaled - plain - xhat * cross)

        sums[2].start(c, lambda d: gact_ref[:, cut(d, width)])
        gdown_ref[...] += mm(act_ref[...], cot, 0, 0)
        gup_ref[...] += mm(n2_ref[...], gpre_ref[...], 0, 0)

    def finish_sums(c):
        own = pl.ds(pl.multiple_of(me * width, width), width)
        gm = cot_ref[span(c), own].astype(jnp.float32) + sums[2].finish(c)
        for lt in range(width // LANES):
            gm_ref[lt, span(c), :] = gm[:, cut(lt, LANES)]
        gm_full[me, span(c), :] = gm.astype(jnp.bfloat16)
        gather_gm.start(c)
        result_ref[span(c), :] = (mid_ref[span(c), :] + sums[1].finish(c)).astype(result_ref.dtype)

    def back_project(c):
        gather_gm.finish(c)
        att = att_ref[span(c), :]
        total = None
        for d in range(4):
            gm = gm_full[d, span(c), :]
            gout_ref[:, cut(d, width)] += mm(att, gm, 0, 0)
            term = mm(gm, w_out_ref[:, cut(d, width)], 1, 1)
            total = term if total is None else total + term
        gatt_ref[span(c), :] = total.astype(gatt_ref.dtype)

    def combine_late(c):
        sums[2].combine(c)
        sums[1].combine(c)

    stages = [(add_middle, 2), (finish_sums, 6), (sums[0].combine, 1), (combine_late, 5), (gather_mid.forward, 3),
              (gather_gm.forward, 7), (project, 0), (feed_forward, 4), (back_project, 8)]

    @pl.loop(0, chunks + 8)
    def _(i):
        for stage, lag in stages:
            @pl.when(jnp.logical_and(i >= lag, i < chunks + lag))
            def _(stage=stage, lag=lag):
                stage(i - lag)

    first = 0
    for total in (gdown_ref, gup_ref, gout_ref):
        grads_ref[first : first + total.shape[0], :] = total[...].astype(jnp.bfloat16)
        first += total.shape[0]


def middle_phase(att, tok, cot_full, w_out, w_up, w_down, gain):
    rows, width = att.shape
    full = cot_full.shape[1]
    hidden = w_up.shape[1]
    chunks = rows // ROWS
    bf = jnp.bfloat16

    def out(shape, dtype):
        return jax.ShapeDtypeStruct(shape, dtype)

    def buf(*shape, dtype=bf):
        return pltpu.VMEM(shape, dtype)

    return pl.pallas_call(
        functools.partial(middle_kernel, chunks),
        out_shape=(out((rows, width), bf), out((width // LANES, rows, LANES), jnp.float32), out((rows, width), bf),
                   out((hidden + full + width, full), bf), out((8, full), jnp.float32)),
        in_specs=[VMEM] * 7, out_specs=(VMEM,) * 5,
        scratch_shapes=[
            buf(hidden, full, dtype=jnp.float32), buf(full, hidden, dtype=jnp.float32), buf(width, full, dtype=jnp.float32),
            buf(4, rows, width), buf(4, rows, width), buf(rows, width, dtype=jnp.float32),
            buf(3, DEEP, 4, ROWS, width), buf(3, chunks, 2, ROWS, width), buf(3, chunks, ROWS, width), buf(3, DEEP, ROWS, width),
            buf(ROWS, full), buf(ROWS, hidden), buf(ROWS, hidden),
            buf(ROWS, hidden, dtype=jnp.float32), buf(ROWS, hidden, dtype=jnp.float32),
            buf(ROWS, 1, dtype=jnp.float32), buf(ROWS, 1, dtype=jnp.float32),
            pltpu.SemaphoreType.DMA((15, chunks)), pltpu.SemaphoreType.DMA((15, chunks)),
        ],
        compiler_params=pltpu.CompilerParams(collective_id=0, has_side_effects=True, vmem_limit_bytes=60 * 2**20),
        cost_estimate=pl.CostEstimate(flops=30 * 10**9, bytes_accessed=30 * 10**6, transcendentals=4 * 10**6),
        name="middle_phase")(att, tok, cot_full, w_out, w_up, w_down, gain)


POINTS = 14


def ring_place(index, count):
    side, along = index % 2, index // 2
    return (1 - side) * along + side * (count - 1 - along)


def ring_index(place, count):
    side = place // (count // 2)
    return (1 - side) * (2 * place) + side * (2 * (count - 1 - place) + 1)


class Ring:
    def __init__(self, count, half, data, total, held, send_sem, recv_sem):
        self.count, self.half = count, half
        self.data, self.total, self.held = data, total, held
        self.send_sem, self.recv_sem = send_sem, recv_sem
        self.place = ring_place(lax.axis_index("dp"), count)
        self.mp = lax.axis_index("mp")
        self.events = 2 * count - 1

    def rows(self, chunk, way):
        return pl.ds(pl.multiple_of((2 * chunk + way) * self.half, self.half), self.half)

    def chunk(self, way, back):
        return (self.place + (1 - 2 * (1 - way)) * back + 2 * self.count) % self.count

    def copy(self, src, dst, way, step):
        peer = ring_index((self.place + 1 - 2 * way + self.count) % self.count, self.count)
        return pltpu.make_async_remote_copy(
            src_ref=src, dst_ref=dst, send_sem=self.send_sem.at[way, step], recv_sem=self.recv_sem.at[way, step],
            device_id=(peer, self.mp), device_id_type=MESH)

    def add_copy(self, way, step):
        return self.copy(self.held.at[way, step], self.held.at[way, step], way, step)

    def give_copy(self, way, step, chunk):
        piece = self.total.at[self.rows(chunk, way)]
        return self.copy(piece, piece, way, self.count - 1 + step)

    def event(self, e):
        n = self.count

        @pl.when(e == 0)
        def _():
            for way in range(2):
                self.copy(self.data.at[self.rows(self.chunk(way, 0), way)], self.held.at[way, 0], way, 0).start()

        @pl.when(jnp.logical_and(e >= 1, e < n - 1))
        def _():
            for way in range(2):
                self.add_copy(way, e - 1).wait_recv()
                own = self.data[self.rows(self.chunk(way, e), way), :].astype(jnp.float32)
                self.held[way, e - 1] = (self.held[way, e - 1].astype(jnp.float32) + own).astype(jnp.bfloat16)
                self.copy(self.held.at[way, e - 1], self.held.at[way, e], way, e).start()

        @pl.when(e == n - 1)
        def _():
            for way in range(2):
                self.add_copy(way, n - 2).wait_recv()
                mine = self.chunk(way, n - 1)
                own = self.data[self.rows(mine, way), :].astype(jnp.float32)
                self.total[self.rows(mine, way), :] = (self.held[way, n - 2].astype(jnp.float32) + own).astype(jnp.bfloat16)
                self.give_copy(way, 0, mine).start()

        @pl.when(jnp.logical_and(e >= n, e < 2 * n - 2))
        def _():
            for way in range(2):
                self.give_copy(way, e - n, self.chunk(way, e - n)).wait_recv()
                self.give_copy(way, e - n + 1, self.chunk(way, e - n)).start()

        @pl.when(e == 2 * n - 2)
        def _():
            for way in range(2):
                self.give_copy(way, n - 2, self.chunk(way, n - 2)).wait_recv()

    def point(self, k):
        first, last = (k * (self.events - 1)) // POINTS, ((k + 1) * (self.events - 1)) // POINTS

        @pl.loop(first + 1, last + 1)
        def _(e):
            self.event(e)

    def settle(self):
        @pl.loop(0, 2 * (self.count - 1))
        def _(step):
            for way in range(2):
                self.copy(self.held.at[way, 0], self.held.at[way, 0], way, step).wait_send()


class Spread:
    def __init__(self, count, send_sem, recv_sem):
        self.count, self.send_sem, self.recv_sem = count, send_sem, recv_sem
        self.me, self.mp = lax.axis_index("dp"), lax.axis_index("mp")

    def copy(self, src, dst, o):
        return pltpu.make_async_remote_copy(
            src_ref=src, dst_ref=dst, send_sem=self.send_sem.at[o], recv_sem=self.recv_sem.at[o],
            device_id=((self.me + o) % self.count, self.mp), device_id_type=MESH)

    def start(self, src, dst):
        @pl.loop(1, self.count)
        def _(o):
            self.copy(src(o), dst(o), o).start()

    def wait(self, src, dst):
        @pl.loop(1, self.count)
        def _(o):
            self.copy(src(o), dst(o), o).wait()


def greet_all(count):
    me, mp = lax.axis_index("dp"), lax.axis_index("mp")
    barrier = pltpu.get_barrier_semaphore()

    @pl.loop(1, count)
    def _(o):
        pl.semaphore_signal(barrier, inc=1, device_id=((me + o) % count, mp), device_id_type=MESH)

    for peer in group_of_four()[1:]:
        pl.semaphore_signal(barrier, inc=1, device_id=(me, peer), device_id_type=MESH)
    pl.semaphore_wait(barrier, count + 2)


def masks_of(bounds_ref, span, group):
    if bounds_ref is None:
        return None
    return [keep_mask(bounds_ref, span, group * GROUP + j) for j in range(GROUP)]


def open_segment(bounds_ref, span, seg):
    if bounds_ref is None:
        return 1.0
    return no_bound_in_seg(bounds_ref, span, seg)


def adjoint_pass(bounds_ref, gk_ref, gv_ref, wide_ref, adj_ref, span, tiles, row0, beside):
    adj_ref[...] = jnp.zeros_like(adj_ref)
    groups = span // GROUP

    @pl.loop(0, groups)
    def _(step):
        group = groups - 1 - step
        keep = masks_of(bounds_ref, span, group)
        for lt in range(tiles):
            gk = [gk_ref[lt, pl.ds(row0 + group * GROUP + j, SEG, stride=span), :] for j in range(GROUP)]
            gv = [gv_ref[lt, pl.ds(row0 + group * GROUP + j, SEG, stride=span), :] for j in range(GROUP)]
            for n in range(STATES):
                mine = slice(n * SEG, (n + 1) * SEG)
                a, ck, cv = wide_ref[0, n, lt], wide_ref[1, n, lt], wide_ref[2, n, lt]
                m = adj_ref[lt, mine, :]
                for j in reversed(range(GROUP)):
                    m = a * (m + (ck * gk[j] + cv * gv[j]))
                    if keep is not None:
                        m = m * keep[j]
                adj_ref[lt, mine, :] = m
        beside(step)


def adjoint_chain(bounds_ref, adj_ref, last, far_ref, span, tiles, write):
    ends = []
    for lt in range(tiles):
        lanes = slice(lt * LANES, (lt + 1) * LANES)
        start, far = last[:, lanes], far_ref[:, lanes]
        for seg in reversed(range(SEG)):
            rows = pl.ds(seg, STATES, stride=SEG)
            end = adj_ref[lt, rows, :]
            if write:
                adj_ref[lt, rows, :] = start
            start = end + far * start * open_segment(bounds_ref, span, seg)
        ends.append(start)
    return jnp.concatenate(ends, axis=1)


def adjoint_full(bounds_ref, u_ref, gk_ref, gv_ref, ckpt_ref, wide_ref, adj_ref, acc_ref, span, tiles, row0, group0, beside):
    groups = span // GROUP

    @pl.loop(0, groups)
    def _(step):
        group = groups - 1 - step
        keep = masks_of(bounds_ref, span, group)
        for lt in range(tiles):
            at = [pl.ds(row0 + group * GROUP + j, SEG, stride=span) for j in range(GROUP)]
            u = [u_ref[lt, r, :] for r in at]
            gk = [gk_ref[lt, r, :] for r in at]
            gv = [gv_ref[lt, r, :] for r in at]
            gu = [jnp.zeros((SEG, LANES), jnp.float32)] * GROUP
            for n in range(STATES):
                mine = slice(n * SEG, (n + 1) * SEG)
                a, ck, cv = wide_ref[0, n, lt], wide_ref[1, n, lt], wide_ref[2, n, lt]
                states = [ckpt_ref[group0 + group, lt, mine, :]]
                for j in range(GROUP):
                    s = a * states[j]
                    if keep is not None:
                        s = s * keep[j]
                    states.append(s + u[j])
                m = adj_ref[lt, mine, :]
                sum_k, sum_v, sum_a = acc_ref[0, lt, mine, :], acc_ref[1, lt, mine, :], acc_ref[2, lt, mine, :]
                for j in reversed(range(GROUP)):
                    lam = m + (ck * gk[j] + cv * gv[j])
                    gu[j] = gu[j] + lam
                    sum_k = sum_k + gk[j] * states[j + 1]
                    sum_v = sum_v + gv[j] * states[j + 1]
                    m = a * lam
                    if keep is not None:
                        m = m * keep[j]
                    sum_a = sum_a + m * states[j]
                acc_ref[0, lt, mine, :] = sum_k
                acc_ref[1, lt, mine, :] = sum_v
                acc_ref[2, lt, mine, :] = sum_a
                adj_ref[lt, mine, :] = m
            for j in range(GROUP):
                u_ref[lt, at[j], :] = gu[j]
        beside(step)


def tail_kernel(count, half, block, bounds_ref, grads_hbm, n1_hbm, u_hbm, gk_hbm, gv_hbm, ckpt_hbm, gm_hbm,
                gq_ref, inv_ref, w_in_ref, w_query_ref, par_ref, far_ref, rate_ref, gain_ref, gain_two_ref,
                grad_tokens_ref, total_ref, win_ref, sums_ref, gains_ref,
                grads_ref, n1_ref, u_ref, gk_ref, gv_ref, ckpt_ref, wide_ref, adj_ref, adj_long, acc_ref,
                gssm_ref, up_ref, ggain_ref, held, win_data, win_held, piece_ref, piece_held, small_ref, small_held, gain_held,
                part, near, across, joint, load_sem, ring_send, ring_recv, mp_send, mp_recv, dp_send, dp_recv):
    rows, width = gq_ref.shape
    tiles = width // LANES
    full = n1_ref.shape[1]
    me = lax.axis_index("dp")
    mp = lax.axis_index("mp")
    chunks = rows // ROWS
    long_span, short_span = LONG_DEV // SEG, (rows - LONG_DEV) // SEG
    long_groups, short_groups = long_span // GROUP, short_span // GROUP
    known = grads_hbm.shape[0]
    loads = [pltpu.make_async_copy(src, dst, load_sem.at[i]) for i, (src, dst) in enumerate(
        [(gk_hbm, gk_ref), (gv_hbm, gv_ref), (n1_hbm, n1_ref), (grads_hbm, grads_ref.at[pl.ds(0, known)]),
         (u_hbm, u_ref), (ckpt_hbm, ckpt_ref), (gm_hbm, gk_ref)])]
    for load in loads[:6]:
        load.start()
    seg_scan_params(par_ref, wide_ref)
    acc_ref[...] = jnp.zeros_like(acc_ref)
    ggain_ref[...] = jnp.zeros_like(ggain_ref)
    ring = Ring(count, half, grads_ref, total_ref, held, ring_send, ring_recv)
    mover = Mover(mp_send, mp_recv)
    token_sum = Scatter(mover, 0, part, near, across, joint)
    first_spread = Spread(count, dp_send.at[0], dp_recv.at[0])
    scatter_spread = Spread(count, dp_send.at[1], dp_recv.at[1])
    gather_spread = Spread(count, dp_send.at[2], dp_recv.at[2])
    small_spread = Spread(count, dp_send.at[3], dp_recv.at[3])
    greet_all(count)

    def nothing(step):
        del step

    loads[0].wait()
    loads[1].wait()
    adjoint_pass(None, gk_ref, gv_ref, wide_ref, adj_long, long_span, tiles, 0, nothing)
    zero = jnp.zeros((STATES, width), jnp.float32)
    piece_ref[...] = adjoint_chain(None, adj_long, zero, far_ref.at[0], long_span, tiles, False)
    first_spread.start(lambda o: piece_ref, lambda o: piece_held.at[me])

    loads[2].wait()
    loads[3].wait()
    for d in range(full // width):
        grads_ref[known : known + width, cut(d, width)] = mm(gq_ref[...], n1_ref[:, cut(d, width)], 0, 0).astype(jnp.bfloat16)
    if grads_ref.shape[0] > known + width:
        grads_ref[known + width :, :] = jnp.zeros((grads_ref.shape[0] - known - width, full), jnp.bfloat16)
    ring.event(0)

    loads[4].wait()
    loads[5].wait()

    def beside_first(step):
        @pl.when(step == short_groups - 1)
        def _():
            ring.point(0)

    adjoint_pass(bounds_ref, gk_ref, gv_ref, wide_ref, adj_ref, short_span, tiles, LONG_DEV, beside_first)
    adjoint_chain(bounds_ref, adj_ref, zero, far_ref.at[1], short_span, tiles, True)

    def beside_second(step):
        @pl.when(step % 6 == 5)
        def _():
            ring.point(1 + step // 6)

    adjoint_full(bounds_ref, u_ref, gk_ref, gv_ref, ckpt_ref, wide_ref, adj_ref, acc_ref,
                 short_span, tiles, LONG_DEV, long_groups, beside_second)

    first_spread.wait(lambda o: piece_ref, lambda o: piece_held.at[me])

    def fold(d, total):
        gap = d - me - 1
        weight = jnp.exp(rate_ref[...] * (-LONG_DEV * jnp.maximum(gap, 0)).astype(jnp.float32))
        return total + jnp.where(gap >= 0, weight * piece_held[d], 0.0)

    piece_held[me] = zero
    last = lax.fori_loop(0, count, fold, zero)
    adjoint_chain(None, adj_long, last, far_ref.at[0], long_span, tiles, True)
    adjoint_full(None, u_ref, gk_ref, gv_ref, ckpt_ref, wide_ref, adj_long, acc_ref,
                 long_span, tiles, 0, 0, nothing)
    loads[6].start()
    ring.point(5)

    for lt in range(tiles):
        gssm_ref[:, lt * LANES : (lt + 1) * LANES] = u_ref[lt].astype(jnp.bfloat16)
        for p in range(3):
            total = acc_ref[p, lt, pl.ds(0, STATES, stride=SEG), :]
            for seg in range(1, SEG):
                total = total + acc_ref[p, lt, pl.ds(seg, STATES, stride=SEG), :]
            small_ref[p * STATES : (p + 1) * STATES, lt * LANES : (lt + 1) * LANES] = total

    for d in range(full // width):
        win_data[:width, cut(d, width)] = mm(gssm_ref[...], n1_ref[:, cut(d, width)], 0, 0).astype(jnp.bfloat16)
    if win_data.shape[0] > width:
        win_data[width:, :] = jnp.zeros((win_data.shape[0] - width, full), jnp.bfloat16)

    def win_rows(device):
        return pl.ds(pl.multiple_of(device * block, block), block)

    scatter_spread.start(lambda o: win_data.at[win_rows((me + o) % count)], lambda o: win_held.at[o])
    loads[6].wait()

    def span_of(c):
        return pl.ds(pl.multiple_of(c * ROWS, ROWS), ROWS)

    def project(c):
        up_ref[...] = mm(gssm_ref[span_of(c), :], w_in_ref[...], 1, 1) + mm(gq_ref[span_of(c), :], w_query_ref[...], 1, 1)

        @pl.loop(0, ROWS // SUB)
        def _(sub):
            mine = pl.ds(pl.multiple_of(sub * SUB, SUB), SUB)
            here = pl.ds(pl.multiple_of(c * ROWS + sub * SUB, SUB), SUB)
            xhat = n1_ref[here, :].astype(jnp.float32) * (1.0 / gain_ref[...])
            up = up_ref[mine, :]
            both = up * xhat
            ggain_ref[...] += jnp.sum(both.reshape(SUB // 8, 8, full), axis=0)
            scaled = up * gain_ref[...]
            plain = jnp.mean(scaled, axis=1, keepdims=True)
            cross = jnp.mean(scaled * xhat, axis=1, keepdims=True)
            up_ref[mine, :] = inv_ref[here, :] * (scaled - plain - xhat * cross)

        token_sum.start(c, lambda d: up_ref[:, cut(d, width)])

    def finish(c):
        gm = jnp.concatenate([gk_ref[lt, span_of(c), :] for lt in range(tiles)], axis=1)
        grad_tokens_ref[span_of(c), :] = (gm + token_sum.finish(c)).astype(grad_tokens_ref.dtype)

    stages = [(finish, 2), (token_sum.combine, 1), (project, 0)]

    @pl.loop(0, chunks + 2)
    def _(i):
        for stage, lag in stages:
            @pl.when(jnp.logical_and(i >= lag, i < chunks + lag))
            def _(stage=stage, lag=lag):
                stage(i - lag)

        @pl.when(i % 2 == 1)
        def _():
            ring.point(6 + i // 2)

    ggain = jnp.sum(ggain_ref[...], axis=0, keepdims=True)
    gtwo = jnp.sum(gain_two_ref[...], axis=0, keepdims=True)
    for d in range(full // width):
        small_ref[3 * STATES + d : 3 * STATES + d + 1, :] = ggain[:, cut(d, width)]
        small_ref[3 * STATES + 4 + d : 3 * STATES + 5 + d, :] = gtwo[:, cut(d, width)]
    small_spread.start(lambda o: small_ref, lambda o: small_held.at[me])
    small_held[me] = small_ref[...]

    scatter_spread.wait(lambda o: win_data.at[win_rows((me + o) % count)], lambda o: win_held.at[o])
    win_held[0] = win_data[win_rows(me), :]
    total = win_held[0].astype(jnp.float32)
    total = lax.fori_loop(1, count, lambda o, t: t + win_held[o].astype(jnp.float32), total)
    win_ref[win_rows(me), :] = total.astype(jnp.bfloat16)
    gather_spread.start(lambda o: win_ref.at[win_rows(me)], lambda o: win_ref.at[win_rows(me)])
    ring.point(11)
    small_spread.wait(lambda o: small_ref, lambda o: small_held.at[me])
    small = lax.fori_loop(1, count, lambda d, t: t + small_held[d], small_held[0])
    sums_ref[...] = small[: 3 * STATES]
    gain_held[mp] = small[3 * STATES :]
    group = group_of_four()
    sends = [mover.copy(gain_held.at[mp], gain_held.at[mp], 3, i, group[1 + i]) for i in range(3)]
    for send in sends:
        send.start()
    ring.point(12)
    for send in sends:
        send.wait()
    gains_ref[...] = ((gain_held[0] + gain_held[1]) + gain_held[2]) + gain_held[3]
    gather_spread.wait(lambda o: win_ref.at[win_rows(me)], lambda o: win_ref.at[win_rows(me)])
    ring.point(13)
    ring.settle()


def round_up(value, unit):
    return -(-value // unit) * unit


def tail_phase(bounds, grads, n1, u, gk, gv, ckpt, gm, gq, inv, w_in_t, w_query_t, par, far, rate, gain, gain_two_parts, count):
    rows, width = gq.shape
    tiles = width // LANES
    full = n1.shape[1]
    bf = jnp.bfloat16
    used = grads.shape[0] + width
    half = round_up(-(-used // (2 * count)), 16)
    block = round_up(-(-width // count), 16)

    def out(shape, dtype):
        return jax.ShapeDtypeStruct(shape, dtype)

    def buf(*shape, dtype=bf):
        return pltpu.VMEM(shape, dtype)

    def wide(*shape):
        return pltpu.VMEM(shape, jnp.float32)

    ANY = pl.BlockSpec(memory_space=pl.ANY)
    chunks = rows // ROWS
    dma = pltpu.SemaphoreType.DMA
    small_rows = 3 * STATES + 8
    return pl.pallas_call(
        functools.partial(tail_kernel, count, half, block),
        out_shape=(out((rows, width), bf), out((2 * count * half, full), bf), out((count * block, full), bf),
                   out((3 * STATES, width), jnp.float32), out((8, width), jnp.float32)),
        in_specs=[SMEM] + [ANY] * 7 + [VMEM] * 9, out_specs=(VMEM,) * 5,
        scratch_shapes=[
            buf(2 * count * half, full), buf(rows, full),
            wide(tiles, rows, LANES), wide(tiles, rows, LANES), wide(tiles, rows, LANES),
            wide(*ckpt.shape), wide(3, STATES, tiles, SEG, LANES), wide(tiles, STATES * SEG, LANES), wide(tiles, STATES * SEG, LANES),
            wide(3, tiles, STATES * SEG, LANES),
            buf(rows, width), wide(ROWS, full), wide(8, full), buf(2, count - 1, half, full),
            buf(count * block, full), buf(count, block, full), wide(STATES, width), wide(count, STATES, width),
            wide(small_rows, width), wide(count, small_rows, width), wide(4, 8, width),
            buf(DEEP, 4, ROWS, width), buf(chunks, 2, ROWS, width), buf(chunks, ROWS, width), buf(DEEP, ROWS, width),
            dma((7,)), dma((2, 2 * (count - 1))), dma((2, 2 * (count - 1))),
            dma((4, chunks)), dma((4, chunks)), dma((4, count)), dma((4, count)),
        ],
        compiler_params=pltpu.CompilerParams(collective_id=1, has_side_effects=True, vmem_limit_bytes=62 * 2**20),
        cost_estimate=pl.CostEstimate(flops=6 * 10**9, bytes_accessed=40 * 10**6, transcendentals=0),
        name="tail_phase")(bounds, grads, n1, u, gk, gv, ckpt, gm, gq, inv, w_in_t, w_query_t, par, far, rate, gain, gain_two_parts)


def gather_features(values_in):
    return lax.all_gather(values_in, "mp", axis=1, tiled=True)


def reduce_features(values_in):
    return lax.psum_scatter(
        values_in.astype(jnp.bfloat16), "mp", scatter_dimension=1, tiled=True
    ).astype(jnp.float32)


def from_behind(value, axis, steps):
    count = lax.axis_size(axis)
    initial, last = (max(0, -steps), min(count, count - steps))
    return lax.ppermute(value, axis, [(source, source + steps) for source in range(initial, last)])


def norm_forward(values_in, gain_vec):
    row_mean = jnp.mean(values_in, axis=1, keepdims=True)
    centred = values_in - row_mean
    row_var = jnp.mean(centred * centred, axis=1, keepdims=True)
    inverse = lax.rsqrt(row_var + EPS)
    normed = centred * inverse
    return (normed, inverse, normed * gain_vec)


def norm_backward(upstream, normed, inverse, gain_vec):
    gain_grad = jnp.sum(upstream * normed, axis=0)
    scaled = upstream * gain_vec
    plain_mean = jnp.mean(scaled, axis=1, keepdims=True)
    cross_mean = jnp.mean(scaled * normed, axis=1, keepdims=True)
    return (inverse * (scaled - plain_mean - normed * cross_mean), gain_grad)


def gelu_exact(values_in):
    return jax.nn.gelu(values_in, approximate=False)


def fold_pieces(pieces, decay_rate, gap_count):
    live_rows = gap_count >= 0
    weights = jnp.exp(
        -decay_rate[None]
        * (LONG_DEV * jnp.maximum(gap_count, 0)).astype(jnp.float32)[:, None, None]
    )
    return jnp.sum(jnp.where(live_rows[:, None, None], weights * pieces, 0.0), axis=0)


def dot(left, right, dims):
    return lax.dot_general(left, right, ((dims[0], dims[1]), ((), ())), preferred_element_type=jnp.float32)


def on_device(
    tokens,
    gain_one,
    gain_two,
    w_in,
    w_query,
    w_out,
    w_up,
    w_down,
    decay_rate,
    b_in,
    c_key,
    c_val,
    short_lengths,
    cotangent,
):
    low = jnp.bfloat16
    device = lax.axis_index("dp")
    local_width = w_in.shape[1]
    lengths = short_lengths[0]
    ends = jnp.cumsum(lengths).astype(jnp.int32)
    short_starts = jnp.concatenate([jnp.zeros((1,), jnp.int32), ends[:-1]])
    no_bound = jnp.full((1,), -1, jnp.int32)
    long_low = jnp.where(device > 0, 0, CTX).astype(jnp.int32).reshape(1)
    rate_t = decay_rate.T
    root = jnp.sqrt(-jnp.expm1(-2.0 * rate_t))
    drive = root * b_in.T
    ck_t, cv_t = c_key.T, c_val.T
    decay = jnp.exp(-rate_t)
    par = jnp.stack([decay, drive * ck_t, drive * cv_t])
    short_rows = tokens.shape[0] - LONG_DEV
    far_long = jnp.exp(-rate_t * (LONG_DEV // SEG))
    far_short = jnp.exp(-rate_t * (short_rows // SEG))

    tokens_full = gather_features(tokens).astype(jnp.float32)
    cotangent_full = gather_features(cotangent)
    normed_one, inverse_one, hidden_one = norm_forward(tokens_full, gain_one)
    normed_one_low = hidden_one.astype(low)
    ssm_input = jnp.dot(normed_one_low, w_in, preferred_element_type=jnp.float32)
    queries = jnp.dot(normed_one_low, w_query, preferred_element_type=jnp.float32).astype(low)
    u_long, u_short = ssm_input[:LONG_DEV], ssm_input[LONG_DEV:]
    local_end = ssm_ends(no_bound, u_long, par, far_long)
    pieces = lax.all_gather(local_end[None], "dp", axis=0, tiled=True)
    others = jnp.arange(pieces.shape[0], dtype=jnp.int32)
    state_in = fold_pieces(pieces, rate_t, device - 1 - others)
    zero_state = jnp.zeros_like(state_in)
    k_short, v_short, ckpt_short = ssm_forward(short_starts, u_short, par, far_short, zero_state, "ssm_short")
    k_long, v_long, ckpt_long = ssm_forward(no_bound, u_long, par, far_long, state_in, "ssm_long")
    ctx_k, ctx_v = from_behind((k_long[LONG_DEV - CTX :], v_long[LONG_DEV - CTX :]), "dp", 1)
    k_long = jnp.concatenate([ctx_k, k_long])
    v_long = jnp.concatenate([ctx_v, v_long])
    q_long, q_short = queries[:LONG_DEV], queries[LONG_DEV:]
    att_short, lse_short = attend(short_starts, q_short, k_short, v_short, 0, "attend_short")
    att_long, lse_long = attend(long_low, q_long, k_long, v_long, CTX, "attend_long")
    attended = jnp.concatenate([att_long, att_short])
    result, grad_middle, grad_attended, grads, gain_two_parts = middle_phase(
        attended, tokens, cotangent_full, w_out, w_up, w_down, gain_two[None]
    )

    gq_long, gk_long, gv_long = attend_back(
        long_low, q_long, k_long, v_long, grad_attended[:LONG_DEV], lse_long, CTX, "attend_back_long"
    )
    back = from_behind(jnp.stack([gk_long[:, :CTX], gv_long[:, :CTX]]).astype(low), "dp", -1).astype(jnp.float32)
    gq_short, gk_short, gv_short = attend_back(
        short_starts, q_short, k_short, v_short, grad_attended[LONG_DEV:], lse_short, 0, "attend_back_short"
    )
    gk_long = gk_long[:, CTX:].at[:, LONG_DEV - CTX :].add(back[0])
    gv_long = gv_long[:, CTX:].at[:, LONG_DEV - CTX :].add(back[1])
    gk = jnp.concatenate([gk_long, gk_short], axis=1)
    gv = jnp.concatenate([gv_long, gv_short], axis=1)
    u_tiles = ssm_input.reshape(-1, local_width // LANES, LANES).transpose(1, 0, 2)
    ckpt = jnp.concatenate([ckpt_long, ckpt_short])
    grad_queries = jnp.concatenate([gq_long, gq_short])
    grad_tokens, total, win_t, sums, gains = tail_phase(
        short_starts, grads, normed_one_low, u_tiles, gk, gv, ckpt, grad_middle, grad_queries, inverse_one,
        w_in, w_query, par, jnp.stack([far_long, far_short]), rate_t, gain_one[None], gain_two_parts, lax.axis_size("dp"),
    )
    hidden, full = w_down.shape
    rows_of = [total[:hidden], total[hidden : hidden + full], total[hidden + full : hidden + full + local_width],
               total[hidden + full + local_width : hidden + full + 2 * local_width].T, win_t[:local_width].T]
    grad_w_down, grad_w_up, grad_w_out, grad_w_query, grad_w_in = (r.astype(jnp.float32) for r in rows_of)
    grad_gain_one, grad_gain_two = gains.reshape(2, full)
    sums = sums.reshape(3, STATES, local_width)

    grad_ck = (drive * sums[0]).T
    grad_cv = (drive * sums[1]).T
    grad_drive = ck_t * sums[0] + cv_t * sums[1]
    grad_b = (root * grad_drive).T
    grad_rate = (grad_drive * b_in.T * jnp.exp(-2.0 * rate_t) / root - sums[2]).T
    return (
        result,
        grad_tokens,
        grad_gain_one,
        grad_gain_two,
        grad_w_in,
        grad_w_query,
        grad_w_out,
        grad_w_up,
        grad_w_down,
        grad_rate,
        grad_b,
        grad_ck,
        grad_cv,
    )


def solution(mesh):
    placed = (
        P("dp", "mp"),
        P(),
        P(),
        P(None, "mp"),
        P(None, "mp"),
        P("mp", None),
        P(None, "mp"),
        P("mp", None),
        P("mp", None),
        P("mp", None),
        P("mp", None),
        P("mp", None),
        P("dp", None),
        P("dp", "mp"),
    )
    return jax.shard_map(
        on_device,
        mesh=mesh,
        in_specs=placed,
        out_specs=(
            P("dp", "mp"),
            P("dp", "mp"),
            P(),
            P(),
            P(None, "mp"),
            P(None, "mp"),
            P("mp", None),
            P(None, "mp"),
            P("mp", None),
            P("mp", None),
            P("mp", None),
            P("mp", None),
            P("mp", None),
        ),
        check_vma=False,
    )
```

```python
import functools

import jax
import jax.numpy as jnp
from jax import lax
from jax.experimental import pallas as pl
from jax.experimental.pallas import tpu as pltpu
from jax.sharding import PartitionSpec as P

HEAD = 128
BLOCK = 512
CTX = 128
LONG_DEV = 512
EPS = 1e-05
SEG = 8
GROUP = 8
STATES = 16
LANES = 128
VMEM = pl.BlockSpec(memory_space=pltpu.VMEM)
SMEM = pl.BlockSpec(memory_space=pltpu.SMEM)


def seg_scan_params(par_ref, wide_ref):
    for p in range(par_ref.shape[0]):
        for n in range(STATES):
            for lt in range(par_ref.shape[2] // LANES):
                row = par_ref[p, n : n + 1, lt * LANES : (lt + 1) * LANES]
                wide_ref[p, n, lt] = jnp.broadcast_to(row, (SEG, LANES))


def keep_mask(bounds_ref, span, step):
    rows = lax.broadcasted_iota(jnp.int32, (SEG, LANES), 0) * span + step
    keep = jnp.ones((SEG, LANES), jnp.float32)
    for k in range(bounds_ref.shape[0]):
        keep = jnp.where(rows == bounds_ref[k], 0.0, keep)
    return keep


def has_bound(bounds_ref, span, group):
    found = False
    for k in range(bounds_ref.shape[0]):
        b = bounds_ref[k]
        inside = lax.rem(b, span) // GROUP == group
        found = jnp.logical_or(found, jnp.logical_and(b >= 0, inside))
    return found


def steps_of(ref, lt, group, span):
    return [ref[lt, pl.ds(group * GROUP + j, SEG, stride=span), :] for j in range(GROUP)]


def split_lanes(src_ref, dst_ref):
    for lt in range(dst_ref.shape[0]):
        dst_ref[lt] = src_ref[:, lt * LANES : (lt + 1) * LANES].astype(jnp.float32)


def with_masks(bounds_ref, span, group, body):
    flag = has_bound(bounds_ref, span, group)

    @pl.when(flag)
    def _():
        body([keep_mask(bounds_ref, span, group * GROUP + j) for j in range(GROUP)])

    @pl.when(jnp.logical_not(flag))
    def _():
        body(None)


def forward_ends(bounds_ref, u_ref, wide_ref, state_ref, span, tiles):
    state_ref[...] = jnp.zeros_like(state_ref)

    @pl.loop(0, span // GROUP)
    def _(group):
        def body(keep):
            for lt in range(tiles):
                u = steps_of(u_ref, lt, group, span)
                for n in range(STATES):
                    a = wide_ref[0, n, lt]
                    s = state_ref[lt, n * SEG : (n + 1) * SEG, :]
                    for j in range(GROUP):
                        s = a * s
                        if keep is not None:
                            s = s * keep[j]
                        s = s + u[j]
                    state_ref[lt, n * SEG : (n + 1) * SEG, :] = s

        with_masks(bounds_ref, span, group, body)


def no_bound_in_seg(bounds_ref, span, seg):
    ok = jnp.float32(1.0)
    for k in range(bounds_ref.shape[0]):
        b = bounds_ref[k]
        inside = jnp.logical_and(b >= seg * span, b < (seg + 1) * span)
        ok = jnp.where(inside, jnp.float32(0.0), ok)
    return ok


def chain_forward(bounds_ref, state_ref, first, far_ref, span, tiles):
    for lt in range(tiles):
        lanes = slice(lt * LANES, (lt + 1) * LANES)
        start = first[:, lanes]
        far = far_ref[:, lanes]
        for seg in range(SEG):
            rows = pl.ds(seg, STATES, stride=SEG)
            end = state_ref[lt, rows, :]
            state_ref[lt, rows, :] = start
            start = end + far * start * no_bound_in_seg(bounds_ref, span, seg)


def chain_backward(bounds_ref, adj_ref, last, far_ref, span, tiles):
    for lt in range(tiles):
        lanes = slice(lt * LANES, (lt + 1) * LANES)
        start = last[:, lanes]
        far = far_ref[:, lanes]
        for seg in reversed(range(SEG)):
            rows = pl.ds(seg, STATES, stride=SEG)
            end = adj_ref[lt, rows, :]
            adj_ref[lt, rows, :] = start
            start = end + far * start * no_bound_in_seg(bounds_ref, span, seg)
        yield start


def ends_kernel(span, tiles, bounds_ref, u_in, par_ref, far_ref, out_ref, u_ref, wide_ref, state_ref):
    split_lanes(u_in, u_ref)
    seg_scan_params(par_ref, wide_ref)
    forward_ends(bounds_ref, u_ref, wide_ref, state_ref, span, tiles)
    for lt in range(tiles):
        lanes = slice(lt * LANES, (lt + 1) * LANES)
        start = jnp.zeros((STATES, LANES), jnp.float32)
        for seg in range(SEG):
            end = state_ref[lt, pl.ds(seg, STATES, stride=SEG), :]
            start = end + far_ref[:, lanes] * start * no_bound_in_seg(bounds_ref, span, seg)
        out_ref[:, lanes] = start


def forward_kernel(span, tiles, bounds_ref, u_in, par_ref, far_ref, first_ref, k_out, v_out, ckpt_ref,
                   u_ref, k_ref, v_ref, wide_ref, state_ref):
    split_lanes(u_in, u_ref)
    seg_scan_params(par_ref, wide_ref)
    forward_ends(bounds_ref, u_ref, wide_ref, state_ref, span, tiles)
    chain_forward(bounds_ref, state_ref, first_ref[...], far_ref, span, tiles)

    @pl.loop(0, span // GROUP)
    def _(group):
        def body(keep):
            for lt in range(tiles):
                u = steps_of(u_ref, lt, group, span)
                ks = [jnp.zeros((SEG, LANES), jnp.float32)] * GROUP
                vs = [jnp.zeros((SEG, LANES), jnp.float32)] * GROUP
                for n in range(STATES):
                    a, ck, cv = wide_ref[0, n, lt], wide_ref[1, n, lt], wide_ref[2, n, lt]
                    s = state_ref[lt, n * SEG : (n + 1) * SEG, :]
                    ckpt_ref[group, lt, n * SEG : (n + 1) * SEG, :] = s
                    for j in range(GROUP):
                        s = a * s
                        if keep is not None:
                            s = s * keep[j]
                        s = s + u[j]
                        ks[j] = ks[j] + ck * s
                        vs[j] = vs[j] + cv * s
                    state_ref[lt, n * SEG : (n + 1) * SEG, :] = s
                for j in range(GROUP):
                    rows = pl.ds(group * GROUP + j, SEG, stride=span)
                    k_ref[lt, rows, :] = ks[j]
                    v_ref[lt, rows, :] = vs[j]

        with_masks(bounds_ref, span, group, body)

    for lt in range(tiles):
        k_out[:, lt * LANES : (lt + 1) * LANES] = k_ref[lt].astype(k_out.dtype)
        v_out[:, lt * LANES : (lt + 1) * LANES] = v_ref[lt].astype(v_out.dtype)


def adjoint_ends(bounds_ref, gk_ref, gv_ref, wide_ref, adj_ref, span, tiles):
    adj_ref[...] = jnp.zeros_like(adj_ref)
    groups = span // GROUP

    @pl.loop(0, groups)
    def _(step):
        group = groups - 1 - step

        def body(keep):
            for lt in range(tiles):
                gk = steps_of(gk_ref, lt, group, span)
                gv = steps_of(gv_ref, lt, group, span)
                for n in range(STATES):
                    a, ck, cv = wide_ref[0, n, lt], wide_ref[1, n, lt], wide_ref[2, n, lt]
                    m = adj_ref[lt, n * SEG : (n + 1) * SEG, :]
                    for j in reversed(range(GROUP)):
                        m = a * (m + (ck * gk[j] + cv * gv[j]))
                        if keep is not None:
                            m = m * keep[j]
                    adj_ref[lt, n * SEG : (n + 1) * SEG, :] = m

        with_masks(bounds_ref, span, group, body)


def adjoint_ends_kernel(span, tiles, bounds_ref, gk_in, gv_in, par_ref, far_ref, out_ref, gk_ref, gv_ref, wide_ref, adj_ref):
    split_lanes(gk_in, gk_ref)
    split_lanes(gv_in, gv_ref)
    seg_scan_params(par_ref, wide_ref)
    adjoint_ends(bounds_ref, gk_ref, gv_ref, wide_ref, adj_ref, span, tiles)
    for lt in range(tiles):
        lanes = slice(lt * LANES, (lt + 1) * LANES)
        start = jnp.zeros((STATES, LANES), jnp.float32)
        for seg in reversed(range(SEG)):
            end = adj_ref[lt, pl.ds(seg, STATES, stride=SEG), :]
            start = end + far_ref[:, lanes] * start * no_bound_in_seg(bounds_ref, span, seg)
        out_ref[:, lanes] = start


def backward_kernel(span, tiles, bounds_ref, u_in, gk_in, gv_in, par_ref, far_ref, last_ref, ckpt_ref,
                    gu_out, sums_out, u_ref, gk_ref, gv_ref, gu_ref, wide_ref, adj_ref, acc_ref):
    split_lanes(u_in, u_ref)
    split_lanes(gk_in, gk_ref)
    split_lanes(gv_in, gv_ref)
    seg_scan_params(par_ref, wide_ref)
    adjoint_ends(bounds_ref, gk_ref, gv_ref, wide_ref, adj_ref, span, tiles)
    for _ in chain_backward(bounds_ref, adj_ref, last_ref[...], far_ref, span, tiles):
        pass
    acc_ref[...] = jnp.zeros_like(acc_ref)
    groups = span // GROUP

    @pl.loop(0, groups)
    def _(step):
        group = groups - 1 - step

        def body(keep):
            for lt in range(tiles):
                u = steps_of(u_ref, lt, group, span)
                gk = steps_of(gk_ref, lt, group, span)
                gv = steps_of(gv_ref, lt, group, span)
                gu = [jnp.zeros((SEG, LANES), jnp.float32)] * GROUP
                for n in range(STATES):
                    mine = slice(n * SEG, (n + 1) * SEG)
                    a, ck, cv = wide_ref[0, n, lt], wide_ref[1, n, lt], wide_ref[2, n, lt]
                    states = [ckpt_ref[group, lt, mine, :]]
                    for j in range(GROUP):
                        s = a * states[j]
                        if keep is not None:
                            s = s * keep[j]
                        states.append(s + u[j])
                    m = adj_ref[lt, mine, :]
                    sum_k, sum_v, sum_a = acc_ref[0, lt, mine, :], acc_ref[1, lt, mine, :], acc_ref[2, lt, mine, :]
                    for j in reversed(range(GROUP)):
                        lam = m + (ck * gk[j] + cv * gv[j])
                        gu[j] = gu[j] + lam
                        sum_k = sum_k + gk[j] * states[j + 1]
                        sum_v = sum_v + gv[j] * states[j + 1]
                        m = a * lam
                        if keep is not None:
                            m = m * keep[j]
                        sum_a = sum_a + m * states[j]
                    acc_ref[0, lt, mine, :] = sum_k
                    acc_ref[1, lt, mine, :] = sum_v
                    acc_ref[2, lt, mine, :] = sum_a
                    adj_ref[lt, mine, :] = m
                for j in range(GROUP):
                    gu_ref[lt, pl.ds(group * GROUP + j, SEG, stride=span), :] = gu[j]

        with_masks(bounds_ref, span, group, body)

    for lt in range(tiles):
        lanes = slice(lt * LANES, (lt + 1) * LANES)
        gu_out[:, lanes] = gu_ref[lt].astype(gu_out.dtype)
        for p in range(3):
            total = acc_ref[p, lt, pl.ds(0, STATES, stride=SEG), :]
            for seg in range(1, SEG):
                total = total + acc_ref[p, lt, pl.ds(seg, STATES, stride=SEG), :]
            sums_out[p, :, lanes] = total


LIMIT = pltpu.CompilerParams(vmem_limit_bytes=48 * 2**20)


def f32(*shape):
    return pltpu.VMEM(shape, jnp.float32)


def ssm_ends(bounds, u, par, far, name="ssm_ends"):
    rows, width = u.shape
    span, tiles = rows // SEG, width // LANES
    return pl.pallas_call(
        functools.partial(ends_kernel, span, tiles),
        out_shape=jax.ShapeDtypeStruct((STATES, width), jnp.float32),
        in_specs=[SMEM] + [VMEM] * 3, out_specs=VMEM,
        scratch_shapes=[f32(tiles, rows, LANES), f32(3, STATES, tiles, SEG, LANES), f32(tiles, STATES * SEG, LANES)],
        compiler_params=LIMIT, name=name)(bounds, u, par, far)


def ssm_forward(bounds, u, par, far, first, name="ssm_forward"):
    rows, width = u.shape
    span, tiles = rows // SEG, width // LANES
    return pl.pallas_call(
        functools.partial(forward_kernel, span, tiles),
        out_shape=(jax.ShapeDtypeStruct((rows, width), jnp.bfloat16), jax.ShapeDtypeStruct((rows, width), jnp.bfloat16),
                   jax.ShapeDtypeStruct((span // GROUP, tiles, STATES * SEG, LANES), jnp.float32)),
        in_specs=[SMEM] + [VMEM] * 4, out_specs=(VMEM,) * 3,
        scratch_shapes=[f32(tiles, rows, LANES)] * 3 + [f32(3, STATES, tiles, SEG, LANES), f32(tiles, STATES * SEG, LANES)],
        compiler_params=LIMIT, name=name)(bounds, u, par, far, first)


def ssm_adjoint_ends(bounds, gk, gv, par, far, name="ssm_adjoint_ends"):
    rows, width = gk.shape
    span, tiles = rows // SEG, width // LANES
    return pl.pallas_call(
        functools.partial(adjoint_ends_kernel, span, tiles),
        out_shape=jax.ShapeDtypeStruct((STATES, width), jnp.float32),
        in_specs=[SMEM] + [VMEM] * 4, out_specs=VMEM,
        scratch_shapes=[f32(tiles, rows, LANES)] * 2 + [f32(3, STATES, tiles, SEG, LANES), f32(tiles, STATES * SEG, LANES)],
        compiler_params=LIMIT, name=name)(bounds, gk, gv, par, far)


def ssm_backward(bounds, u, gk, gv, par, far, last, ckpt, name="ssm_backward"):
    rows, width = u.shape
    span, tiles = rows // SEG, width // LANES
    return pl.pallas_call(
        functools.partial(backward_kernel, span, tiles),
        out_shape=(jax.ShapeDtypeStruct((rows, width), jnp.bfloat16), jax.ShapeDtypeStruct((3, STATES, width), jnp.float32)),
        in_specs=[SMEM] + [VMEM] * 7, out_specs=(VMEM,) * 2,
        scratch_shapes=[f32(tiles, rows, LANES)] * 4 + [f32(3, STATES, tiles, SEG, LANES), f32(tiles, STATES * SEG, LANES), f32(3, tiles, STATES * SEG, LANES)],
        compiler_params=LIMIT, name=name)(bounds, u, gk, gv, par, far, last, ckpt)


QT = 256
NEG = -1e30
SCALE = HEAD ** (-0.5)


def tiles_of(rows, shift):
    out = []
    for r in range(0, rows, QT):
        first = max(0, r + shift - (BLOCK + CTX)) if shift == 0 else 0
        out.append((r, first, r + shift + QT))
    return out


def lowest_key(starts_ref, row0, shift):
    if shift:
        return jnp.full((1, QT), starts_ref[0], jnp.int32)
    rows = lax.broadcasted_iota(jnp.int32, (1, QT), 1) + row0
    start = jnp.zeros((1, QT), jnp.int32)
    for k in range(starts_ref.shape[0]):
        start = jnp.where(rows >= starts_ref[k], starts_ref[k], start)
    block = ((rows - start) // BLOCK) * BLOCK - CTX
    return start + jnp.maximum(block, 0)


def allowed_keys(starts_ref, q0, k0, k1, shift):
    low = lowest_key(starts_ref, q0, shift)
    high = lax.broadcasted_iota(jnp.int32, (1, QT), 1) + (q0 + shift)
    keys = lax.broadcasted_iota(jnp.int32, (k1 - k0, QT), 0) + k0
    return (keys >= low) & (keys <= high)


def dot_nt(a, b):
    return lax.dot_general(a, b, (((1,), (1,)), ((), ())), preferred_element_type=jnp.float32)


def dot_nn(a, b):
    return lax.dot_general(a, b, (((1,), (0,)), ((), ())), preferred_element_type=jnp.float32)


def attend_kernel(tiles, shift, starts_ref, q_ref, k_ref, v_ref, o_ref, lse_ref, vt_ref):
    vt_ref[...] = v_ref[...].T
    for q0, k0, k1 in tiles:
        scores = dot_nt(k_ref[k0:k1, :], q_ref[q0 : q0 + QT, :]) * SCALE
        scores = jnp.where(allowed_keys(starts_ref, q0, k0, k1, shift), scores, NEG)
        top = jnp.max(scores, axis=0, keepdims=True)
        exps = jnp.exp(scores - top)
        total = jnp.sum(exps, axis=0, keepdims=True)
        probs = (exps * (1.0 / total)).astype(jnp.bfloat16)
        mixed = dot_nn(vt_ref[:, k0:k1], probs)
        o_ref[q0 : q0 + QT, :] = mixed.T.astype(o_ref.dtype)
        lse_ref[0, 0, q0 : q0 + QT] = (top + jnp.log(total))[0]


def attend(starts, q, k, v, shift, name):
    rows, width = q.shape
    heads = width // HEAD
    keys = k.shape[0]
    lane = lambda h: (0, h)
    return pl.pallas_call(
        functools.partial(attend_kernel, tiles_of(rows, shift), shift),
        grid=(heads,),
        out_shape=(jax.ShapeDtypeStruct((rows, width), jnp.bfloat16), jax.ShapeDtypeStruct((heads, 1, rows), jnp.float32)),
        in_specs=[SMEM, pl.BlockSpec((rows, HEAD), lane), pl.BlockSpec((keys, HEAD), lane), pl.BlockSpec((keys, HEAD), lane)],
        out_specs=(pl.BlockSpec((rows, HEAD), lane), pl.BlockSpec((1, 1, rows), lambda h: (h, 0, 0))),
        scratch_shapes=[pltpu.VMEM((HEAD, keys), jnp.bfloat16)],
        compiler_params=pltpu.CompilerParams(vmem_limit_bytes=40 * 2**20),
        name=name)(starts, q, k, v)


def attend_back_kernel(tiles, shift, starts_ref, q_ref, k_ref, v_ref, g_ref, lse_ref, dq_ref, dk_ref, dv_ref, kt_ref):
    kt_ref[...] = k_ref[...].T
    dk_ref[...] = jnp.zeros_like(dk_ref)
    dv_ref[...] = jnp.zeros_like(dv_ref)
    for q0, k0, k1 in tiles:
        q = q_ref[q0 : q0 + QT, :]
        g = g_ref[q0 : q0 + QT, :]
        lse = lse_ref[0, :, q0 : q0 + QT]
        scores = dot_nt(k_ref[k0:k1, :], q) * SCALE
        probs = jnp.where(allowed_keys(starts_ref, q0, k0, k1, shift), jnp.exp(scores - lse), 0.0)
        grad_probs = dot_nt(v_ref[k0:k1, :], g)
        dv_ref[0, k0:k1, :] += dot_nn(probs.astype(jnp.bfloat16), g)
        delta = jnp.sum(probs * grad_probs, axis=0, keepdims=True)
        grad_scores = (probs * (grad_probs - delta)).astype(jnp.bfloat16)
        dk_ref[0, k0:k1, :] += dot_nn(grad_scores, q) * SCALE
        dq_ref[q0 : q0 + QT, :] = (dot_nn(kt_ref[:, k0:k1], grad_scores) * SCALE).T.astype(dq_ref.dtype)


def attend_back(starts, q, k, v, g, lse, shift, name):
    rows, width = q.shape
    heads = width // HEAD
    keys = k.shape[0]
    lane = lambda h: (0, h)
    rspec, kspec = pl.BlockSpec((rows, HEAD), lane), pl.BlockSpec((keys, HEAD), lane)
    gspec = pl.BlockSpec((1, keys, HEAD), lambda h: (h, 0, 0))
    return pl.pallas_call(
        functools.partial(attend_back_kernel, tiles_of(rows, shift), shift),
        grid=(heads,),
        out_shape=(jax.ShapeDtypeStruct((rows, width), jnp.bfloat16), jax.ShapeDtypeStruct((heads, keys, HEAD), jnp.float32), jax.ShapeDtypeStruct((heads, keys, HEAD), jnp.float32)),
        in_specs=[SMEM, rspec, kspec, kspec, rspec, pl.BlockSpec((1, 1, rows), lambda h: (h, 0, 0))],
        out_specs=(rspec, gspec, gspec),
        scratch_shapes=[pltpu.VMEM((HEAD, keys), jnp.bfloat16)],
        compiler_params=pltpu.CompilerParams(vmem_limit_bytes=40 * 2**20),
        name=name)(starts, q, k, v, g, lse)


ROWS = 256
SUB = 32
DEEP = 3
MESH = pl.DeviceIdType.MESH


def group_of_four():
    me = lax.axis_index("mp")
    mate = me + 1 - 2 * (me % 2)
    return me, mate, (me + 2) % 4, (mate + 2) % 4


def greet_group():
    _, mate, over, _ = group_of_four()
    dp = lax.axis_index("dp")
    barrier = pltpu.get_barrier_semaphore()
    for peer in (mate, over):
        pl.semaphore_signal(barrier, inc=1, device_id=(dp, peer), device_id_type=MESH)
    pl.semaphore_wait(barrier, 2)


class Mover:
    def __init__(self, send_sem, recv_sem):
        self.send_sem, self.recv_sem = send_sem, recv_sem
        self.dp = lax.axis_index("dp")

    def copy(self, src, dst, kind, c, peer):
        return pltpu.make_async_remote_copy(
            src_ref=src, dst_ref=dst, send_sem=self.send_sem.at[kind, c], recv_sem=self.recv_sem.at[kind, c],
            device_id=(self.dp, peer), device_id_type=MESH)


class Gather:
    def __init__(self, mover, base, full, rows, own=None):
        self.mover, self.base, self.full, self.rows, self.own = mover, base, full, rows, own
        self.me, self.mate, self.over, self.far = group_of_four()

    def at(self, owner, c):
        return self.full.at[owner, pl.ds(pl.multiple_of(c * self.rows, self.rows), self.rows)]

    def mine(self, c):
        if self.own is None:
            return self.at(self.me, c)
        return self.own.at[pl.ds(pl.multiple_of(c * self.rows, self.rows), self.rows)]

    def near(self, c):
        return self.mover.copy(self.mine(c), self.at(self.me, c), self.base, c, self.mate)

    def across(self, c):
        return self.mover.copy(self.mine(c), self.at(self.me, c), self.base + 1, c, self.over)

    def onward(self, c):
        return self.mover.copy(self.at(self.over, c), self.at(self.over, c), self.base + 2, c, self.mate)

    def start(self, c):
        self.across(c).start()
        self.near(c).start()

    def forward(self, c):
        self.across(c).wait_recv()
        self.onward(c).start()

    def finish(self, c):
        self.near(c).wait()
        self.across(c).wait_send()
        self.onward(c).wait()


class Scatter:
    def __init__(self, mover, base, part, near, across, joint):
        self.mover, self.base = mover, base
        self.part, self.near, self.across, self.joint = part, near, across, joint
        self.me, self.mate, self.over, self.far = group_of_four()

    def to_join(self, c):
        return self.mover.copy(self.part.at[c % DEEP, self.far], self.near.at[c, 1], self.base + 1, c, self.mate)

    def to_keep(self, c):
        return self.mover.copy(self.part.at[c % DEEP, self.mate], self.near.at[c, 0], self.base, c, self.mate)

    def joined(self, c):
        return self.mover.copy(self.joint.at[c % DEEP], self.across.at[c], self.base + 2, c, self.over)

    def start(self, c, parts):
        for d in range(4):
            self.part[c % DEEP, d] = parts(d).astype(jnp.bfloat16)
        self.to_join(c).start()
        self.to_keep(c).start()

    def combine(self, c):
        s = c % DEEP
        self.to_join(c).wait_recv()
        self.joint[s] = (self.part[s, self.over].astype(jnp.float32) + self.near[c, 1].astype(jnp.float32)).astype(jnp.bfloat16)
        self.joined(c).start()

    def finish(self, c):
        self.to_join(c).wait_send()
        self.to_keep(c).wait()
        self.joined(c).wait()
        return (self.part[c % DEEP, self.me].astype(jnp.float32) + self.near[c, 0].astype(jnp.float32)
                + self.across[c].astype(jnp.float32))


def mm(left, right, left_dim, right_dim):
    return lax.dot_general(left, right, (((left_dim,), (right_dim,)), ((), ())), preferred_element_type=jnp.float32)


def cut(d, width):
    return slice(d * width, (d + 1) * width)


def normed(full, c, sub, rows):
    first = pl.multiple_of(c * rows + sub * SUB, SUB)
    return jnp.concatenate([full[d, pl.ds(first, SUB), :].astype(jnp.float32) for d in range(4)], axis=1)


def middle_kernel(chunks, att_ref, tok_ref, cot_ref, w_out_ref, w_up_ref, w_down_ref, gain_ref,
                  result_ref, gm_ref, gatt_ref, grads_ref, ggain_ref,
                  gdown_ref, gup_ref, gout_ref, mid_full, gm_full, mid_ref, part, near, across, joint, n2_ref, act_ref, gpre_ref, pre_ref, gact_ref, mean_ref, inv_ref,
                  send_sem, recv_sem):
    width = att_ref.shape[1]
    rows = ROWS
    me = lax.axis_index("mp")
    mover = Mover(send_sem, recv_sem)
    sums = [Scatter(mover, 3 * r, part.at[r], near.at[r], across.at[r], joint.at[r]) for r in range(3)]
    gather_mid = Gather(mover, 9, mid_full, rows)
    gather_gm = Gather(mover, 12, gm_full, rows)
    greet_group()
    gdown_ref[...] = jnp.zeros_like(gdown_ref)
    gup_ref[...] = jnp.zeros_like(gup_ref)
    gout_ref[...] = jnp.zeros_like(gout_ref)
    ggain_ref[...] = jnp.zeros_like(ggain_ref)

    def span(c):
        return pl.ds(pl.multiple_of(c * rows, rows), rows)

    def project(c):
        att = att_ref[span(c), :]
        sums[0].start(c, lambda d: mm(att, w_out_ref[:, cut(d, width)], 1, 0))

    def add_middle(c):
        middle = tok_ref[span(c), :].astype(jnp.float32) + sums[0].finish(c)
        mid_ref[span(c), :] = middle
        mid_full[me, span(c), :] = middle.astype(jnp.bfloat16)
        gather_mid.start(c)

    def feed_forward(c):
        gather_mid.finish(c)

        @pl.loop(0, rows // SUB)
        def _(sub):
            mine = pl.ds(pl.multiple_of(sub * SUB, SUB), SUB)
            v = normed(mid_full, c, sub, rows)
            mean = jnp.mean(v, axis=1, keepdims=True)
            centred = v - mean
            inv = lax.rsqrt(jnp.mean(centred * centred, axis=1, keepdims=True) + EPS)
            mean_ref[mine, :] = mean
            inv_ref[mine, :] = inv
            n2_ref[mine, :] = (centred * inv * gain_ref[...]).astype(jnp.bfloat16)

        cot = jnp.concatenate([cot_ref[d, span(c), :] for d in range(4)], axis=1)
        pre_ref[...] = mm(n2_ref[...], w_up_ref[...], 1, 0)
        gact_ref[...] = mm(cot, w_down_ref[...], 1, 1)

        @pl.loop(0, rows // SUB)
        def _(sub):
            mine = pl.ds(pl.multiple_of(sub * SUB, SUB), SUB)
            v = pre_ref[mine, :]
            cdf = 0.5 * (1.0 + lax.erf(v * (0.5**0.5)))
            act_ref[mine, :] = (v * cdf).astype(jnp.bfloat16)
            slope = cdf + v * (jnp.exp(-0.5 * v * v) * 0.3989422804014327)
            gpre_ref[mine, :] = (slope * gact_ref[mine, :]).astype(jnp.bfloat16)

        sums[1].start(c, lambda d: mm(act_ref[...], w_down_ref[:, cut(d, width)], 1, 0))
        gact_ref[...] = mm(gpre_ref[...], w_up_ref[...], 1, 1)

        @pl.loop(0, rows // SUB)
        def _(sub):
            mine = pl.ds(pl.multiple_of(sub * SUB, SUB), SUB)
            xhat = (normed(mid_full, c, sub, rows) - mean_ref[mine, :]) * inv_ref[mine, :]
            up = gact_ref[mine, :]
            both = up * xhat
            ggain_ref[...] += jnp.sum(both.reshape(SUB // 8, 8, both.shape[1]), axis=0)
            scaled = up * gain_ref[...]
            plain = jnp.mean(scaled, axis=1, keepdims=True)
            cross = jnp.mean(scaled * xhat, axis=1, keepdims=True)
            gact_ref[mine, :] = inv_ref[mine, :] * (scaled - plain - xhat * cross)

        sums[2].start(c, lambda d: gact_ref[:, cut(d, width)])
        gdown_ref[...] += mm(act_ref[...], cot, 0, 0)
        gup_ref[...] += mm(n2_ref[...], gpre_ref[...], 0, 0)

    def finish_sums(c):
        gm = cot_ref[me, span(c), :].astype(jnp.float32) + sums[2].finish(c)
        for lt in range(width // LANES):
            gm_ref[lt, span(c), :] = gm[:, cut(lt, LANES)]
        gm_full[me, span(c), :] = gm.astype(jnp.bfloat16)
        gather_gm.start(c)
        result_ref[span(c), :] = (mid_ref[span(c), :] + sums[1].finish(c)).astype(result_ref.dtype)

    def back_project(c):
        gather_gm.finish(c)
        att = att_ref[span(c), :]
        total = None
        for d in range(4):
            gm = gm_full[d, span(c), :]
            gout_ref[:, cut(d, width)] += mm(att, gm, 0, 0)
            term = mm(gm, w_out_ref[:, cut(d, width)], 1, 1)
            total = term if total is None else total + term
        gatt_ref[span(c), :] = total.astype(gatt_ref.dtype)

    def combine_late(c):
        sums[2].combine(c)
        sums[1].combine(c)

    stages = [(add_middle, 2), (finish_sums, 6), (sums[0].combine, 1), (combine_late, 5), (gather_mid.forward, 3),
              (gather_gm.forward, 7), (project, 0), (feed_forward, 4), (back_project, 8)]

    @pl.loop(0, chunks + 8)
    def _(i):
        for stage, lag in stages:
            @pl.when(jnp.logical_and(i >= lag, i < chunks + lag))
            def _(stage=stage, lag=lag):
                stage(i - lag)

    first = 0
    for total in (gdown_ref, gup_ref, gout_ref):
        grads_ref[first : first + total.shape[0], :] = total[...].astype(jnp.bfloat16)
        first += total.shape[0]


def middle_phase(att, tok, cot_full, w_out, w_up, w_down, gain):
    rows, width = att.shape
    full = w_out.shape[1]
    hidden = w_up.shape[1]
    chunks = rows // ROWS
    bf = jnp.bfloat16

    def out(shape, dtype):
        return jax.ShapeDtypeStruct(shape, dtype)

    def buf(*shape, dtype=bf):
        return pltpu.VMEM(shape, dtype)

    return pl.pallas_call(
        functools.partial(middle_kernel, chunks),
        out_shape=(out((rows, width), bf), out((width // LANES, rows, LANES), jnp.float32), out((rows, width), bf),
                   out((hidden + full + width, full), bf), out((8, full), jnp.float32)),
        in_specs=[VMEM] * 7, out_specs=(VMEM,) * 5,
        scratch_shapes=[
            buf(hidden, full, dtype=jnp.float32), buf(full, hidden, dtype=jnp.float32), buf(width, full, dtype=jnp.float32),
            buf(4, rows, width), buf(4, rows, width), buf(rows, width, dtype=jnp.float32),
            buf(3, DEEP, 4, ROWS, width), buf(3, chunks, 2, ROWS, width), buf(3, chunks, ROWS, width), buf(3, DEEP, ROWS, width),
            buf(ROWS, full), buf(ROWS, hidden), buf(ROWS, hidden),
            buf(ROWS, hidden, dtype=jnp.float32), buf(ROWS, hidden, dtype=jnp.float32),
            buf(ROWS, 1, dtype=jnp.float32), buf(ROWS, 1, dtype=jnp.float32),
            pltpu.SemaphoreType.DMA((15, chunks)), pltpu.SemaphoreType.DMA((15, chunks)),
        ],
        compiler_params=pltpu.CompilerParams(collective_id=0, has_side_effects=True, vmem_limit_bytes=60 * 2**20),
        cost_estimate=pl.CostEstimate(flops=30 * 10**9, bytes_accessed=30 * 10**6, transcendentals=4 * 10**6),
        name="middle_phase")(att, tok, cot_full, w_out, w_up, w_down, gain)


POINTS = 14


def ring_place(index, count):
    side, along = index % 2, index // 2
    return (1 - side) * along + side * (count - 1 - along)


def ring_index(place, count):
    side = place // (count // 2)
    return (1 - side) * (2 * place) + side * (2 * (count - 1 - place) + 1)


class Ring:
    def __init__(self, count, half, data, total, held, send_sem, recv_sem):
        self.count, self.half = count, half
        self.data, self.total, self.held = data, total, held
        self.send_sem, self.recv_sem = send_sem, recv_sem
        self.place = ring_place(lax.axis_index("dp"), count)
        self.mp = lax.axis_index("mp")
        self.events = 2 * count - 1

    def rows(self, chunk, way):
        return pl.ds(pl.multiple_of((2 * chunk + way) * self.half, self.half), self.half)

    def chunk(self, way, back):
        return (self.place + (1 - 2 * (1 - way)) * back + 2 * self.count) % self.count

    def copy(self, src, dst, way, step):
        peer = ring_index((self.place + 1 - 2 * way + self.count) % self.count, self.count)
        return pltpu.make_async_remote_copy(
            src_ref=src, dst_ref=dst, send_sem=self.send_sem.at[way, step], recv_sem=self.recv_sem.at[way, step],
            device_id=(peer, self.mp), device_id_type=MESH)

    def add_copy(self, way, step):
        return self.copy(self.held.at[way, step], self.held.at[way, step], way, step)

    def give_copy(self, way, step, chunk):
        piece = self.total.at[self.rows(chunk, way)]
        return self.copy(piece, piece, way, self.count - 1 + step)

    def event(self, e):
        n = self.count

        @pl.when(e == 0)
        def _():
            for way in range(2):
                self.copy(self.data.at[self.rows(self.chunk(way, 0), way)], self.held.at[way, 0], way, 0).start()

        @pl.when(jnp.logical_and(e >= 1, e < n - 1))
        def _():
            for way in range(2):
                self.add_copy(way, e - 1).wait_recv()
                own = self.data[self.rows(self.chunk(way, e), way), :].astype(jnp.float32)
                self.held[way, e - 1] = (self.held[way, e - 1].astype(jnp.float32) + own).astype(jnp.bfloat16)
                self.copy(self.held.at[way, e - 1], self.held.at[way, e], way, e).start()

        @pl.when(e == n - 1)
        def _():
            for way in range(2):
                self.add_copy(way, n - 2).wait_recv()
                mine = self.chunk(way, n - 1)
                own = self.data[self.rows(mine, way), :].astype(jnp.float32)
                self.total[self.rows(mine, way), :] = (self.held[way, n - 2].astype(jnp.float32) + own).astype(jnp.bfloat16)
                self.give_copy(way, 0, mine).start()

        @pl.when(jnp.logical_and(e >= n, e < 2 * n - 2))
        def _():
            for way in range(2):
                self.give_copy(way, e - n, self.chunk(way, e - n)).wait_recv()
                self.give_copy(way, e - n + 1, self.chunk(way, e - n)).start()

        @pl.when(e == 2 * n - 2)
        def _():
            for way in range(2):
                self.give_copy(way, n - 2, self.chunk(way, n - 2)).wait_recv()

    def point(self, k):
        first, last = (k * (self.events - 1)) // POINTS, ((k + 1) * (self.events - 1)) // POINTS

        @pl.loop(first + 1, last + 1)
        def _(e):
            self.event(e)

    def settle(self):
        @pl.loop(0, 2 * (self.count - 1))
        def _(step):
            for way in range(2):
                self.copy(self.held.at[way, 0], self.held.at[way, 0], way, step).wait_send()


class Spread:
    def __init__(self, count, send_sem, recv_sem):
        self.count, self.send_sem, self.recv_sem = count, send_sem, recv_sem
        self.me, self.mp = lax.axis_index("dp"), lax.axis_index("mp")

    def copy(self, src, dst, o):
        return pltpu.make_async_remote_copy(
            src_ref=src, dst_ref=dst, send_sem=self.send_sem.at[o], recv_sem=self.recv_sem.at[o],
            device_id=((self.me + o) % self.count, self.mp), device_id_type=MESH)

    def start(self, src, dst):
        @pl.loop(1, self.count)
        def _(o):
            self.copy(src(o), dst(o), o).start()

    def wait(self, src, dst):
        @pl.loop(1, self.count)
        def _(o):
            self.copy(src(o), dst(o), o).wait()


def greet_all(count):
    me, mp = lax.axis_index("dp"), lax.axis_index("mp")
    barrier = pltpu.get_barrier_semaphore()

    @pl.loop(1, count)
    def _(o):
        pl.semaphore_signal(barrier, inc=1, device_id=((me + o) % count, mp), device_id_type=MESH)

    for peer in group_of_four()[1:]:
        pl.semaphore_signal(barrier, inc=1, device_id=(me, peer), device_id_type=MESH)
    pl.semaphore_wait(barrier, count + 2)


def masks_of(bounds_ref, span, group):
    if bounds_ref is None:
        return None
    return [keep_mask(bounds_ref, span, group * GROUP + j) for j in range(GROUP)]


def open_segment(bounds_ref, span, seg):
    if bounds_ref is None:
        return 1.0
    return no_bound_in_seg(bounds_ref, span, seg)


def adjoint_pass(bounds_ref, gk_ref, gv_ref, wide_ref, adj_ref, span, tiles, row0, beside):
    adj_ref[...] = jnp.zeros_like(adj_ref)
    groups = span // GROUP

    @pl.loop(0, groups)
    def _(step):
        group = groups - 1 - step
        keep = masks_of(bounds_ref, span, group)
        for lt in range(tiles):
            gk = [gk_ref[lt, pl.ds(row0 + group * GROUP + j, SEG, stride=span), :] for j in range(GROUP)]
            gv = [gv_ref[lt, pl.ds(row0 + group * GROUP + j, SEG, stride=span), :] for j in range(GROUP)]
            for n in range(STATES):
                mine = slice(n * SEG, (n + 1) * SEG)
                a, ck, cv = wide_ref[0, n, lt], wide_ref[1, n, lt], wide_ref[2, n, lt]
                m = adj_ref[lt, mine, :]
                for j in reversed(range(GROUP)):
                    m = a * (m + (ck * gk[j] + cv * gv[j]))
                    if keep is not None:
                        m = m * keep[j]
                adj_ref[lt, mine, :] = m
        beside(step)


def adjoint_chain(bounds_ref, adj_ref, last, far_ref, span, tiles, write):
    ends = []
    for lt in range(tiles):
        lanes = slice(lt * LANES, (lt + 1) * LANES)
        start, far = last[:, lanes], far_ref[:, lanes]
        for seg in reversed(range(SEG)):
            rows = pl.ds(seg, STATES, stride=SEG)
            end = adj_ref[lt, rows, :]
            if write:
                adj_ref[lt, rows, :] = start
            start = end + far * start * open_segment(bounds_ref, span, seg)
        ends.append(start)
    return jnp.concatenate(ends, axis=1)


def adjoint_full(bounds_ref, u_ref, gk_ref, gv_ref, ckpt_ref, wide_ref, adj_ref, acc_ref, span, tiles, row0, group0, beside):
    groups = span // GROUP

    @pl.loop(0, groups)
    def _(step):
        group = groups - 1 - step
        keep = masks_of(bounds_ref, span, group)
        for lt in range(tiles):
            at = [pl.ds(row0 + group * GROUP + j, SEG, stride=span) for j in range(GROUP)]
            u = [u_ref[lt, r, :] for r in at]
            gk = [gk_ref[lt, r, :] for r in at]
            gv = [gv_ref[lt, r, :] for r in at]
            gu = [jnp.zeros((SEG, LANES), jnp.float32)] * GROUP
            for n in range(STATES):
                mine = slice(n * SEG, (n + 1) * SEG)
                a, ck, cv = wide_ref[0, n, lt], wide_ref[1, n, lt], wide_ref[2, n, lt]
                states = [ckpt_ref[group0 + group, lt, mine, :]]
                for j in range(GROUP):
                    s = a * states[j]
                    if keep is not None:
                        s = s * keep[j]
                    states.append(s + u[j])
                m = adj_ref[lt, mine, :]
                sum_k, sum_v, sum_a = acc_ref[0, lt, mine, :], acc_ref[1, lt, mine, :], acc_ref[2, lt, mine, :]
                for j in reversed(range(GROUP)):
                    lam = m + (ck * gk[j] + cv * gv[j])
                    gu[j] = gu[j] + lam
                    sum_k = sum_k + gk[j] * states[j + 1]
                    sum_v = sum_v + gv[j] * states[j + 1]
                    m = a * lam
                    if keep is not None:
                        m = m * keep[j]
                    sum_a = sum_a + m * states[j]
                acc_ref[0, lt, mine, :] = sum_k
                acc_ref[1, lt, mine, :] = sum_v
                acc_ref[2, lt, mine, :] = sum_a
                adj_ref[lt, mine, :] = m
            for j in range(GROUP):
                u_ref[lt, at[j], :] = gu[j]
        beside(step)


def tail_kernel(count, half, block, bounds_ref, grads_hbm, n1_hbm, u_hbm, gk_hbm, gv_hbm, ckpt_hbm, gm_hbm,
                gq_ref, inv_ref, w_in_ref, w_query_ref, par_ref, far_ref, rate_ref, gain_ref, gain_two_ref,
                grad_tokens_ref, total_ref, win_ref, sums_ref, gains_ref,
                grads_ref, n1_ref, u_ref, gk_ref, gv_ref, ckpt_ref, wide_ref, adj_ref, adj_long, acc_ref,
                gssm_ref, up_ref, ggain_ref, held, win_data, win_held, piece_ref, piece_held, small_ref, small_held, gain_held,
                part, near, across, joint, load_sem, ring_send, ring_recv, mp_send, mp_recv, dp_send, dp_recv):
    rows, width = gq_ref.shape
    tiles = width // LANES
    full = n1_ref.shape[1]
    me = lax.axis_index("dp")
    mp = lax.axis_index("mp")
    chunks = rows // ROWS
    long_span, short_span = LONG_DEV // SEG, (rows - LONG_DEV) // SEG
    long_groups, short_groups = long_span // GROUP, short_span // GROUP
    known = grads_hbm.shape[0]
    loads = [pltpu.make_async_copy(src, dst, load_sem.at[i]) for i, (src, dst) in enumerate(
        [(gk_hbm, gk_ref), (gv_hbm, gv_ref), (n1_hbm, n1_ref), (grads_hbm, grads_ref.at[pl.ds(0, known)]),
         (u_hbm, u_ref), (ckpt_hbm, ckpt_ref), (gm_hbm, gk_ref)])]
    for load in loads[:6]:
        load.start()
    seg_scan_params(par_ref, wide_ref)
    acc_ref[...] = jnp.zeros_like(acc_ref)
    ggain_ref[...] = jnp.zeros_like(ggain_ref)
    ring = Ring(count, half, grads_ref, total_ref, held, ring_send, ring_recv)
    mover = Mover(mp_send, mp_recv)
    token_sum = Scatter(mover, 0, part, near, across, joint)
    first_spread = Spread(count, dp_send.at[0], dp_recv.at[0])
    scatter_spread = Spread(count, dp_send.at[1], dp_recv.at[1])
    gather_spread = Spread(count, dp_send.at[2], dp_recv.at[2])
    small_spread = Spread(count, dp_send.at[3], dp_recv.at[3])
    greet_all(count)

    def nothing(step):
        del step

    loads[0].wait()
    loads[1].wait()
    adjoint_pass(None, gk_ref, gv_ref, wide_ref, adj_long, long_span, tiles, 0, nothing)
    zero = jnp.zeros((STATES, width), jnp.float32)
    piece_ref[...] = adjoint_chain(None, adj_long, zero, far_ref.at[0], long_span, tiles, False)
    first_spread.start(lambda o: piece_ref, lambda o: piece_held.at[me])

    loads[2].wait()
    loads[3].wait()
    for d in range(full // width):
        grads_ref[known : known + width, cut(d, width)] = mm(gq_ref[...], n1_ref[:, cut(d, width)], 0, 0).astype(jnp.bfloat16)
    if grads_ref.shape[0] > known + width:
        grads_ref[known + width :, :] = jnp.zeros((grads_ref.shape[0] - known - width, full), jnp.bfloat16)
    ring.event(0)

    loads[4].wait()
    loads[5].wait()

    def beside_first(step):
        @pl.when(step == short_groups - 1)
        def _():
            ring.point(0)

    adjoint_pass(bounds_ref, gk_ref, gv_ref, wide_ref, adj_ref, short_span, tiles, LONG_DEV, beside_first)
    adjoint_chain(bounds_ref, adj_ref, zero, far_ref.at[1], short_span, tiles, True)

    def beside_second(step):
        @pl.when(step % 6 == 5)
        def _():
            ring.point(1 + step // 6)

    adjoint_full(bounds_ref, u_ref, gk_ref, gv_ref, ckpt_ref, wide_ref, adj_ref, acc_ref,
                 short_span, tiles, LONG_DEV, long_groups, beside_second)

    first_spread.wait(lambda o: piece_ref, lambda o: piece_held.at[me])

    def fold(d, total):
        gap = d - me - 1
        weight = jnp.exp(rate_ref[...] * (-LONG_DEV * jnp.maximum(gap, 0)).astype(jnp.float32))
        return total + jnp.where(gap >= 0, weight * piece_held[d], 0.0)

    piece_held[me] = zero
    last = lax.fori_loop(0, count, fold, zero)
    adjoint_chain(None, adj_long, last, far_ref.at[0], long_span, tiles, True)
    adjoint_full(None, u_ref, gk_ref, gv_ref, ckpt_ref, wide_ref, adj_long, acc_ref,
                 long_span, tiles, 0, 0, nothing)
    loads[6].start()
    ring.point(5)

    for lt in range(tiles):
        gssm_ref[:, lt * LANES : (lt + 1) * LANES] = u_ref[lt].astype(jnp.bfloat16)
        for p in range(3):
            total = acc_ref[p, lt, pl.ds(0, STATES, stride=SEG), :]
            for seg in range(1, SEG):
                total = total + acc_ref[p, lt, pl.ds(seg, STATES, stride=SEG), :]
            small_ref[p * STATES : (p + 1) * STATES, lt * LANES : (lt + 1) * LANES] = total

    for d in range(full // width):
        win_data[:width, cut(d, width)] = mm(gssm_ref[...], n1_ref[:, cut(d, width)], 0, 0).astype(jnp.bfloat16)
    if win_data.shape[0] > width:
        win_data[width:, :] = jnp.zeros((win_data.shape[0] - width, full), jnp.bfloat16)

    def win_rows(device):
        return pl.ds(pl.multiple_of(device * block, block), block)

    scatter_spread.start(lambda o: win_data.at[win_rows((me + o) % count)], lambda o: win_held.at[o])
    loads[6].wait()

    def span_of(c):
        return pl.ds(pl.multiple_of(c * ROWS, ROWS), ROWS)

    def project(c):
        up_ref[...] = mm(gssm_ref[span_of(c), :], w_in_ref[...], 1, 1) + mm(gq_ref[span_of(c), :], w_query_ref[...], 1, 1)

        @pl.loop(0, ROWS // SUB)
        def _(sub):
            mine = pl.ds(pl.multiple_of(sub * SUB, SUB), SUB)
            here = pl.ds(pl.multiple_of(c * ROWS + sub * SUB, SUB), SUB)
            xhat = n1_ref[here, :].astype(jnp.float32) * (1.0 / gain_ref[...])
            up = up_ref[mine, :]
            both = up * xhat
            ggain_ref[...] += jnp.sum(both.reshape(SUB // 8, 8, full), axis=0)
            scaled = up * gain_ref[...]
            plain = jnp.mean(scaled, axis=1, keepdims=True)
            cross = jnp.mean(scaled * xhat, axis=1, keepdims=True)
            up_ref[mine, :] = inv_ref[here, :] * (scaled - plain - xhat * cross)

        token_sum.start(c, lambda d: up_ref[:, cut(d, width)])

    def finish(c):
        gm = jnp.concatenate([gk_ref[lt, span_of(c), :] for lt in range(tiles)], axis=1)
        grad_tokens_ref[span_of(c), :] = (gm + token_sum.finish(c)).astype(grad_tokens_ref.dtype)

    stages = [(finish, 2), (token_sum.combine, 1), (project, 0)]

    @pl.loop(0, chunks + 2)
    def _(i):
        for stage, lag in stages:
            @pl.when(jnp.logical_and(i >= lag, i < chunks + lag))
            def _(stage=stage, lag=lag):
                stage(i - lag)

        @pl.when(i % 2 == 1)
        def _():
            ring.point(6 + i // 2)

    ggain = jnp.sum(ggain_ref[...], axis=0, keepdims=True)
    gtwo = jnp.sum(gain_two_ref[...], axis=0, keepdims=True)
    for d in range(full // width):
        small_ref[3 * STATES + d : 3 * STATES + d + 1, :] = ggain[:, cut(d, width)]
        small_ref[3 * STATES + 4 + d : 3 * STATES + 5 + d, :] = gtwo[:, cut(d, width)]
    small_spread.start(lambda o: small_ref, lambda o: small_held.at[me])
    small_held[me] = small_ref[...]

    scatter_spread.wait(lambda o: win_data.at[win_rows((me + o) % count)], lambda o: win_held.at[o])
    win_held[0] = win_data[win_rows(me), :]
    total = win_held[0].astype(jnp.float32)
    total = lax.fori_loop(1, count, lambda o, t: t + win_held[o].astype(jnp.float32), total)
    win_ref[win_rows(me), :] = total.astype(jnp.bfloat16)
    gather_spread.start(lambda o: win_ref.at[win_rows(me)], lambda o: win_ref.at[win_rows(me)])
    ring.point(11)
    small_spread.wait(lambda o: small_ref, lambda o: small_held.at[me])
    small = lax.fori_loop(1, count, lambda d, t: t + small_held[d], small_held[0])
    sums_ref[...] = small[: 3 * STATES]
    gain_held[mp] = small[3 * STATES :]
    group = group_of_four()
    sends = [mover.copy(gain_held.at[mp], gain_held.at[mp], 3, i, group[1 + i]) for i in range(3)]
    for send in sends:
        send.start()
    ring.point(12)
    for send in sends:
        send.wait()
    gains_ref[...] = ((gain_held[0] + gain_held[1]) + gain_held[2]) + gain_held[3]
    gather_spread.wait(lambda o: win_ref.at[win_rows(me)], lambda o: win_ref.at[win_rows(me)])
    ring.point(13)
    ring.settle()


def round_up(value, unit):
    return -(-value // unit) * unit


def tail_phase(bounds, grads, n1, u, gk, gv, ckpt, gm, gq, inv, w_in_t, w_query_t, par, far, rate, gain, gain_two_parts, count):
    rows, width = gq.shape
    tiles = width // LANES
    full = n1.shape[1]
    bf = jnp.bfloat16
    used = grads.shape[0] + width
    half = round_up(-(-used // (2 * count)), 16)
    block = round_up(-(-width // count), 16)

    def out(shape, dtype):
        return jax.ShapeDtypeStruct(shape, dtype)

    def buf(*shape, dtype=bf):
        return pltpu.VMEM(shape, dtype)

    def wide(*shape):
        return pltpu.VMEM(shape, jnp.float32)

    ANY = pl.BlockSpec(memory_space=pl.ANY)
    chunks = rows // ROWS
    dma = pltpu.SemaphoreType.DMA
    small_rows = 3 * STATES + 8
    return pl.pallas_call(
        functools.partial(tail_kernel, count, half, block),
        out_shape=(out((rows, width), bf), out((2 * count * half, full), bf), out((count * block, full), bf),
                   out((3 * STATES, width), jnp.float32), out((8, width), jnp.float32)),
        in_specs=[SMEM] + [ANY] * 7 + [VMEM] * 9, out_specs=(VMEM,) * 5,
        scratch_shapes=[
            buf(2 * count * half, full), buf(rows, full),
            wide(tiles, rows, LANES), wide(tiles, rows, LANES), wide(tiles, rows, LANES),
            wide(*ckpt.shape), wide(3, STATES, tiles, SEG, LANES), wide(tiles, STATES * SEG, LANES), wide(tiles, STATES * SEG, LANES),
            wide(3, tiles, STATES * SEG, LANES),
            buf(rows, width), wide(ROWS, full), wide(8, full), buf(2, count - 1, half, full),
            buf(count * block, full), buf(count, block, full), wide(STATES, width), wide(count, STATES, width),
            wide(small_rows, width), wide(count, small_rows, width), wide(4, 8, width),
            buf(DEEP, 4, ROWS, width), buf(chunks, 2, ROWS, width), buf(chunks, ROWS, width), buf(DEEP, ROWS, width),
            dma((7,)), dma((2, 2 * (count - 1))), dma((2, 2 * (count - 1))),
            dma((4, chunks)), dma((4, chunks)), dma((4, count)), dma((4, count)),
        ],
        compiler_params=pltpu.CompilerParams(collective_id=1, has_side_effects=True, vmem_limit_bytes=62 * 2**20),
        cost_estimate=pl.CostEstimate(flops=6 * 10**9, bytes_accessed=40 * 10**6, transcendentals=0),
        name="tail_phase")(bounds, grads, n1, u, gk, gv, ckpt, gm, gq, inv, w_in_t, w_query_t, par, far, rate, gain, gain_two_parts)


def forward_pass(bounds_ref, u_ref, wide_ref, state_ref, span, tiles, row0, beside):
    state_ref[...] = jnp.zeros_like(state_ref)

    @pl.loop(0, span // GROUP)
    def _(group):
        keep = masks_of(bounds_ref, span, group)
        for lt in range(tiles):
            u = [u_ref[lt, pl.ds(row0 + group * GROUP + j, SEG, stride=span), :] for j in range(GROUP)]
            for n in range(STATES):
                mine = slice(n * SEG, (n + 1) * SEG)
                a = wide_ref[0, n, lt]
                s = state_ref[lt, mine, :]
                for j in range(GROUP):
                    s = a * s
                    if keep is not None:
                        s = s * keep[j]
                    s = s + u[j]
                state_ref[lt, mine, :] = s
        beside(group)


def forward_chain(bounds_ref, state_ref, first, far_ref, span, tiles, write):
    ends = []
    for lt in range(tiles):
        lanes = slice(lt * LANES, (lt + 1) * LANES)
        start, far = first[:, lanes], far_ref[:, lanes]
        for seg in range(SEG):
            rows = pl.ds(seg, STATES, stride=SEG)
            end = state_ref[lt, rows, :]
            if write:
                state_ref[lt, rows, :] = start
            start = end + far * start * open_segment(bounds_ref, span, seg)
        ends.append(start)
    return jnp.concatenate(ends, axis=1)


def forward_full(bounds_ref, u_ref, k_ref, v_ref, ckpt_ref, wide_ref, state_ref, span, tiles, row0, group0, beside):
    @pl.loop(0, span // GROUP)
    def _(group):
        keep = masks_of(bounds_ref, span, group)
        for lt in range(tiles):
            at = [pl.ds(row0 + group * GROUP + j, SEG, stride=span) for j in range(GROUP)]
            u = [u_ref[lt, r, :] for r in at]
            ks = [jnp.zeros((SEG, LANES), jnp.float32)] * GROUP
            vs = [jnp.zeros((SEG, LANES), jnp.float32)] * GROUP
            for n in range(STATES):
                mine = slice(n * SEG, (n + 1) * SEG)
                a, ck, cv = wide_ref[0, n, lt], wide_ref[1, n, lt], wide_ref[2, n, lt]
                s = state_ref[lt, mine, :]
                ckpt_ref[group0 + group, lt, mine, :] = s
                for j in range(GROUP):
                    s = a * s
                    if keep is not None:
                        s = s * keep[j]
                    s = s + u[j]
                    ks[j] = ks[j] + ck * s
                    vs[j] = vs[j] + cv * s
                state_ref[lt, mine, :] = s
            for j in range(GROUP):
                k_ref[lt, at[j], :] = ks[j]
                v_ref[lt, at[j], :] = vs[j]
        beside(group)


COT_ROWS = 512


def head_kernel(count, bounds_ref, cot_in, tok_ref, w_in_ref, w_query_ref, par_ref, far_ref, rate_ref, gain_ref,
                inv_ref, n1_hbm, u_hbm, q_hbm, k_hbm, v_hbm, ckpt_hbm, cot_hbm,
                tok_full, n1_ref, u_ref, q_ref, k_ref, v_ref, k_wide, v_wide, ckpt_ref, wide_ref, state_long, state_short,
                piece_ref, piece_held, save_sem, mp_send, mp_recv, cot_send, cot_recv, dp_send, dp_recv, ctx_send, ctx_recv):
    rows, width = tok_ref.shape
    tiles = width // LANES
    full = n1_ref.shape[1]
    me = lax.axis_index("dp")
    mp = lax.axis_index("mp")
    chunks = rows // ROWS
    cot_chunks = rows // COT_ROWS
    long_span, short_span = LONG_DEV // SEG, (rows - LONG_DEV) // SEG
    long_groups, short_groups = long_span // GROUP, short_span // GROUP
    tokens = Gather(Mover(mp_send, mp_recv), 0, tok_full, ROWS, tok_ref)
    cots = Gather(Mover(cot_send, cot_recv), 0, cot_hbm, COT_ROWS, cot_in)
    pieces = Spread(count, dp_send, dp_recv)
    greet_all(count)
    for c in range(chunks):
        tokens.start(c)
    for c in range(cot_chunks):
        cots.start(c)

    def save(src, dst, i):
        return pltpu.make_async_copy(src, dst, save_sem.at[i])

    own_cot = save(cot_in, cot_hbm.at[mp], 0)
    own_cot.start()
    seg_scan_params(par_ref, wide_ref)
    tok_full[mp] = tok_ref[...]
    zero = jnp.zeros((STATES, width), jnp.float32)

    def nothing(step):
        del step

    def span_of(c):
        return pl.ds(pl.multiple_of(c * ROWS, ROWS), ROWS)

    def project(c):
        tokens.finish(c)

        @pl.loop(0, ROWS // SUB)
        def _(sub):
            here = pl.ds(pl.multiple_of(c * ROWS + sub * SUB, SUB), SUB)
            v = normed(tok_full, c, sub, ROWS)
            mean = jnp.mean(v, axis=1, keepdims=True)
            centred = v - mean
            inv = lax.rsqrt(jnp.mean(centred * centred, axis=1, keepdims=True) + EPS)
            inv_ref[here, :] = inv
            n1_ref[here, :] = (centred * inv * gain_ref[...]).astype(jnp.bfloat16)

        n1 = n1_ref[span_of(c), :]
        u = mm(n1, w_in_ref[...], 1, 0)
        for lt in range(tiles):
            u_ref[lt, span_of(c), :] = u[:, lt * LANES : (lt + 1) * LANES]
        q_ref[span_of(c), :] = mm(n1, w_query_ref[...], 1, 0).astype(jnp.bfloat16)

    def context(src, i):
        rows_out = src.at[pl.ds(LONG_DEV, CTX)]
        return pltpu.make_async_remote_copy(
            src_ref=rows_out, dst_ref=src.at[pl.ds(0, CTX)], send_sem=ctx_send.at[i], recv_sem=ctx_recv.at[i],
            device_id=((me + 1) % count, mp), device_id_type=MESH)

    def narrow(first, size):
        for lt in range(tiles):
            lanes = slice(lt * LANES, (lt + 1) * LANES)
            k_ref[CTX + first : CTX + first + size, lanes] = k_wide[lt, first : first + size, :].astype(jnp.bfloat16)
            v_ref[CTX + first : CTX + first + size, lanes] = v_wide[lt, first : first + size, :].astype(jnp.bfloat16)

    @pl.loop(0, chunks + 1)
    def _(i):
        @pl.when(i < chunks)
        def _():
            tokens.forward(i)

        @pl.when(i >= 1)
        def _():
            project(i - 1)

        @pl.when(i == LONG_DEV // ROWS)
        def _():
            forward_pass(None, u_ref, wide_ref, state_long, long_span, tiles, 0, nothing)
            piece_ref[...] = forward_chain(None, state_long, zero, far_ref.at[0], long_span, tiles, False)
            pieces.start(lambda o: piece_ref, lambda o: piece_held.at[me])

    pieces.wait(lambda o: piece_ref, lambda o: piece_held.at[me])
    piece_held[me] = zero

    def fold(d, total):
        gap = me - 1 - d
        weight = jnp.exp(rate_ref[...] * (-LONG_DEV * jnp.maximum(gap, 0)).astype(jnp.float32))
        return total + jnp.where(gap >= 0, weight * piece_held[d], 0.0)

    first = lax.fori_loop(0, count, fold, zero)
    saves = [save(n1_ref, n1_hbm, 1), save(u_ref, u_hbm, 2), save(q_ref, q_hbm, 3)]
    for s in saves:
        s.start()
    forward_chain(None, state_long, first, far_ref.at[0], long_span, tiles, True)
    forward_full(None, u_ref, k_wide, v_wide, ckpt_ref, wide_ref, state_long, long_span, tiles, 0, 0, nothing)
    narrow(0, LONG_DEV)
    contexts = [context(k_ref, 0), context(v_ref, 1)]
    for copy in contexts:
        copy.start()

    cots.forward(0)
    forward_pass(bounds_ref, u_ref, wide_ref, state_short, short_span, tiles, LONG_DEV, nothing)
    cots.forward(1)
    forward_chain(bounds_ref, state_short, zero, far_ref.at[1], short_span, tiles, True)

    def beside(group):
        @pl.when(group == short_groups // 2)
        def _():
            cots.forward(2)

    forward_full(bounds_ref, u_ref, k_wide, v_wide, ckpt_ref, wide_ref, state_short, short_span, tiles, LONG_DEV, long_groups, beside)
    cots.forward(3)
    last = [save(ckpt_ref, ckpt_hbm, 4)]
    last[0].start()
    narrow(LONG_DEV, rows - LONG_DEV)
    for copy in contexts:
        copy.wait()
    for s in (save(k_ref, k_hbm, 5), save(v_ref, v_hbm, 6)):
        s.start()
        last.append(s)
    for c in range(cot_chunks):
        cots.finish(c)
    for s in saves + last + [own_cot]:
        s.wait()


def head_phase(bounds, cot, tok, w_in, w_query, par, far, rate, gain, count):
    rows, width = tok.shape
    full = w_in.shape[0]
    tiles = width // LANES
    bf = jnp.bfloat16
    groups = rows // SEG // GROUP

    def out(shape, dtype):
        return jax.ShapeDtypeStruct(shape, dtype)

    def buf(*shape):
        return pltpu.VMEM(shape, bf)

    def wide(*shape):
        return pltpu.VMEM(shape, jnp.float32)

    ANY = pl.BlockSpec(memory_space=pl.ANY)
    dma = pltpu.SemaphoreType.DMA
    chunks, cot_chunks = rows // ROWS, rows // COT_ROWS
    return pl.pallas_call(
        functools.partial(head_kernel, count),
        out_shape=(out((rows, 1), jnp.float32), out((rows, full), bf), out((tiles, rows, LANES), jnp.float32), out((rows, width), bf),
                   out((CTX + rows, width), bf), out((CTX + rows, width), bf),
                   out((groups, tiles, STATES * SEG, LANES), jnp.float32), out((4, rows, width), bf)),
        in_specs=[SMEM, ANY] + [VMEM] * 7, out_specs=(VMEM,) + (ANY,) * 7,
        scratch_shapes=[
            buf(4, rows, width), buf(rows, full), wide(tiles, rows, LANES), buf(rows, width), buf(CTX + rows, width), buf(CTX + rows, width),
            wide(tiles, rows, LANES), wide(tiles, rows, LANES), wide(groups, tiles, STATES * SEG, LANES),
            wide(3, STATES, tiles, SEG, LANES), wide(tiles, STATES * SEG, LANES), wide(tiles, STATES * SEG, LANES),
            wide(STATES, width), wide(count, STATES, width),
            dma((7,)), dma((3, chunks)), dma((3, chunks)), dma((3, cot_chunks)), dma((3, cot_chunks)), dma((count,)), dma((count,)),
            dma((2,)), dma((2,)),
        ],
        compiler_params=pltpu.CompilerParams(collective_id=2, has_side_effects=True, vmem_limit_bytes=56 * 2**20),
        cost_estimate=pl.CostEstimate(flops=3 * 10**9, bytes_accessed=40 * 10**6, transcendentals=0),
        name="head_phase")(bounds, cot, tok, w_in, w_query, par, far, rate, gain)


def gather_features(values_in):
    return lax.all_gather(values_in, "mp", axis=1, tiled=True)


def reduce_features(values_in):
    return lax.psum_scatter(
        values_in.astype(jnp.bfloat16), "mp", scatter_dimension=1, tiled=True
    ).astype(jnp.float32)


def from_behind(value, axis, steps):
    count = lax.axis_size(axis)
    initial, last = (max(0, -steps), min(count, count - steps))
    return lax.ppermute(value, axis, [(source, source + steps) for source in range(initial, last)])


def norm_forward(values_in, gain_vec):
    row_mean = jnp.mean(values_in, axis=1, keepdims=True)
    centred = values_in - row_mean
    row_var = jnp.mean(centred * centred, axis=1, keepdims=True)
    inverse = lax.rsqrt(row_var + EPS)
    normed = centred * inverse
    return (normed, inverse, normed * gain_vec)


def norm_backward(upstream, normed, inverse, gain_vec):
    gain_grad = jnp.sum(upstream * normed, axis=0)
    scaled = upstream * gain_vec
    plain_mean = jnp.mean(scaled, axis=1, keepdims=True)
    cross_mean = jnp.mean(scaled * normed, axis=1, keepdims=True)
    return (inverse * (scaled - plain_mean - normed * cross_mean), gain_grad)


def gelu_exact(values_in):
    return jax.nn.gelu(values_in, approximate=False)


def fold_pieces(pieces, decay_rate, gap_count):
    live_rows = gap_count >= 0
    weights = jnp.exp(
        -decay_rate[None]
        * (LONG_DEV * jnp.maximum(gap_count, 0)).astype(jnp.float32)[:, None, None]
    )
    return jnp.sum(jnp.where(live_rows[:, None, None], weights * pieces, 0.0), axis=0)


def dot(left, right, dims):
    return lax.dot_general(left, right, ((dims[0], dims[1]), ((), ())), preferred_element_type=jnp.float32)


def on_device(
    tokens,
    gain_one,
    gain_two,
    w_in,
    w_query,
    w_out,
    w_up,
    w_down,
    decay_rate,
    b_in,
    c_key,
    c_val,
    short_lengths,
    cotangent,
):
    low = jnp.bfloat16
    device = lax.axis_index("dp")
    local_width = w_in.shape[1]
    lengths = short_lengths[0]
    ends = jnp.cumsum(lengths).astype(jnp.int32)
    short_starts = jnp.concatenate([jnp.zeros((1,), jnp.int32), ends[:-1]])
    no_bound = jnp.full((1,), -1, jnp.int32)
    long_low = jnp.where(device > 0, 0, CTX).astype(jnp.int32).reshape(1)
    rate_t = decay_rate.T
    root = jnp.sqrt(-jnp.expm1(-2.0 * rate_t))
    drive = root * b_in.T
    ck_t, cv_t = c_key.T, c_val.T
    decay = jnp.exp(-rate_t)
    par = jnp.stack([decay, drive * ck_t, drive * cv_t])
    short_rows = tokens.shape[0] - LONG_DEV
    far_long = jnp.exp(-rate_t * (LONG_DEV // SEG))
    far_short = jnp.exp(-rate_t * (short_rows // SEG))

    count = lax.axis_size("dp")
    far = jnp.stack([far_long, far_short])
    inverse_one, normed_one_low, u_tiles, queries, k_ext, v_ext, ckpt, cotangent_full = head_phase(
        short_starts, cotangent, tokens, w_in, w_query, par, far, rate_t, gain_one[None], count
    )
    k_long, v_long = k_ext[: CTX + LONG_DEV], v_ext[: CTX + LONG_DEV]
    k_short, v_short = k_ext[CTX + LONG_DEV :], v_ext[CTX + LONG_DEV :]
    q_long, q_short = queries[:LONG_DEV], queries[LONG_DEV:]
    att_short, lse_short = attend(short_starts, q_short, k_short, v_short, 0, "attend_short")
    att_long, lse_long = attend(long_low, q_long, k_long, v_long, CTX, "attend_long")
    attended = jnp.concatenate([att_long, att_short])
    result, grad_middle, grad_attended, grads, gain_two_parts = middle_phase(
        attended, tokens, cotangent_full, w_out, w_up, w_down, gain_two[None]
    )

    gq_long, gk_long, gv_long = attend_back(
        long_low, q_long, k_long, v_long, grad_attended[:LONG_DEV], lse_long, CTX, "attend_back_long"
    )
    back = from_behind(jnp.stack([gk_long[:, :CTX], gv_long[:, :CTX]]).astype(low), "dp", -1).astype(jnp.float32)
    gq_short, gk_short, gv_short = attend_back(
        short_starts, q_short, k_short, v_short, grad_attended[LONG_DEV:], lse_short, 0, "attend_back_short"
    )
    gk_long = gk_long[:, CTX:].at[:, LONG_DEV - CTX :].add(back[0])
    gv_long = gv_long[:, CTX:].at[:, LONG_DEV - CTX :].add(back[1])
    gk = jnp.concatenate([gk_long, gk_short], axis=1)
    gv = jnp.concatenate([gv_long, gv_short], axis=1)
    grad_queries = jnp.concatenate([gq_long, gq_short])
    grad_tokens, total, win_t, sums, gains = tail_phase(
        short_starts, grads, normed_one_low, u_tiles, gk, gv, ckpt, grad_middle, grad_queries, inverse_one,
        w_in, w_query, par, far, rate_t, gain_one[None], gain_two_parts, count,
    )
    hidden, full = w_down.shape
    rows_of = [total[:hidden], total[hidden : hidden + full], total[hidden + full : hidden + full + local_width],
               total[hidden + full + local_width : hidden + full + 2 * local_width].T, win_t[:local_width].T]
    grad_w_down, grad_w_up, grad_w_out, grad_w_query, grad_w_in = (r.astype(jnp.float32) for r in rows_of)
    grad_gain_one, grad_gain_two = gains.reshape(2, full)
    sums = sums.reshape(3, STATES, local_width)

    grad_ck = (drive * sums[0]).T
    grad_cv = (drive * sums[1]).T
    grad_drive = ck_t * sums[0] + cv_t * sums[1]
    grad_b = (root * grad_drive).T
    grad_rate = (grad_drive * b_in.T * jnp.exp(-2.0 * rate_t) / root - sums[2]).T
    return (
        result,
        grad_tokens,
        grad_gain_one,
        grad_gain_two,
        grad_w_in,
        grad_w_query,
        grad_w_out,
        grad_w_up,
        grad_w_down,
        grad_rate,
        grad_b,
        grad_ck,
        grad_cv,
    )


def solution(mesh):
    placed = (
        P("dp", "mp"),
        P(),
        P(),
        P(None, "mp"),
        P(None, "mp"),
        P("mp", None),
        P(None, "mp"),
        P("mp", None),
        P("mp", None),
        P("mp", None),
        P("mp", None),
        P("mp", None),
        P("dp", None),
        P("dp", "mp"),
    )
    return jax.shard_map(
        on_device,
        mesh=mesh,
        in_specs=placed,
        out_specs=(
            P("dp", "mp"),
            P("dp", "mp"),
            P(),
            P(),
            P(None, "mp"),
            P(None, "mp"),
            P("mp", None),
            P(None, "mp"),
            P("mp", None),
            P("mp", None),
            P("mp", None),
            P("mp", None),
            P("mp", None),
        ),
        check_vma=False,
    )
```
